32 devices in a mesh: dp: 16 (over z, y, x), opt: 2 (over core).
Axes of the slice: x: 2, y: 2, z: 4, core: 2. Of those that a mesh axis runs over, the one named last changes fastest.
Arguments:
- enc_in: bfloat16 [49152, 768], P(('dp', 'opt')), may hold values from -6 to 6
- enc_cot: bfloat16 [49152, 768], P(('dp', 'opt')), may hold values from -0.59765625 to 0.59765625
- dec_in: bfloat16 [640, 768], P(('dp', 'opt')), may hold values from -6 to 6
- dec_cot: bfloat16 [640, 768], P(('dp', 'opt')), may hold values from -6 to 6
- passage_lengths: int32 [96], P(('dp', 'opt')), may hold values from 250 to 500, as said below
- passage_example: int32 [96], P(('dp', 'opt')), may hold values from 0 to 31, as said below
- answer_tokens: int32 [32, 20], P(('dp', 'opt')), may hold values from 0 to 32127, as said below
- owner_slot: int32 [1008], replicated, may hold values from 0 to 1023, as said below
- master: float32 [1024, 128, 128], P(('dp', 'opt'))
- kron_stats: float32 [1024, 2, 128, 128], P(('dp', 'opt'))
- inverse_roots: float32 [1024, 2, 128, 128], P(('dp', 'opt'))
- small_params: float32 [5376], P(('dp', 'opt'))
- small_moment: float32 [5376], P(('dp', 'opt')), may hold values from -9.797959 to 9.797959
Outputs:
- dec_out: bfloat16 [640, 768], P(('dp', 'opt'))
- encodings: bfloat16 [49152, 768], P(('dp', 'opt'))
- enc_in_grad: float32 [49152, 768], P(('dp', 'opt'))
- dec_in_grad: float32 [640, 768], P(('dp', 'opt'))
- block_grads: float32 [1024, 128, 128], P(('dp', 'opt'))
- new_stats: float32 [1024, 2, 128, 128], P(('dp', 'opt'))
- new_master: float32 [1024, 128, 128], P(('dp', 'opt'))
- small_grads: float32 [5376], P(('dp', 'opt'))
- new_moment: float32 [5376], P(('dp', 'opt'))
- new_small: float32 [5376], P(('dp', 'opt'))
The draws below stay inside these ranges and needn't reach their ends.
Inputs may be any that keep to these rules, and one draw needn't show every extreme that they name: `passage_lengths`: each length is 250 or 500; the first passage has 500 tokens and the second 250. `passage_example`: devices are numbered dp-major (index dp times the opt size plus opt); example e belongs to device e. A passage on device (a, o) belongs to an example of device (b, o) with k = (a - b) mod the dp size below 3; every example has exactly one passage with each k, and its passages are ordered by k. `answer_tokens`: ids of 1 to 32127, then 0 to the end of the row; every answer has one token or more, the first one 20. `owner_slot`: distinct slots; slot s belongs to device s // 32, devices numbered dp-major.
All inputs are finite; a program needn't handle non-finite values.
Results may differ from the reference program's by a relative error of at most 0.018.
Values may be sent and summed in bfloat16 or wider, within the bound.
A program may use at most 448 MiB of HBM per device.

```python
import math
import jax
import jax.numpy as jnp
import numpy as np
from jax import lax

D = 768
H = 12
HD = 64
FF = 3072
NB = 32
MAXD = 128
VOCAB = 32128
BLK = 128
PASS_SLOT = 512
LONG = 500
SHORT = 250
PASS_EX = 3
ALEN = 20
EX_DEV = 1
P_DEV = 3
PASSAGES = 96
EXAMPLES = 32
BLOCKS = 1008
SLOTS = 1024
NSMALL = 5376
N_DP = 16
N_OPT = 2


def slot_choice(key):
    return jax.random.permutation(jax.random.fold_in(key, 91), SLOTS)[:BLOCKS].astype(jnp.int32)


def block_counts():
    square_count = D * D // (BLK * BLK)
    wide_count = D * FF // (BLK * BLK)
    return [square_count] * 4 + [wide_count, wide_count] + [square_count] * 8 + [wide_count, wide_count]


def block_scales():
    fan_list = [D * HD, D, D, D * 8 // LONG, D, FF, D * HD, D, D, D * 8 // ALEN, D * HD, D, D, D * 8 // (PASS_EX * LONG), D, FF]
    return np.concatenate([np.full((count_each,), 1.0 / math.sqrt(fan_each), np.float32) for fan_each, count_each in zip(fan_list, block_counts())])


def stat_levels():
    enc_square = 0.05 * PASSAGES * (SHORT + LONG) / 2.0
    dec_square = EXAMPLES * (ALEN + 1) / 2.0
    factors = [0.1, 0.1, 1.0, 0.03, 1.0, 0.3, 0.1, 0.1, 1.0, 0.3, 0.1, 0.1, 1.0, 0.03, 1.0, 0.3]
    squares = [enc_square] * 6 + [dec_square] * 10
    return np.concatenate([np.full((count_each,), 0.0125 * BLK * factor_each * square_each, np.float32) for factor_each, square_each, count_each in zip(factors, squares, block_counts())])


def symmetric_draw(key, level):
    diagonal = jax.random.uniform(jax.random.fold_in(key, 1), (SLOTS, 2, BLK), jnp.float32, 1.0, 4.0)
    normal_part = jax.random.normal(jax.random.fold_in(key, 2), (SLOTS, 2, BLK, BLK), jnp.float32) * 0.3
    identity = (jnp.arange(BLK)[:, None] == jnp.arange(BLK)[None, :]).astype(jnp.float32)
    return level * (0.5 * (normal_part + jnp.swapaxes(normal_part, 2, 3)) * (1.0 - identity) + identity * diagonal[..., None])


def draw_owner_slot(key, part):
    chosen = slot_choice(key)
    return chosen


def draw_master(key, part):
    chosen = slot_choice(key)
    key = jax.random.fold_in(key, 5)
    filler = jax.random.normal(jax.random.fold_in(key, 1), (SLOTS, BLK, BLK), jnp.float32) / math.sqrt(D)
    placed = jax.random.normal(jax.random.fold_in(key, 2), (BLOCKS, BLK, BLK), jnp.float32) * jnp.asarray(block_scales())[:, None, None]
    return filler.at[chosen].set(placed)


def draw_kron_stats(key, part):
    chosen = slot_choice(key)
    key = jax.random.fold_in(key, 7)
    base_level = 0.0125 * BLK * EXAMPLES * (ALEN + 1) / 2.0
    levels = jnp.full((SLOTS,), base_level, jnp.float32).at[chosen].set(jnp.asarray(stat_levels()))
    return symmetric_draw(key, levels[:, None, None, None])


def draw_inverse_roots(key, part):
    key = jax.random.fold_in(key, 11)
    return symmetric_draw(key, 1.0)


def draw_small_params(key, part):
    key = jax.random.fold_in(key, 13)
    norm_gains = jax.random.uniform(jax.random.fold_in(key, 1), (6 * D,), jnp.float32, 0.5, 1.5)
    tables = jax.random.normal(jax.random.fold_in(key, 2), (2 * NB * H,), jnp.float32) * 0.5
    return jnp.concatenate([norm_gains, tables])


def draw_passage_lengths(key, part):
    key = jax.random.fold_in(key, 17)
    picks = jax.random.randint(key, (PASSAGES,), 0, 2)
    picks = picks.at[0].set(1).at[1].set(0)
    return (SHORT + (LONG - SHORT) * picks).astype(jnp.int32)


def draw_passage_example(key, part):
    key = jax.random.fold_in(key, 19)
    device_count = PASSAGES // P_DEV
    scores = jax.random.randint(key, (device_count, P_DEV), 0, 1048576) * P_DEV + jnp.arange(P_DEV)[None, :]
    placing = jnp.argsort(scores, axis=1, stable=True).astype(jnp.int32)
    device = jnp.arange(device_count, dtype=jnp.int32)[:, None]
    offset = placing // EX_DEV
    within = placing % EX_DEV
    owner_device = (device // N_OPT - offset) % N_DP * N_OPT + device % N_OPT
    return (owner_device * EX_DEV + within).reshape(-1).astype(jnp.int32)


def draw_answer_tokens(key, part):
    key = jax.random.fold_in(key, 23)
    answer_len = jax.random.randint(jax.random.fold_in(key, 1), (EXAMPLES, 1), 1, ALEN + 1)
    answer_len = answer_len.at[0, 0].set(ALEN)
    words = jax.random.randint(jax.random.fold_in(key, 2), (EXAMPLES, ALEN), 1, VOCAB)
    return jnp.where(jnp.arange(ALEN)[None, :] < answer_len, words, 0).astype(jnp.int32)


def block_levels(stream_key, dims, cuts, least, high):
    def one(axis_at, shards_of):
        steps = jax.random.uniform(jax.random.fold_in(jax.random.fold_in(stream_key, 6), axis_at), (shards_of,), jnp.float32, least / len(cuts), high / len(cuts))
        return jnp.repeat(jnp.exp(steps), dims[axis_at] // shards_of).reshape((-1,) + (1,) * (len(dims) - axis_at - 1))

    gain = one(*cuts[0])
    for cut in cuts[1:]:
        gain = gain * one(*cut)
    return gain


def centred(own_key, extent, width, bound, split=(), kind=jnp.bfloat16):
    drawn = jax.random.normal(own_key, extent, jnp.float32) * width
    if len(split) > 0:
        drawn = block_levels(own_key, extent, split, -0.22, 0.18) * drawn
    return jnp.clip(drawn, min=-bound, max=bound).astype(kind)


def setup_inputs(seed: int = 0) -> dict:
    seeds = jax.random.split(jax.random.key(seed), 14)
    enc_in = centred(seeds[0], (PASSAGES * PASS_SLOT, D), 1.0, 6.0, ((0, 32),))
    enc_cot = centred(seeds[1], (PASSAGES * PASS_SLOT, D), 0.1, 0.59765625, ((0, 32),))
    dec_in = centred(seeds[2], (EXAMPLES * ALEN, D), 1.0, 6.0, ((0, 32),))
    dec_cot = centred(seeds[3], (EXAMPLES * ALEN, D), 1.0, 6.0, ((0, 32),))
    passage_lengths = draw_passage_lengths(jax.random.fold_in(seeds[13], 71), 0)
    passage_example = draw_passage_example(jax.random.fold_in(seeds[13], 71), 0)
    answer_tokens = draw_answer_tokens(jax.random.fold_in(seeds[13], 71), 0)
    owner_slot = draw_owner_slot(jax.random.fold_in(seeds[13], 71), 0)
    master = draw_master(jax.random.fold_in(seeds[13], 71), 0)
    kron_stats = draw_kron_stats(jax.random.fold_in(seeds[13], 71), 0)
    inverse_roots = draw_inverse_roots(jax.random.fold_in(seeds[13], 71), 0)
    small_params = draw_small_params(jax.random.fold_in(seeds[13], 71), 0)
    small_moment = centred(seeds[12], (NSMALL,), (0.2 * PASSAGES ** 0.5), 9.797959, ((0, 32),), jnp.float32)
    return {"enc_in": enc_in, "enc_cot": enc_cot, "dec_in": dec_in, "dec_cot": dec_cot, "passage_lengths": passage_lengths, "passage_example": passage_example, "answer_tokens": answer_tokens, "owner_slot": owner_slot, "master": master, "kron_stats": kron_stats, "inverse_roots": inverse_roots, "small_params": small_params, "small_moment": small_moment}


exact_prec = lax.Precision.HIGHEST
neg_fill = -1000000000.0
stat_decay = 0.95
block_rate = 0.5
moment_decay = 0.9
small_rate = 0.002

@jax.custom_vjp
def low(v):
    return lax.optimization_barrier(v.astype(jnp.bfloat16)).astype(jnp.float32)

@jax.custom_vjp
def low_back(v):
    return v

def low_keep(v):
    return (low(v), None)

def low_pass(kept, grad):
    return (grad,)

def back_keep(v):
    return (v, None)

def back_low(kept, grad):
    return (low(grad),)
low.defvjp(low_keep, low_pass)
low_back.defvjp(back_keep, back_low)

def both_ways(values):
    return low_back(low(values))

def bucket_index(length, both_sides):
    offsets = np.arange(-(length - 1), length)
    if both_sides:
        halves = NB // 2
        bucket_base = (offsets > 0) * halves
        distance = np.abs(offsets)
    else:
        halves = NB
        bucket_base = offsets * 0
        distance = np.maximum(-offsets, 0)
    exact_count = halves // 2
    widened = np.maximum(distance, 1) * 1.0
    far_bucket = exact_count + np.floor(np.log(widened / exact_count) / np.log(MAXD / exact_count) * (halves - exact_count)).astype(np.int32)
    far_bucket = np.minimum(far_bucket, halves - 1)
    return (bucket_base + np.where(distance < exact_count, distance, far_bucket)).astype(np.int32)

def bias_offsets(bias_table, length, both_sides):
    onehot = (bucket_index(length, both_sides)[:, None] == np.arange(NB)[None, :]).astype(np.float32)
    return jnp.dot(bias_table.T, jnp.asarray(onehot, jnp.float32).T, precision=exact_prec, preferred_element_type=jnp.float32)

def spread_offsets(offset_bias, length):
    head_count = offset_bias.shape[0]
    tiled_rows = jnp.broadcast_to(offset_bias[:, None, :], (head_count, length, 2 * length - 1))
    flattened = tiled_rows.reshape(head_count, length * (2 * length - 1))
    flattened = jnp.concatenate([flattened, jnp.zeros((head_count, length), flattened.dtype)], axis=1)
    return flattened.reshape(head_count, length, 2 * length)[:, ::-1, :length]

def rms_scale(values, norm_gain):
    return values * lax.rsqrt(lax.optimization_barrier(jnp.mean(values * values, axis=-1, keepdims=True)) + 1e-06) * norm_gain

def smooth_gate(inner_act):
    return jax.nn.gelu(inner_act, approximate=True)

def project(rows_in, weight):
    return jnp.dot(rows_in, weight, precision=exact_prec, preferred_element_type=jnp.float32)

def matrix_shapes():
    square = (D, D)
    return [square, square, square, square, (D, FF), (FF, D), square, square, square, square, square, square, square, square, (D, FF), (FF, D)]

def assemble(ordered):
    matrices = []
    first_block = 0
    for rows_in, cols_out in matrix_shapes():
        block_count = rows_in // BLK * (cols_out // BLK)
        block_grid = ordered[first_block:first_block + block_count].reshape(rows_in // BLK, cols_out // BLK, BLK, BLK)
        matrices.append(block_grid.transpose(0, 2, 1, 3).reshape(rows_in, cols_out))
        first_block = first_block + block_count
    return matrices

def attention(queries, key_rows, value_rows, score_bias, pair_valid):
    scores = jnp.einsum('brhe,bche->bhrc', queries, key_rows, precision=exact_prec) + score_bias
    scores = low_back(jnp.where(pair_valid[:, None], scores, neg_fill))
    weights = low(jax.nn.softmax(scores, axis=-1))
    return jnp.einsum('bhrc,bche->brhe', weights, value_rows, precision=exact_prec)

def encoder(matrices, norm_gains, score_bias, passages, key_valid):
    passage_count, slot_rows = (passages.shape[0], passages.shape[1])
    row_total = passage_count * slot_rows
    heads_shape = (passage_count, slot_rows, H, HD)
    inputs = passages.reshape(row_total, D)
    normed = low(rms_scale(inputs, norm_gains[0]))
    queries = both_ways(project(normed, matrices[0])).reshape(heads_shape)
    key_rows = both_ways(project(normed, matrices[1])).reshape(heads_shape)
    value_rows = both_ways(project(normed, matrices[2])).reshape(heads_shape)
    pair_valid = jnp.broadcast_to(key_valid[:, None, :], (passage_count, slot_rows, slot_rows))
    mixed_heads = both_ways(attention(queries, key_rows, value_rows, score_bias, pair_valid).reshape(row_total, D))
    hidden = inputs + low_back(project(mixed_heads, matrices[3]))
    inner_act = low_back(project(low(rms_scale(hidden, norm_gains[1])), matrices[4]))
    output = hidden + low_back(project(low(smooth_gate(inner_act)), matrices[5]))
    return low(rms_scale(output, norm_gains[2])).reshape(passages.shape)

def decoder(matrices, norm_gains, score_bias, answer_rows, memory, memory_valid):
    self_shape = (1, ALEN, H, HD)
    memory_len = memory.shape[0]
    memory_shape = (1, memory_len, H, HD)
    normed = low(rms_scale(answer_rows, norm_gains[3]))
    queries = both_ways(project(normed, matrices[6])).reshape(self_shape)
    key_rows = both_ways(project(normed, matrices[7])).reshape(self_shape)
    value_rows = both_ways(project(normed, matrices[8])).reshape(self_shape)
    causal = jnp.broadcast_to((jnp.arange(ALEN)[:, None] >= jnp.arange(ALEN)[None, :])[None], (1, ALEN, ALEN))
    mixed_heads = both_ways(attention(queries, key_rows, value_rows, score_bias, causal).reshape(ALEN, D))
    first = answer_rows + low_back(project(mixed_heads, matrices[9]))
    cross_queries = both_ways(project(low(rms_scale(first, norm_gains[4])), matrices[10])).reshape(self_shape)
    memory_low = low_back(memory)
    cross_keys = both_ways(project(memory_low, matrices[11])).reshape(memory_shape)
    cross_values = both_ways(project(memory_low, matrices[12])).reshape(memory_shape)
    cross_valid = jnp.broadcast_to(memory_valid[None, None, :], (1, ALEN, memory_len))
    cross_heads = both_ways(attention(cross_queries, cross_keys, cross_values, 0.0, cross_valid).reshape(ALEN, D))
    second = first + low_back(project(cross_heads, matrices[13]))
    inner_act = low_back(project(low(rms_scale(second, norm_gains[5])), matrices[14]))
    return second + low_back(project(low(smooth_gate(inner_act)), matrices[15]))

def reference(enc_in, enc_cot, dec_in, dec_cot, passage_lengths, passage_example, answer_tokens, owner_slot, master, kron_stats, inverse_roots, small_params, small_moment):
    count_pass = passage_lengths.shape[0]
    examples = answer_tokens.shape[0]
    home_dp = jnp.arange(count_pass, dtype=jnp.int32) // P_DEV // N_OPT
    owner_dp = passage_example // EX_DEV // N_OPT
    position = passage_example * PASS_EX + (home_dp - owner_dp) % N_DP
    members = jnp.zeros((examples * PASS_EX,), jnp.int32).at[position].set(jnp.arange(count_pass, dtype=jnp.int32)).reshape(examples, PASS_EX)
    key_valid = jnp.arange(PASS_SLOT)[None, :] < passage_lengths[:, None]
    table_size = NB * H

    def forward(master_in, small_in, enc_rows, dec_rows):
        matrices = assemble(low(master_in)[owner_slot])
        small_low = low(small_in)
        norm_gains = [small_low[gain_index * D:(gain_index + 1) * D] for gain_index in range(6)]
        enc_bias = spread_offsets(bias_offsets(small_low[6 * D:6 * D + table_size].reshape(NB, H), PASS_SLOT, True), PASS_SLOT)
        dec_bias = spread_offsets(bias_offsets(small_low[6 * D + table_size:].reshape(NB, H), ALEN, False), ALEN)
        passages = enc_rows.reshape(count_pass, PASS_SLOT, D)
        answers = dec_rows.reshape(examples, ALEN, D)

        def one_example(operands):
            member_rows, member_valid, answer_rows = operands
            encoded = encoder(matrices, norm_gains, enc_bias, member_rows, member_valid)
            decoded = decoder(matrices, norm_gains, dec_bias, answer_rows, encoded.reshape(PASS_EX * PASS_SLOT, D), member_valid.reshape(PASS_EX * PASS_SLOT))
            return (encoded, decoded)
        encoded, decoded = lax.map(jax.checkpoint(one_example), (passages[members], key_valid[members], answers))
        encoded = encoded.reshape(examples * PASS_EX, PASS_SLOT, D)[position]
        return (encoded.reshape(count_pass * PASS_SLOT, D), decoded.reshape(examples * ALEN, D))
    outputs, pullback = jax.vjp(forward, master, small_params, enc_in.astype(jnp.float32), dec_in.astype(jnp.float32))
    row_valid = key_valid.reshape(-1, 1).astype(jnp.float32)
    answer_valid = (answer_tokens != 0).reshape(-1, 1).astype(jnp.float32)
    block_grads, small_grads, enc_in_grad, dec_in_grad = pullback((enc_cot.astype(jnp.float32) * row_valid, dec_cot.astype(jnp.float32) * answer_valid))
    left_gram = jnp.einsum('sij,skj->sik', block_grads, block_grads, precision=exact_prec)
    right_gram = jnp.einsum('sji,sjk->sik', block_grads, block_grads, precision=exact_prec)
    new_stats = stat_decay * kron_stats + (1.0 - stat_decay) * jnp.stack([left_gram, right_gram], axis=1)
    shaped = jnp.einsum('sij,sjk->sik', inverse_roots[:, 0], block_grads, precision=exact_prec)
    shaped = jnp.einsum('sij,sjk->sik', shaped, inverse_roots[:, 1], precision=exact_prec)
    shaped_rms = jnp.sqrt(lax.optimization_barrier(jnp.mean(shaped * shaped, axis=(1, 2), keepdims=True)) + 1e-06)
    weight_rms = jnp.sqrt(lax.optimization_barrier(jnp.mean(master * master, axis=(1, 2), keepdims=True)) + 1e-06)
    new_master = master - block_rate * weight_rms * shaped / shaped_rms
    new_moment = moment_decay * small_moment + small_grads
    new_small = small_params - small_rate * new_moment
    return (outputs[1].astype(jnp.bfloat16), outputs[0].astype(jnp.bfloat16), enc_in_grad, dec_in_grad, block_grads, new_stats, new_master, small_grads, new_moment, new_small)
```

```python
import functools

import jax
import jax.numpy as jnp
import numpy as np
from jax import lax
from jax.experimental import pallas as pl
from jax.experimental.pallas import tpu as pltpu
from jax.sharding import PartitionSpec as P

D = 768
H = 12
HD = 64
FF = 3072
NB = 32
MAXD = 128
BLK = 128
PASS_SLOT = 512
PASS_EX = 3
ALEN = 20
EX_DEV = 1
AROWS = 32
PAIRS = H // 2
STRIP = 7 * BLK
EXTRA = 16

exact_prec = lax.Precision.HIGHEST
neg_fill = -1000000000.0
stat_decay = 0.95
block_rate = 0.5
moment_decay = 0.9
small_rate = 0.002
MESH = pl.DeviceIdType.MESH
VMEM_CAP = 60 << 20
f32 = jnp.float32
bf16 = jnp.bfloat16

ENC_QKV, ENC_OUT, ENC_UP, ENC_DOWN = 0, 108, 144, 288
DEC_QKV, DEC_OUT, CROSS_Q, CROSS_KV, CROSS_OUT, DEC_UP, DEC_DOWN = 432, 540, 576, 612, 684, 720, 864


def dot(left, right):
    return jnp.dot(left, right, preferred_element_type=f32)


def dot_nt(left, right):
    return lax.dot_general(left, right, (((1,), (1,)), ((), ())), preferred_element_type=f32)


def dot_tn(left, right):
    return lax.dot_general(left, right, (((0,), (0,)), ((), ())), preferred_element_type=f32)


def to_low(values):
    return values.astype(bf16)


def rms_factor(values):
    return lax.rsqrt(jnp.mean(values * values, axis=-1, keepdims=True) + 1e-06)


def rms_scale(values, gain):
    return values * rms_factor(values) * gain


def norm_back(values, gain, upstream):
    factor = rms_factor(values)
    scaled = values * factor
    lifted = upstream * gain
    inner = jnp.mean(lifted * scaled, axis=-1, keepdims=True)
    rows = factor * (lifted - scaled * inner)
    return rows, jnp.sum(upstream * scaled, axis=0, keepdims=True)


GATE_A = float(np.sqrt(2.0 / np.pi))
GATE_B = 0.044715


def gate(values):
    return 0.5 * values * (1.0 + jnp.tanh(GATE_A * (values + GATE_B * values * values * values)))


def gate_both(values):
    square = values * values
    bend = jnp.tanh(GATE_A * values * (1.0 + GATE_B * square))
    half = 0.5 * (1.0 + bend)
    slope = half + 0.5 * values * (1.0 - bend * bend) * (GATE_A * (1.0 + 3.0 * GATE_B * square))
    return values * half, slope


def bucket_of(offsets, both_sides):
    if both_sides:
        halves = NB // 2
        bucket_base = (offsets > 0) * halves
        distance = np.abs(offsets)
    else:
        halves = NB
        bucket_base = offsets * 0
        distance = np.maximum(-offsets, 0)
    exact_count = halves // 2
    widened = np.maximum(distance, 1) * 1.0
    far_bucket = exact_count + np.floor(
        np.log(widened / exact_count) / np.log(MAXD / exact_count) * (halves - exact_count)
    ).astype(np.int32)
    far_bucket = np.minimum(far_bucket, halves - 1)
    return (bucket_base + np.where(distance < exact_count, distance, far_bucket)).astype(np.int32)


def strip_buckets():
    rho = np.arange(2 * BLK, 5 * BLK)[:, None]
    return bucket_of(rho - 3 * BLK - np.arange(BLK)[None, :], True)


def start_blocks(rows_ref, gathered, first, rows, cols, dest, sem):
    across = cols // BLK

    def body(b, carry):
        i = b // across
        j = b - i * across
        source = pl.multiple_of(rows_ref[first + b], 16)
        pltpu.make_async_copy(
            gathered.at[pl.ds(source, BLK)],
            dest.at[pl.ds(pl.multiple_of(i * BLK, BLK), BLK), pl.ds(pl.multiple_of(j * BLK, BLK), BLK)],
            sem,
        ).start()
        return carry

    lax.fori_loop(0, rows // BLK * across, body, 0)


def wait_whole(dest, sem):
    pltpu.make_async_copy(dest, dest, sem).wait()


def head_lanes(rows, head):
    lane = lax.broadcasted_iota(jnp.int32, (rows, BLK), 1)
    return (lane < HD) if head == 0 else (lane >= HD)


def chunk_plan(rows, nbits):
    if nbits != 4:
        return [(0, rows, list(range(nbits - 1, -1, -1)))]
    A = [3, 2, 0, 1]; B = [3, 2, 1, 0]; C = [0, 1, 3, 2]; D = [1, 0, 3, 2]
    orders = [A, B, C, D, A, B]
    unit = rows // 16
    sizes = [768, 768, 512, 512, 768]
    sizes.append(rows - sum(sizes))
    out = []; s = 0
    for z, o in zip(sizes, orders):
        out.append((s, z, o)); s += z
    return out

def tree_info(order):
    n = len(order)
    stage = {b: t for t, b in enumerate(order)}
    def last(m):
        return max([stage[b] for b in range(n) if m >> b & 1], default=-1)
    return stage, last

def gather_kernel(plan, nbits, rows, x_ref, out_ref, ssem, rsem, ssib, rsib, lsem):
    me = lax.axis_index("dp"); core = lax.axis_index("opt")
    bar = pltpu.get_barrier_semaphore()
    for b in range(nbits):
        pl.semaphore_signal(bar, inc=1, device_id=(me ^ (1 << b), core), device_id_type=MESH)
    pl.semaphore_signal(bar, inc=1, device_id=(me, 1 - core), device_id_type=MESH)
    pl.semaphore_wait(bar, nbits + 1)
    nm = 1 << nbits
    def region(c, m, o=None):
        s, z, _ = plan[c]
        dev = (me ^ m) * 2 + (core if o is None else o)
        return out_ref.at[pl.ds(pl.multiple_of(dev * rows + s, 16), z)]
    def own(c):
        s, z, _ = plan[c]
        return x_ref.at[pl.ds(s, z)]
    waits = []
    events = []
    for c, (s, z, order) in enumerate(plan):
        stage, last = tree_info(order)
        for m in range(nm):
            events.append((last(m) * 2 + (c if last(m) >= 0 else 0), c, m))
    events.sort()
    idx = {c: 0 for c in range(len(plan))}
    local = []
    for _, c, m in events:
        s, z, order = plan[c]
        stage, last = tree_info(order)
        if m:
            b = order[last(m)]
            pltpu.make_async_remote_copy(region(c, m), region(c, m), ssem.at[c, 0], rsem.at[c, m], device_id=(me ^ (1 << b), core), device_id_type=MESH).wait_recv()
        src = region(c, m) if m else own(c)
        for t in range(last(m) + 1, nbits):
            b = order[t]
            cp = pltpu.make_async_remote_copy(src, region(c, m), ssem.at[c, idx[c]], rsem.at[c, m | (1 << b)], device_id=(me ^ (1 << b), core), device_id_type=MESH)
            cp.start(); waits.append(cp); idx[c] += 1
        cp = pltpu.make_async_remote_copy(src, region(c, m), ssib.at[c, m], rsib.at[c, m], device_id=(me, 1 - core), device_id_type=MESH)
        cp.start(); waits.append(cp)
        if m == 0:
            cp = pltpu.make_async_copy(src, region(c, 0), lsem.at[c]); cp.start(); local.append(cp)
    for c in range(len(plan)):
        for m in range(nm):
            r = region(c, m, 1 - core)
            pltpu.make_async_remote_copy(r, r, ssib.at[c, m], rsib.at[c, m], device_id=(me, 1 - core), device_id_type=MESH).wait_recv()
    for cp in waits: cp.wait_send()
    for cp in local: cp.wait()

def gather_rows(x, dp_count, cid):
    rows = x.shape[0]
    nbits = dp_count.bit_length() - 1
    plan = chunk_plan(rows, nbits)
    nm = 1 << nbits; nc = len(plan)
    return pl.pallas_call(functools.partial(gather_kernel, plan, nbits, rows),
        out_shape=jax.ShapeDtypeStruct((dp_count * 2 * rows, 128), x.dtype),
        in_specs=[pl.BlockSpec(memory_space=pl.ANY)], out_specs=pl.BlockSpec(memory_space=pl.ANY),
        scratch_shapes=[pltpu.SemaphoreType.DMA((nc, nm)), pltpu.SemaphoreType.DMA((nc, nm)), pltpu.SemaphoreType.DMA((nc, nm)), pltpu.SemaphoreType.DMA((nc, nm)), pltpu.SemaphoreType.DMA((nc,))],
        name="gather_rows",
        compiler_params=pltpu.CompilerParams(collective_id=cid, has_side_effects=True))(x)

def scatter_kernel(plan, nbits, rows, s_ref, out_ref, own, sib, land, ssem, rsem, ssib, rsib, lsem):
    me = lax.axis_index("dp"); core = lax.axis_index("opt")
    bar = pltpu.get_barrier_semaphore()
    for b in range(nbits):
        pl.semaphore_signal(bar, inc=1, device_id=(me ^ (1 << b), core), device_id_type=MESH)
    pl.semaphore_signal(bar, inc=1, device_id=(me, 1 - core), device_id_type=MESH)
    nm = 1 << nbits
    def src(c, m, o):
        s, z, _ = plan[c]
        dev = (me ^ m) * 2 + o
        return s_ref.at[pl.ds(pl.multiple_of(dev * rows + s, 16), z)]
    def send_stage(order, m):
        rev = order[::-1]
        return min([t for t in range(nbits) if m >> rev[t] & 1], default=nbits)
    events = sorted((send_stage(order, m) * 2 + c, c, m) for c, (s, z, order) in enumerate(plan) for m in range(nm))
    loads = {}
    for _, c, m in events:
        s, z, _o = plan[c]
        cp = pltpu.make_async_copy(src(c, m, core), own.at[m, pl.ds(s, z)], lsem.at[c, m]); cp.start(); loads[c, m] = cp
    pl.semaphore_wait(bar, nbits + 1)
    sends = []
    for _, c, m in events:
        s, z, _o = plan[c]
        cp = pltpu.make_async_remote_copy(src(c, m, 1 - core), sib.at[m, pl.ds(s, z)], ssib.at[c, m], rsib.at[c, m], device_id=(me, 1 - core), device_id_type=MESH)
        cp.start(); sends.append(cp)
    for _, c, m in events:
        s, z, order = plan[c]
        rev = order[::-1]
        st = send_stage(order, m)
        loads[c, m].wait()
        here = own.at[m, pl.ds(s, z)]
        pltpu.make_async_remote_copy(here, sib.at[m, pl.ds(s, z)], ssib.at[c, m], rsib.at[c, m], device_id=(me, 1 - core), device_id_type=MESH).wait_recv()
        terms = [own.at[m], sib.at[m]]
        for t in range(st):
            mm = m | (1 << rev[t])
            pltpu.make_async_remote_copy(here, land.at[mm - 1, pl.ds(s, z)], ssem.at[c, mm], rsem.at[c, mm], device_id=(me ^ (1 << rev[t]), core), device_id_type=MESH).wait_recv()
            terms.append(land.at[mm - 1])
        step = 128
        def add(i, k):
            r = pl.ds(pl.multiple_of(s + i * step, 16), k)
            total = terms[0][r, :].astype(jnp.float32) + terms[1][r, :].astype(jnp.float32)
            for x in terms[2:]:
                total = total + x[r, :].astype(jnp.float32)
            if m:
                own[m, r, :] = total.astype(jnp.bfloat16)
            else:
                out_ref[r, :] = total
        def body(i, carry):
            add(i, step); return carry
        lax.fori_loop(0, z // step, body, 0)
        if z % step:
            add(z // step, z % step)
        if m:
            cp = pltpu.make_async_remote_copy(here, land.at[m - 1, pl.ds(s, z)], ssem.at[c, m], rsem.at[c, m], device_id=(me ^ (1 << rev[st]), core), device_id_type=MESH)
            cp.start(); sends.append(cp)
    for cp in sends: cp.wait_send()

def scatter_rows(s, dp_count, cid):
    rows = s.shape[0] // (dp_count * 2)
    nbits = dp_count.bit_length() - 1
    plan = chunk_plan(rows, nbits)
    nm = 1 << nbits; nc = len(plan)
    return pl.pallas_call(functools.partial(scatter_kernel, plan, nbits, rows),
        out_shape=jax.ShapeDtypeStruct((rows, 128), jnp.float32),
        in_specs=[pl.BlockSpec(memory_space=pl.ANY)], out_specs=pl.BlockSpec(memory_space=pltpu.VMEM),
        scratch_shapes=[pltpu.VMEM((nm, rows, 128), jnp.bfloat16), pltpu.VMEM((nm, rows, 128), jnp.bfloat16), pltpu.VMEM((nm - 1, rows, 128), jnp.bfloat16)]
          + [pltpu.SemaphoreType.DMA((nc, nm))] * 5,
        name="scatter_rows",
        compiler_params=pltpu.CompilerParams(collective_id=cid, has_side_effects=True, vmem_limit_bytes=60 << 20))(s)


def strip_kernel(table, buckets, out):
    head = pl.program_id(0)
    which = buckets[...]
    total = jnp.zeros((3 * BLK, BLK), f32)
    for b in range(NB):
        total = jnp.where(which == b, table[b * H + head], total)
    out[0, 0 : 2 * BLK, :] = jnp.full((2 * BLK, BLK), table[(NB // 2 - 1) * H + head], f32)
    out[0, 2 * BLK : 5 * BLK, :] = total
    out[0, 5 * BLK :, :] = jnp.full((2 * BLK, BLK), table[(NB - 1) * H + head], f32)


def bias_strips(table):
    return pl.pallas_call(
        strip_kernel,
        grid=(H,),
        in_specs=[
            pl.BlockSpec(memory_space=pltpu.SMEM),
            pl.BlockSpec((3 * BLK, BLK), lambda h: (0, 0)),
        ],
        out_specs=pl.BlockSpec((1, STRIP, BLK), lambda h: (h, 0, 0)),
        out_shape=jax.ShapeDtypeStruct((H, STRIP, BLK), f32),
        name="bias_strips",
    )(table, jnp.asarray(strip_buckets()))


def masked_scores(keys, queries, strip, offset, length):
    rows = keys.shape[0]
    scores = dot_nt(keys, queries)
    bias = jnp.concatenate(
        [strip[(3 - n) * BLK : (3 - n) * BLK + rows, :] for n in (offset, offset + 1)], axis=1
    )
    key_at = lax.broadcasted_iota(jnp.int32, scores.shape, 0)
    return jnp.where(key_at < length, scores + bias, neg_fill)


def attend_kernel(rows_ref, lengths, x_ref, gathered, gains, strips, qkv, lse, mixed, hidden, wqkv, wout, sems):
    step = pl.program_id(0)

    @pl.when(step == 0)
    def _():
        for m in range(3):
            start_blocks(rows_ref, gathered, ENC_QKV + 36 * m, D, D, wqkv.at[m], sems.at[m])
        start_blocks(rows_ref, gathered, ENC_OUT, D, D, wout, sems.at[3])

    values = x_ref[...].astype(f32)
    normed = to_low(rms_scale(values, gains[0:1, :]))
    for m in range(3):

        @pl.when(step == 0)
        def _(m=m):
            wait_whole(wqkv.at[m], sems.at[m])

        qkv[:, m * D : (m + 1) * D] = to_low(dot(normed, wqkv[m]))
    length = lengths[step]

    def one_pair(pair, carry):
        at = pl.multiple_of(pair * BLK, BLK)
        queries = qkv[:, pl.ds(at, BLK)]
        keys = qkv[:, pl.ds(pl.multiple_of(at + D, BLK), BLK)]
        turned = qkv[:, pl.ds(pl.multiple_of(at + 2 * D, BLK), BLK)].T
        for n in range(2):
            part = queries[n * 256 : (n + 1) * 256]
            outs = []
            for head in range(2):
                only = jnp.where(head_lanes(256, head), part, jnp.zeros_like(part))
                scores = masked_scores(keys, only, strips.at[2 * pair + head], 2 * n, length)
                peak = jnp.max(scores, axis=0, keepdims=True)
                expos = jnp.exp(scores - peak)
                total = jnp.sum(expos, axis=0, keepdims=True)
                lse[0, pl.ds(2 * pair + head, 1), n * 256 : (n + 1) * 256] = peak + jnp.log(total)
                outs.append(dot(turned, to_low(expos * (1.0 / total))))
            lane = lax.broadcasted_iota(jnp.int32, (BLK, 256), 0)
            both = jnp.where(lane < HD, outs[0], outs[1])
            mixed[n * 256 : (n + 1) * 256, pl.ds(at, BLK)] = to_low(both.T)
        return carry

    lax.fori_loop(0, PAIRS, one_pair, 0)

    @pl.when(step == 0)
    def _():
        wait_whole(wout, sems.at[3])

    hidden[...] = x_ref[...].astype(f32) + dot(mixed[...], wout[...])


def encoder_attend(rows, lengths, enc_in, gathered, gains, strips):
    count = lengths.shape[0]
    total = count * PASS_SLOT
    by_row = lambda p, *_: (p, 0)
    return pl.pallas_call(
        attend_kernel,
        grid_spec=pltpu.PrefetchScalarGridSpec(
            num_scalar_prefetch=2,
            grid=(count,),
            in_specs=[
                pl.BlockSpec((PASS_SLOT, D), by_row),
                pl.BlockSpec(memory_space=pl.ANY),
                pl.BlockSpec((8, D), lambda p, *_: (0, 0)),
                pl.BlockSpec((H, STRIP, BLK), lambda p, *_: (0, 0, 0)),
            ],
            out_specs=[
                pl.BlockSpec((PASS_SLOT, 3 * D), by_row),
                pl.BlockSpec((1, 16, PASS_SLOT), lambda p, *_: (p, 0, 0)),
                pl.BlockSpec((PASS_SLOT, D), by_row),
                pl.BlockSpec((PASS_SLOT, D), by_row),
            ],
            scratch_shapes=[
                pltpu.VMEM((3, D, D), bf16),
                pltpu.VMEM((D, D), bf16),
                pltpu.SemaphoreType.DMA((4,)),
            ],
        ),
        out_shape=[
            jax.ShapeDtypeStruct((total, 3 * D), bf16),
            jax.ShapeDtypeStruct((count, 16, PASS_SLOT), f32),
            jax.ShapeDtypeStruct((total, D), bf16),
            jax.ShapeDtypeStruct((total, D), f32),
        ],
        compiler_params=pltpu.CompilerParams(vmem_limit_bytes=VMEM_CAP),
        name="encoder_attend",
    )(rows, lengths, enc_in, gathered, gains, strips)


FCHUNK = 512


def feed_kernel(rows_ref, hidden, gathered, gains, inner, output, encoded, cross, wup, wdown, wkv, sems):
    step = pl.program_id(0)

    @pl.when(step == 0)
    def _():
        start_blocks(rows_ref, gathered, ENC_UP, D, FF, wup, sems.at[0])
        start_blocks(rows_ref, gathered, ENC_DOWN, FF, D, wdown, sems.at[1])
        for m in range(2):
            start_blocks(rows_ref, gathered, CROSS_KV + 36 * m, D, D, wkv.at[m], sems.at[2 + m])

    normed = to_low(rms_scale(hidden[...], gains[1:2, :]))

    @pl.when(step == 0)
    def _():
        wait_whole(wup, sems.at[0])
        wait_whole(wdown, sems.at[1])

    total = hidden[...]
    for c in range(FF // FCHUNK):
        cols = slice(c * FCHUNK, (c + 1) * FCHUNK)
        act = dot(normed, wup[:, cols])
        inner[:, cols] = to_low(act)
        total = total + dot(to_low(gate(act)), wdown[cols, :])
    output[...] = total
    low = to_low(rms_scale(total, gains[2:3, :]))
    encoded[...] = low
    for m in range(2):

        @pl.when(step == 0)
        def _(m=m):
            wait_whole(wkv.at[m], sems.at[2 + m])

        cross[:, m * D : (m + 1) * D] = to_low(dot(low, wkv[m]))


def encoder_feed(rows, hidden, gathered, gains):
    total = hidden.shape[0]
    tile = 256
    by_row = lambda p, *_: (p, 0)
    return pl.pallas_call(
        feed_kernel,
        grid_spec=pltpu.PrefetchScalarGridSpec(
            num_scalar_prefetch=1,
            grid=(total // tile,),
            in_specs=[
                pl.BlockSpec((tile, D), by_row),
                pl.BlockSpec(memory_space=pl.ANY),
                pl.BlockSpec((8, D), lambda p, *_: (0, 0)),
            ],
            out_specs=[
                pl.BlockSpec((tile, FF), by_row),
                pl.BlockSpec((tile, D), by_row),
                pl.BlockSpec((tile, D), by_row),
                pl.BlockSpec((tile, 2 * D), by_row),
            ],
            scratch_shapes=[
                pltpu.VMEM((D, FF), bf16),
                pltpu.VMEM((FF, D), bf16),
                pltpu.VMEM((2, D, D), bf16),
                pltpu.SemaphoreType.DMA((4,)),
            ],
        ),
        out_shape=[
            jax.ShapeDtypeStruct((total, FF), bf16),
            jax.ShapeDtypeStruct((total, D), f32),
            jax.ShapeDtypeStruct((total, D), bf16),
            jax.ShapeDtypeStruct((total, 2 * D), bf16),
        ],
        compiler_params=pltpu.CompilerParams(vmem_limit_bytes=VMEM_CAP),
        name="encoder_feed",
    )(rows, hidden, gathered, gains)


def feed_back_kernel(
    rows_ref, output, hidden, inner, upstream, gathered, gains,
    act_low, inner_grad, branch, normed, hidden_grad, attn_grad, mixed_grad, gain_sums,
    wup, wdown, wout, sems,
):
    step = pl.program_id(0)

    @pl.when(step == 0)
    def _():
        start_blocks(rows_ref, gathered, ENC_DOWN, FF, D, wdown, sems.at[0])
        start_blocks(rows_ref, gathered, ENC_UP, D, FF, wup, sems.at[1])
        start_blocks(rows_ref, gathered, ENC_OUT, D, D, wout, sems.at[2])
        gain_sums[...] = jnp.zeros_like(gain_sums)

    output_grad, final_gain = norm_back(output[...], gains[2:3, :], upstream[...])
    low = to_low(output_grad)
    branch[...] = low

    @pl.when(step == 0)
    def _():
        wait_whole(wdown, sems.at[0])
        wait_whole(wup, sems.at[1])

    total = jnp.zeros(hidden.shape, f32)
    for c in range(FF // FCHUNK):
        cols = slice(c * FCHUNK, (c + 1) * FCHUNK)
        value, slope = gate_both(inner[:, cols].astype(f32))
        act_low[:, cols] = to_low(value)
        grad = to_low(slope * dot_nt(low, wdown[cols, :]))
        inner_grad[:, cols] = grad
        total = total + dot_nt(grad, wup[:, cols])
    values = hidden[...]
    normed[...] = to_low(rms_scale(values, gains[1:2, :]))
    part, second_gain = norm_back(values, gains[1:2, :], total)
    grad = output_grad + part
    hidden_grad[...] = grad
    low = to_low(grad)
    attn_grad[...] = low

    @pl.when(step == 0)
    def _():
        wait_whole(wout, sems.at[2])

    mixed_grad[...] = to_low(dot_nt(low, wout[...]))
    gain_sums[0:1, :] += second_gain
    gain_sums[1:2, :] += final_gain


def feed_back(rows, output, hidden, inner, upstream, gathered, gains):
    total = hidden.shape[0]
    tile = 256
    by_row = lambda p, *_: (p, 0)
    fixed = lambda p, *_: (0, 0)
    row = pl.BlockSpec((tile, D), by_row)
    wide = pl.BlockSpec((tile, FF), by_row)
    return pl.pallas_call(
        feed_back_kernel,
        grid_spec=pltpu.PrefetchScalarGridSpec(
            num_scalar_prefetch=1,
            grid=(total // tile,),
            in_specs=[row, row, wide, row, pl.BlockSpec(memory_space=pl.ANY), pl.BlockSpec((8, D), fixed)],
            out_specs=[wide, wide, row, row, row, row, row, pl.BlockSpec((8, D), fixed)],
            scratch_shapes=[
                pltpu.VMEM((D, FF), bf16),
                pltpu.VMEM((FF, D), bf16),
                pltpu.VMEM((D, D), bf16),
                pltpu.SemaphoreType.DMA((3,)),
            ],
        ),
        out_shape=[
            jax.ShapeDtypeStruct((total, FF), bf16),
            jax.ShapeDtypeStruct((total, FF), bf16),
            jax.ShapeDtypeStruct((total, D), bf16),
            jax.ShapeDtypeStruct((total, D), bf16),
            jax.ShapeDtypeStruct((total, D), f32),
            jax.ShapeDtypeStruct((total, D), bf16),
            jax.ShapeDtypeStruct((total, D), bf16),
            jax.ShapeDtypeStruct((8, D), f32),
        ],
        compiler_params=pltpu.CompilerParams(vmem_limit_bytes=VMEM_CAP),
        name="feed_back",
    )(rows, output, hidden, inner, upstream, gathered, gains)


def attend_back_kernel(lengths, q_ref, k_ref, v_ref, go_ref, lse, strips, gq_ref, gk_ref, gv_ref, bias_sums):
    pair = pl.program_id(0)
    step = pl.program_id(1)

    @pl.when(step == 0)
    def _():
        bias_sums[...] = jnp.zeros_like(bias_sums)

    length = lengths[step]
    keys = k_ref[...]
    values = v_ref[...]
    turned = keys.T
    lane = lax.broadcasted_iota(jnp.int32, turned.shape, 0)
    halves = [
        jnp.where(lane < HD, turned, jnp.zeros_like(turned)),
        jnp.where(lane >= HD, turned, jnp.zeros_like(turned)),
    ]
    key_grad = jnp.zeros((PASS_SLOT, BLK), f32)
    value_grad = jnp.zeros((PASS_SLOT, BLK), f32)
    for n in range(2):
        span = slice(n * 256, (n + 1) * 256)
        query_grad = jnp.zeros((BLK, 256), f32)
        for head in range(2):
            mask = head_lanes(256, head)
            queries = jnp.where(mask, q_ref[span, :], jnp.zeros((256, BLK), bf16))
            grads = jnp.where(mask, go_ref[span, :], jnp.zeros((256, BLK), bf16))
            scores = masked_scores(keys, queries, strips.at[head], 2 * n, length)
            probs = jnp.exp(scores - lse[0, pl.ds(2 * pair + head, 1), span])
            prob_grad = dot_nt(values, grads)
            inner = jnp.sum(probs * prob_grad, axis=0, keepdims=True)
            score_grad = to_low(probs * (prob_grad - inner))
            wide = score_grad.astype(f32)
            for m in range(2):
                first = (3 - 2 * n - m) * BLK
                bias_sums[head, first : first + PASS_SLOT, :] += wide[:, m * BLK : (m + 1) * BLK]
            value_grad = value_grad + dot(to_low(probs), grads)
            key_grad = key_grad + dot(score_grad, queries)
            query_grad = query_grad + dot(halves[head], score_grad)
        gq_ref[span, :] = to_low(query_grad.T)
    gk_ref[...] = to_low(key_grad)
    gv_ref[...] = to_low(value_grad)


def attend_back(lengths, qkv, mixed_grad, lse, strips):
    count = lengths.shape[0]
    total = count * PASS_SLOT
    block = (PASS_SLOT, BLK)
    place = pl.BlockSpec(block, lambda a, p, *_: (p, a))
    return pl.pallas_call(
        attend_back_kernel,
        grid_spec=pltpu.PrefetchScalarGridSpec(
            num_scalar_prefetch=1,
            grid=(PAIRS, count),
            in_specs=[
                place,
                pl.BlockSpec(block, lambda a, p, *_: (p, a + PAIRS)),
                pl.BlockSpec(block, lambda a, p, *_: (p, a + 2 * PAIRS)),
                place,
                pl.BlockSpec((1, 16, PASS_SLOT), lambda a, p, *_: (p, 0, 0)),
                pl.BlockSpec((2, STRIP, BLK), lambda a, p, *_: (a, 0, 0)),
            ],
            out_specs=[place, place, place, pl.BlockSpec((2, STRIP, BLK), lambda a, p, *_: (a, 0, 0))],
        ),
        out_shape=[jax.ShapeDtypeStruct((total, D), bf16)] * 3
        + [jax.ShapeDtypeStruct((H, STRIP, BLK), f32)],
        compiler_params=pltpu.CompilerParams(vmem_limit_bytes=VMEM_CAP),
        name="attend_back",
    )(lengths, qkv, qkv, qkv, mixed_grad, lse, strips)


def input_back_kernel(
    rows_ref, x_ref, gq, gk, gv, hidden_grad, gathered, gains, result, normed, gain_sums, wqkv, sems
):
    step = pl.program_id(0)

    @pl.when(step == 0)
    def _():
        for m in range(3):
            start_blocks(rows_ref, gathered, ENC_QKV + 36 * m, D, D, wqkv.at[m], sems.at[m])
        gain_sums[...] = jnp.zeros_like(gain_sums)

    values = x_ref[...].astype(f32)
    normed[...] = to_low(rms_scale(values, gains[0:1, :]))
    total = jnp.zeros(values.shape, f32)
    for m, grads in enumerate((gq, gk, gv)):

        @pl.when(step == 0)
        def _(m=m):
            wait_whole(wqkv.at[m], sems.at[m])

        total = total + dot_nt(grads[...], wqkv[m])
    part, first_gain = norm_back(values, gains[0:1, :], total)
    result[...] = hidden_grad[...] + part
    gain_sums[0:1, :] += first_gain


def input_back(rows, enc_in, gq, gk, gv, hidden_grad, gathered, gains):
    total = enc_in.shape[0]
    tile = 256
    fixed = lambda p, *_: (0, 0)
    row = pl.BlockSpec((tile, D), lambda p, *_: (p, 0))
    return pl.pallas_call(
        input_back_kernel,
        grid_spec=pltpu.PrefetchScalarGridSpec(
            num_scalar_prefetch=1,
            grid=(total // tile,),
            in_specs=[row, row, row, row, row, pl.BlockSpec(memory_space=pl.ANY), pl.BlockSpec((8, D), fixed)],
            out_specs=[row, row, pl.BlockSpec((8, D), fixed)],
            scratch_shapes=[pltpu.VMEM((3, D, D), bf16), pltpu.SemaphoreType.DMA((3,))],
        ),
        out_shape=[
            jax.ShapeDtypeStruct((total, D), f32),
            jax.ShapeDtypeStruct((total, D), bf16),
            jax.ShapeDtypeStruct((8, D), f32),
        ],
        compiler_params=pltpu.CompilerParams(vmem_limit_bytes=VMEM_CAP),
        name="input_back",
    )(rows, enc_in, gq, gk, gv, hidden_grad, gathered, gains)


HROWS = H * AROWS
SIDE = D + 2 * BLK


def spread_heads(rows):
    lane = lax.broadcasted_iota(jnp.int32, rows.shape, 1)
    zero = jnp.zeros_like(rows)
    return jnp.concatenate(
        [jnp.where((lane >= h * HD) & (lane < (h + 1) * HD), rows, zero) for h in range(H)], axis=0
    )


def gather_heads(spread):
    lane = lax.broadcasted_iota(jnp.int32, (AROWS, D), 1)
    total = jnp.zeros((AROWS, D), f32)
    for h in range(H):
        total = jnp.where(
            (lane >= h * HD) & (lane < (h + 1) * HD), spread[h * AROWS : (h + 1) * AROWS], total
        )
    return total


def heads_to_lanes(column):
    lane = lax.broadcasted_iota(jnp.int32, (AROWS, BLK), 1)
    total = jnp.zeros((AROWS, BLK), f32)
    for h in range(H):
        total = jnp.where(lane == h, column[h * AROWS : (h + 1) * AROWS], total)
    return total


def lanes_to_heads(lanes):
    return jnp.concatenate([lanes[:, h : h + 1] for h in range(H)], axis=0)


def lanes_over_heads(lanes):
    lane = lax.broadcasted_iota(jnp.int32, (AROWS, D), 1)
    total = jnp.zeros((AROWS, D), f32)
    for h in range(H):
        total = jnp.where((lane >= h * HD) & (lane < (h + 1) * HD), lanes[:, h : h + 1], total)
    return total


def causal_scores(queries, keys, bias):
    scores = dot_nt(spread_heads(queries), keys) + bias
    row = lax.broadcasted_iota(jnp.int32, scores.shape, 0)
    key_at = lax.broadcasted_iota(jnp.int32, scores.shape, 1)
    return jnp.where(key_at <= row % AROWS, scores, neg_fill)


def self_kernel(rows_ref, dec_ref, gathered, gains, bias, qkv, mixed, first, normed, normed_two, cross, wqkv, wout, wcq, sems):
    for m in range(3):
        start_blocks(rows_ref, gathered, DEC_QKV + 36 * m, D, D, wqkv.at[m], sems.at[m])
    start_blocks(rows_ref, gathered, DEC_OUT, D, D, wout, sems.at[3])
    start_blocks(rows_ref, gathered, CROSS_Q, D, D, wcq, sems.at[4])
    values = dec_ref[...].astype(f32)
    low = to_low(rms_scale(values, gains[3:4, :]))
    normed[...] = low
    for m in range(3):
        wait_whole(wqkv.at[m], sems.at[m])
        qkv[:, m * D : (m + 1) * D] = to_low(dot(low, wqkv[m]))
    scores = causal_scores(qkv[:, 0:D], qkv[:, D : 2 * D], bias[...])
    peak = jnp.max(scores, axis=1, keepdims=True)
    expos = jnp.exp(scores - peak)
    probs = to_low(expos / jnp.sum(expos, axis=1, keepdims=True))
    heads = to_low(gather_heads(dot(probs, qkv[:, 2 * D : 3 * D])))
    mixed[...] = heads
    wait_whole(wout, sems.at[3])
    after = values + dot(heads, wout[...])
    first[...] = after
    low = to_low(rms_scale(after, gains[4:5, :]))
    normed_two[...] = low
    wait_whole(wcq, sems.at[4])
    cross[...] = to_low(dot(low, wcq[...]))


def whole_spec(shape):
    return pl.BlockSpec(shape, lambda *_: (0,) * len(shape))


def decoder_call(body, name, rows, ins, outs, scratch):
    specs = [pl.BlockSpec(memory_space=pl.ANY) if x.shape[0] > 65536 else whole_spec(x.shape) for x in ins]
    return pl.pallas_call(
        body,
        grid_spec=pltpu.PrefetchScalarGridSpec(
            num_scalar_prefetch=1,
            grid=(1,),
            in_specs=specs,
            out_specs=[whole_spec(shape) for shape, kind in outs],
            scratch_shapes=scratch,
        ),
        out_shape=[jax.ShapeDtypeStruct(shape, kind) for shape, kind in outs],
        compiler_params=pltpu.CompilerParams(vmem_limit_bytes=VMEM_CAP),
        name=name,
    )(rows, *ins)


def decoder_self(rows, dec_rows, gathered, gains, bias):
    low, full = ((AROWS, D), bf16), ((AROWS, D), f32)
    square = pltpu.VMEM((D, D), bf16)
    return decoder_call(
        self_kernel, "decoder_self", rows, (dec_rows, gathered, gains, bias),
        [((AROWS, 3 * D), bf16), low, full, low, low, low],
        [pltpu.VMEM((3, D, D), bf16), square, square, pltpu.SemaphoreType.DMA((5,))],
    )


def cross_kernel(lengths, offsets, queries, memory, result):
    length = lengths[pl.program_id(0)]
    scores = dot_nt(spread_heads(queries[0]), memory[:, 0:D])
    key_at = lax.broadcasted_iota(jnp.int32, scores.shape, 1)
    scores = jnp.where(key_at < length, scores, neg_fill)
    peak = jnp.max(scores, axis=1, keepdims=True)
    expos = jnp.exp(scores - peak)
    result[0, :, 0:D] = gather_heads(dot(to_low(expos), memory[:, D : 2 * D]))
    result[0, :, D : D + BLK] = heads_to_lanes(peak)
    result[0, :, D + BLK :] = heads_to_lanes(jnp.sum(expos, axis=1, keepdims=True))


def cross_attend(lengths, offsets, queries, memory):
    count = lengths.shape[0]
    at_offset = lambda p, lens, offs: (offs[p], 0, 0)
    return pl.pallas_call(
        cross_kernel,
        grid_spec=pltpu.PrefetchScalarGridSpec(
            num_scalar_prefetch=2,
            grid=(count,),
            in_specs=[
                pl.BlockSpec((1, AROWS, D), at_offset),
                pl.BlockSpec((PASS_SLOT, 2 * D), lambda p, *_: (p, 0)),
            ],
            out_specs=pl.BlockSpec((1, AROWS, SIDE), at_offset),
        ),
        out_shape=jax.ShapeDtypeStruct((count, AROWS, SIDE), f32),
        compiler_params=pltpu.CompilerParams(vmem_limit_bytes=VMEM_CAP),
        name="cross_attend",
    )(lengths, offsets, queries, memory)


def feed_decoder_kernel(
    rows_ref, parts, first, dec_cot, valid, gathered, gains,
    result, mixed, normed, act_low, inner_grad, branch, cross_grad, back, second_grad, gain_sums,
    wout, wup, wdown, sems,
):
    start_blocks(rows_ref, gathered, CROSS_OUT, D, D, wout, sems.at[0])
    start_blocks(rows_ref, gathered, DEC_UP, D, FF, wup, sems.at[1])
    start_blocks(rows_ref, gathered, DEC_DOWN, FF, D, wdown, sems.at[2])
    peaks = [parts[k, :, D : D + BLK] for k in range(PASS_EX)]
    peak = functools.reduce(jnp.maximum, peaks)
    scales = [jnp.exp(one - peak) for one in peaks]
    total = sum(parts[k, :, D + BLK :] * scales[k] for k in range(PASS_EX))
    lane = lax.broadcasted_iota(jnp.int32, total.shape, 1)
    total = jnp.where(lane < H, total, 1.0)
    heads = sum(parts[k, :, 0:D] * lanes_over_heads(scales[k] / total) for k in range(PASS_EX))
    low = to_low(heads)
    mixed[...] = low
    wait_whole(wout, sems.at[0])
    second = first[...] + dot(low, wout[...])
    low = to_low(rms_scale(second, gains[5:6, :]))
    normed[...] = low
    output_grad = dec_cot[...].astype(f32) * valid[:, 0:1]
    grad_low = to_low(output_grad)
    branch[...] = grad_low
    wait_whole(wup, sems.at[1])
    wait_whole(wdown, sems.at[2])
    after = second
    back_sum = jnp.zeros((AROWS, D), f32)
    for c in range(FF // D):
        cols = slice(c * D, (c + 1) * D)
        value, slope = gate_both(dot(low, wup[:, cols]))
        value = to_low(value)
        act_low[:, cols] = value
        after = after + dot(value, wdown[cols, :])
        grad = to_low(slope * dot_nt(grad_low, wdown[cols, :]))
        inner_grad[:, cols] = grad
        back_sum = back_sum + dot_nt(grad, wup[:, cols])
    result[...] = to_low(after)
    part, gain_grad = norm_back(second, gains[5:6, :], back_sum)
    grad = output_grad + part
    second_grad[...] = grad
    gain_sums[...] = jnp.broadcast_to(gain_grad, gain_sums.shape)
    low = to_low(grad)
    cross_grad[...] = low
    head_grad = to_low(dot_nt(low, wout[...])).astype(f32)
    back[:, 0:D] = head_grad
    back[:, D : D + BLK] = peak + jnp.log(total)
    product = head_grad * heads
    at = lax.broadcasted_iota(jnp.int32, (AROWS, D), 1)
    inner = jnp.zeros((AROWS, BLK), f32)
    for h in range(H):
        one = jnp.where((at >= h * HD) & (at < (h + 1) * HD), product, 0.0)
        inner = jnp.where(lane == h, jnp.sum(one, axis=1, keepdims=True), inner)
    back[:, D + BLK :] = inner


def decoder_feed(rows, parts, first, dec_cot, valid, gathered, gains):
    low, full, wide = ((AROWS, D), bf16), ((AROWS, D), f32), ((AROWS, FF), bf16)
    return decoder_call(
        feed_decoder_kernel, "decoder_feed", rows, (parts, first, dec_cot, valid, gathered, gains),
        [low, low, low, wide, wide, low, low, ((AROWS, SIDE), f32), full, ((8, D), f32)],
        [pltpu.VMEM((D, D), bf16), pltpu.VMEM((D, FF), bf16), pltpu.VMEM((FF, D), bf16), pltpu.SemaphoreType.DMA((3,))],
    )


def cross_back_kernel(
    rows_ref, lengths, offsets, queries, back, memory, enc_cot, gathered,
    memory_grad, query_grad, upstream, wkv, sems,
):
    step = pl.program_id(0)

    @pl.when(step == 0)
    def _():
        for m in range(2):
            start_blocks(rows_ref, gathered, CROSS_KV + 36 * m, D, D, wkv.at[m], sems.at[m])

    length = lengths[step]
    spread = spread_heads(queries[0])
    grads = spread_heads(to_low(back[0, :, 0:D]))
    keys = memory[:, 0:D]
    scores = dot_nt(spread, keys)
    key_at = lax.broadcasted_iota(jnp.int32, scores.shape, 1)
    scores = jnp.where(key_at < length, scores, neg_fill)
    probs = jnp.exp(scores - lanes_to_heads(back[0, :, D : D + BLK]))
    prob_grad = dot_nt(grads, memory[:, D : 2 * D])
    score_grad = to_low(probs * (prob_grad - lanes_to_heads(back[0, :, D + BLK :])))
    query_grad[0] = gather_heads(dot(score_grad, keys))
    key_low = to_low(dot_tn(score_grad, spread))
    value_low = to_low(dot_tn(to_low(probs), grads))
    memory_grad[:, 0:D] = key_low
    memory_grad[:, D : 2 * D] = value_low

    @pl.when(step == 0)
    def _():
        for m in range(2):
            wait_whole(wkv.at[m], sems.at[m])

    total = to_low(dot_nt(key_low, wkv[0]) + dot_nt(value_low, wkv[1])).astype(f32)
    row = lax.broadcasted_iota(jnp.int32, total.shape, 0)
    upstream[...] = total + jnp.where(row < length, enc_cot[...].astype(f32), 0.0)


def cross_back(rows, lengths, offsets, queries, back, memory, enc_cot, gathered):
    count = lengths.shape[0]
    total = count * PASS_SLOT
    at_offset = lambda p, rows, lens, offs: (offs[p], 0, 0)
    by_row = lambda p, *_: (p, 0)
    return pl.pallas_call(
        cross_back_kernel,
        grid_spec=pltpu.PrefetchScalarGridSpec(
            num_scalar_prefetch=3,
            grid=(count,),
            in_specs=[
                pl.BlockSpec((1, AROWS, D), at_offset),
                pl.BlockSpec((1, AROWS, SIDE), at_offset),
                pl.BlockSpec((PASS_SLOT, 2 * D), by_row),
                pl.BlockSpec((PASS_SLOT, D), by_row),
                pl.BlockSpec(memory_space=pl.ANY),
            ],
            out_specs=[
                pl.BlockSpec((PASS_SLOT, 2 * D), by_row),
                pl.BlockSpec((1, AROWS, D), at_offset),
                pl.BlockSpec((PASS_SLOT, D), by_row),
            ],
            scratch_shapes=[pltpu.VMEM((2, D, D), bf16), pltpu.SemaphoreType.DMA((2,))],
        ),
        out_shape=[
            jax.ShapeDtypeStruct((total, 2 * D), bf16),
            jax.ShapeDtypeStruct((count, AROWS, D), f32),
            jax.ShapeDtypeStruct((total, D), f32),
        ],
        compiler_params=pltpu.CompilerParams(vmem_limit_bytes=VMEM_CAP),
        name="cross_back",
    )(rows, lengths, offsets, queries, back, memory, enc_cot, gathered)


def self_back_kernel(
    rows_ref, parts, second_grad, first, dec_ref, qkv, gathered, gains, bias,
    result, cross_grad, out_grad, qkv_grad, score_grads, gain_sums, wqkv, wout, wcq, sems,
):
    start_blocks(rows_ref, gathered, CROSS_Q, D, D, wcq, sems.at[4])
    start_blocks(rows_ref, gathered, DEC_OUT, D, D, wout, sems.at[3])
    for m in range(3):
        start_blocks(rows_ref, gathered, DEC_QKV + 36 * m, D, D, wqkv.at[m], sems.at[m])
    low = to_low(parts[0] + parts[1] + parts[2])
    cross_grad[...] = low
    wait_whole(wcq, sems.at[4])
    part, second_gain = norm_back(first[...], gains[4:5, :], dot_nt(low, wcq[...]))
    first_grad = second_grad[...] + part
    low = to_low(first_grad)
    out_grad[...] = low
    wait_whole(wout, sems.at[3])
    heads_grad = spread_heads(to_low(dot_nt(low, wout[...])))
    queries = qkv[:, 0:D]
    keys = qkv[:, D : 2 * D]
    scores = causal_scores(queries, keys, bias[...])
    peak = jnp.max(scores, axis=1, keepdims=True)
    expos = jnp.exp(scores - peak)
    probs = expos / jnp.sum(expos, axis=1, keepdims=True)
    prob_grad = dot_nt(heads_grad, qkv[:, 2 * D : 3 * D])
    inner = jnp.sum(probs * prob_grad, axis=1, keepdims=True)
    score_grad = to_low(probs * (prob_grad - inner))
    score_grads[...] = score_grad.astype(f32)
    grads = (
        gather_heads(dot(score_grad, keys)),
        dot_tn(score_grad, spread_heads(queries)),
        dot_tn(to_low(probs), heads_grad),
    )
    total = jnp.zeros((AROWS, D), f32)
    for m in range(3):
        low = to_low(grads[m])
        qkv_grad[:, m * D : (m + 1) * D] = low
        wait_whole(wqkv.at[m], sems.at[m])
        total = total + dot_nt(low, wqkv[m])
    part, first_gain = norm_back(dec_ref[...].astype(f32), gains[3:4, :], total)
    result[...] = first_grad + part
    gain_sums[0:1, :] = first_gain
    gain_sums[1:2, :] = second_gain


def decoder_self_back(rows, parts, second_grad, first, dec_rows, qkv, gathered, gains, bias):
    low, full = ((AROWS, D), bf16), ((AROWS, D), f32)
    square = pltpu.VMEM((D, D), bf16)
    return decoder_call(
        self_back_kernel, "decoder_self_back", rows,
        (parts, second_grad, first, dec_rows, qkv, gathered, gains, bias),
        [full, low, low, ((AROWS, 3 * D), bf16), ((HROWS, AROWS), f32), ((8, D), f32)],
        [pltpu.VMEM((3, D, D), bf16), square, square, pltpu.SemaphoreType.DMA((5,))],
    )


def shift_kernel(way, one, two, got_one, got_two, ssem, rsem):
    size = lax.axis_size("dp")
    me = lax.axis_index("dp")
    core = lax.axis_index("opt")
    bar = pltpu.get_barrier_semaphore()
    for k in (1, 2):
        pl.semaphore_signal(bar, inc=1, device_id=((me - way * k + size) % size, core), device_id_type=MESH)
    pl.semaphore_wait(bar, 2)
    copies = []
    for k, source, dest in ((1, one, got_one), (2, two, got_two)):
        copies.append(
            pltpu.make_async_remote_copy(
                src_ref=source, dst_ref=dest, send_sem=ssem.at[k - 1], recv_sem=rsem.at[k - 1],
                device_id=((me + way * k + size) % size, core), device_id_type=MESH,
            )
        )
    for copy in copies:
        copy.start()
    for copy in copies:
        copy.wait()


def shifted(one, two, way, cid):
    vmem = pl.BlockSpec(memory_space=pltpu.VMEM)
    return pl.pallas_call(
        functools.partial(shift_kernel, way),
        in_specs=[vmem, vmem],
        out_specs=[vmem, vmem],
        out_shape=[jax.ShapeDtypeStruct(one.shape, one.dtype), jax.ShapeDtypeStruct(two.shape, two.dtype)],
        scratch_shapes=[pltpu.SemaphoreType.DMA((2,)), pltpu.SemaphoreType.DMA((2,))],
        compiler_params=pltpu.CompilerParams(collective_id=cid, has_side_effects=True),
        name="shift_rows",
    )(one, two)


def weight_kernel(first, tile, chunk, cols, has_into, rows_ref, *refs):
    if has_into:
        left, right, into, slots, turned, held, sems = refs
    else:
        left, right, slots, turned, held, sems = refs
    step = pl.program_id(0)
    steps = pl.num_programs(0)
    across = cols // BLK
    down = tile // BLK
    turned[...] = left[...].T
    parts = cols // chunk
    for c in range(parts):
        slot = c % 2
        buffer = held.at[slot]

        def drain():
            wait_whole(held.at[slot], sems.at[slot])

        if c >= 2:
            drain()
        else:
            pl.when(step > 0)(drain)
        held[slot] = to_low(dot(turned[...], right[:, c * chunk : (c + 1) * chunk]))
        for i in range(down):
            for j in range(chunk // BLK):
                row = pl.multiple_of(rows_ref[first + (step * down + i) * across + c * (chunk // BLK) + j], 16)
                pltpu.make_async_copy(
                    buffer.at[pl.ds(i * BLK, BLK), pl.ds(j * BLK, BLK)], slots.at[pl.ds(row, BLK)], sems.at[slot]
                ).start()

    @pl.when(step == steps - 1)
    def _():
        for slot in range(min(2, parts)):
            wait_whole(held.at[slot], sems.at[slot])


def weight_slots(rows, left, right, first, into, total_rows, chunk=D, tile=256):
    count, down = left.shape
    cols = right.shape[1]
    assert cols // chunk >= 2 or cols == chunk
    any_space = pl.BlockSpec(memory_space=pl.ANY)
    operands = (rows, left, right) + (() if into is None else (into,))
    if cols == chunk:
        chunk = cols // 2
    return pl.pallas_call(
        functools.partial(weight_kernel, first, tile, chunk, cols, into is not None),
        grid_spec=pltpu.PrefetchScalarGridSpec(
            num_scalar_prefetch=1,
            grid=(down // tile,),
            in_specs=[
                pl.BlockSpec((count, tile), lambda p, *_: (0, p)),
                pl.BlockSpec((count, cols), lambda p, *_: (0, 0)),
            ]
            + ([] if into is None else [any_space]),
            out_specs=any_space,
            scratch_shapes=[
                pltpu.VMEM((tile, count), bf16),
                pltpu.VMEM((2, tile, chunk), bf16),
                pltpu.SemaphoreType.DMA((2,)),
            ],
        ),
        out_shape=jax.ShapeDtypeStruct((total_rows, BLK), bf16),
        input_output_aliases={} if into is None else {3: 0},
        compiler_params=pltpu.CompilerParams(vmem_limit_bytes=VMEM_CAP),
        name="weight_slots",
    )(*operands)


def exact(left, right, dims):
    return lax.dot_general(left, right, (dims, ((), ())), precision=exact_prec, preferred_element_type=f32)


def update_kernel(slots, has_ref, sums, master, stats, roots, grads, new_stats, new_master):
    for s in range(slots):
        has = has_ref[pl.program_id(0) * slots + s]
        grad = sums[s * BLK : (s + 1) * BLK, :]
        grad = jnp.where(has > 0, grad, 0.0)
        grads[s] = grad
        new_stats[s, 0] = stat_decay * stats[s, 0] + (1.0 - stat_decay) * exact(grad, grad, ((1,), (1,)))
        new_stats[s, 1] = stat_decay * stats[s, 1] + (1.0 - stat_decay) * exact(grad, grad, ((0,), (0,)))
        shaped = exact(roots[s, 0], grad, ((1,), (0,)))
        shaped = exact(shaped, roots[s, 1], ((1,), (0,)))
        old = master[s]
        shaped_rms = jnp.sqrt(jnp.mean(shaped * shaped) + 1e-06)
        weight_rms = jnp.sqrt(jnp.mean(old * old) + 1e-06)
        new_master[s] = old - block_rate * weight_rms * shaped / shaped_rms


def update_blocks(has, sums, master, kron_stats, inverse_roots):
    count = master.shape[0]
    slots = min(4, count)
    one = pl.BlockSpec((slots, BLK, BLK), lambda p, *_: (p, 0, 0))
    two = pl.BlockSpec((slots, 2, BLK, BLK), lambda p, *_: (p, 0, 0, 0))
    return pl.pallas_call(
        functools.partial(update_kernel, slots),
        grid_spec=pltpu.PrefetchScalarGridSpec(
            num_scalar_prefetch=1,
            grid=(count // slots,),
            in_specs=[pl.BlockSpec((slots * BLK, BLK), lambda p, *_: (p, 0)), one, two, two],
            out_specs=[one, two, one],
        ),
        out_shape=[
            jax.ShapeDtypeStruct(master.shape, f32),
            jax.ShapeDtypeStruct(kron_stats.shape, f32),
            jax.ShapeDtypeStruct(master.shape, f32),
        ],
        name="update_blocks",
    )(has, sums, master, kron_stats, inverse_roots)


def gather_all(shard, dp_count):
    if dp_count == 16:
        return gather_rows(shard, dp_count, 0)
    return lax.all_gather(shard, ("dp", "opt"), axis=0, tiled=True)


def scatter_all(terms, dp_count):
    if dp_count == 16:
        return scatter_rows(terms, dp_count, 1)
    return lax.psum_scatter(terms, ("dp", "opt"), scatter_dimension=0, tiled=True).astype(f32)


def pad_rows(array, rows):
    return jnp.pad(array, ((0, rows - array.shape[0]),) + ((0, 0),) * (array.ndim - 1))


def per_device(
    enc_in,
    enc_cot,
    dec_in,
    dec_cot,
    passage_lengths,
    passage_example,
    answer_tokens,
    owner_slot,
    master,
    kron_stats,
    inverse_roots,
    small_params,
    small_moment,
):
    dp_count = lax.axis_size("dp")
    pair_count = lax.axis_size("opt")
    devices = dp_count * pair_count
    slot_dev = master.shape[0]
    small_dev = small_params.shape[0]
    dev_rows = slot_dev * BLK + EXTRA
    total_rows = devices * dev_rows
    table_size = NB * H

    padded = jnp.pad(to_low(small_params), (0, EXTRA * BLK - small_dev)).reshape(EXTRA, BLK)
    gathered = gather_all(
        jnp.concatenate([to_low(master).reshape(slot_dev * BLK, BLK), padded], axis=0), dp_count
    )
    small_all = gathered.reshape(devices, dev_rows, BLK)[:, slot_dev * BLK :]
    small_all = small_all.reshape(devices, EXTRA * BLK)[:, :small_dev].reshape(-1).astype(f32)
    gains = pad_rows(small_all[: 6 * D].reshape(6, D), 8)
    rows = (owner_slot // slot_dev * dev_rows + owner_slot % slot_dev * BLK).astype(jnp.int32)
    strips = bias_strips(small_all[6 * D : 6 * D + table_size])
    answer_at = np.arange(AROWS)
    dec_buckets = bucket_of(np.minimum(answer_at, ALEN - 1)[None, :] - np.minimum(answer_at, ALEN - 1)[:, None], False)
    dec_onehot = jnp.asarray((dec_buckets[..., None] == np.arange(NB)).reshape(-1, NB).astype(np.float32))
    dec_bias = jnp.dot(
        small_all[6 * D + table_size :].reshape(NB, H).T, dec_onehot.T, precision=exact_prec, preferred_element_type=f32
    ).reshape(HROWS, AROWS)

    dec_rows = pad_rows(dec_in, AROWS)
    dec_qkv, dec_mixed, first, dec_normed, dec_normed_two, cross_queries = decoder_self(
        rows, dec_rows, gathered, gains, dec_bias
    )
    from_one, from_two = shifted(cross_queries, cross_queries, 1, 2)
    queries = jnp.stack([cross_queries, from_one, from_two])

    owner_dp = passage_example // EX_DEV // pair_count
    offsets = ((lax.axis_index("dp") - owner_dp) % dp_count).astype(jnp.int32)
    qkv, log_total, mixed, hidden = encoder_attend(rows, passage_lengths, enc_in, gathered, gains, strips)
    inner, output, encoded, memory = encoder_feed(rows, hidden, gathered, gains)

    parts = cross_attend(passage_lengths, offsets, queries, memory)
    part_one, part_two = shifted(parts[1], parts[2], -1, 3)
    valid = (pad_rows(answer_tokens.reshape(ALEN, 1), AROWS) != 0).astype(f32)
    dec_out, cross_mixed, dec_normed_three, dec_act, dec_inner_grad, dec_branch, cross_out_grad, back, second_grad, gain_six = (
        decoder_feed(
            rows, jnp.stack([parts[0], part_one, part_two]), first, pad_rows(dec_cot, AROWS),
            jnp.broadcast_to(valid, (AROWS, BLK)), gathered, gains,
        )
    )
    back_one, back_two = shifted(back, back, 1, 4)
    memory_grad, query_parts, upstream = cross_back(
        rows, passage_lengths, offsets, queries, jnp.stack([back, back_one, back_two]), memory, enc_cot, gathered
    )
    query_one, query_two = shifted(query_parts[1], query_parts[2], -1, 5)
    dec_in_grad, cross_query_grad, dec_out_grad, dec_qkv_grad, dec_scores, gain_four = decoder_self_back(
        rows, jnp.stack([query_parts[0], query_one, query_two]), second_grad, first, dec_rows, dec_qkv, gathered, gains, dec_bias
    )

    act, inner_grad, branch, normed_two, hidden_grad, attn_grad, mixed_grad, gain_two = feed_back(
        rows, output, hidden, inner, upstream, gathered, gains
    )
    grad_query, grad_key, grad_value, bias_sums = attend_back(passage_lengths, qkv, mixed_grad, log_total, strips)
    enc_in_grad, normed, gain_one = input_back(
        rows, enc_in, grad_query, grad_key, grad_value, hidden_grad, gathered, gains
    )

    slots = None
    for left, right, at in (
        (act, branch, ENC_DOWN),
        (normed_two, inner_grad, ENC_UP),
        (mixed, attn_grad, ENC_OUT),
        (encoded, memory_grad[:, :D], CROSS_KV),
        (encoded, memory_grad[:, D:], CROSS_KV + 36),
        (normed, grad_query, ENC_QKV),
        (normed, grad_key, ENC_QKV + 36),
        (normed, grad_value, ENC_QKV + 72),
        (dec_normed, dec_qkv_grad[:, :D], DEC_QKV),
        (dec_normed, dec_qkv_grad[:, D : 2 * D], DEC_QKV + 36),
        (dec_normed, dec_qkv_grad[:, 2 * D :], DEC_QKV + 72),
        (dec_mixed, dec_out_grad, DEC_OUT),
        (dec_normed_two, cross_query_grad, CROSS_Q),
        (cross_mixed, cross_out_grad, CROSS_OUT),
        (dec_normed_three, dec_inner_grad, DEC_UP),
        (dec_act, dec_branch, DEC_DOWN),
    ):
        slots = weight_slots(rows, left, right, at, slots, total_rows)

    middle = bias_sums[:, 2 * BLK : 5 * BLK].reshape(H, -1)
    strip_onehot = jnp.asarray(strip_buckets().reshape(-1, 1) == np.arange(NB)[None, :]).astype(f32)
    enc_table = jnp.dot(middle, strip_onehot, precision=exact_prec, preferred_element_type=f32).T
    enc_table = enc_table.at[NB // 2 - 1].add(jnp.sum(bias_sums[:, : 2 * BLK], axis=(1, 2)))
    enc_table = enc_table.at[NB - 1].add(jnp.sum(bias_sums[:, 5 * BLK :], axis=(1, 2)))
    dec_table = jnp.dot(
        dec_scores.reshape(H, AROWS * AROWS), dec_onehot, precision=exact_prec, preferred_element_type=f32
    ).T
    small_terms = jnp.concatenate(
        [gain_one[0], gain_two[0], gain_two[1], gain_four[0], gain_four[1], gain_six[0], enc_table.reshape(-1), dec_table.reshape(-1)]
    )
    small_rows = jnp.pad(
        to_low(small_terms).reshape(devices, small_dev), ((0, 0), (0, EXTRA * BLK - small_dev))
    ).reshape(devices, EXTRA, BLK)
    slots = slots.reshape(devices, dev_rows, BLK).at[:, slot_dev * BLK :].set(small_rows).reshape(total_rows, BLK)

    sums = scatter_all(slots, dp_count)
    small_grads = sums[slot_dev * BLK :].reshape(-1)[:small_dev]
    here = (lax.axis_index("dp") * pair_count + lax.axis_index("opt")) * slot_dev + jnp.arange(slot_dev)
    has = jnp.any(owner_slot[None, :] == here[:, None], axis=1).astype(jnp.int32)
    block_grads, new_stats, new_master = update_blocks(has, sums, master, kron_stats, inverse_roots)
    new_moment = moment_decay * small_moment + small_grads
    new_small = small_params - small_rate * new_moment
    return (
        dec_out[:ALEN],
        encoded,
        enc_in_grad,
        dec_in_grad[:ALEN],
        block_grads,
        new_stats,
        new_master,
        small_grads,
        new_moment,
        new_small,
    )


def solution(mesh):
    placed = (
        P(("dp", "opt"), None),
        P(("dp", "opt"), None),
        P(("dp", "opt"), None),
        P(("dp", "opt"), None),
        P(("dp", "opt")),
        P(("dp", "opt")),
        P(("dp", "opt"), None),
        P(),
        P(("dp", "opt"), None, None),
        P(("dp", "opt"), None, None, None),
        P(("dp", "opt"), None, None, None),
        P(("dp", "opt")),
        P(("dp", "opt")),
    )
    return jax.shard_map(
        per_device,
        mesh=mesh,
        in_specs=placed,
        out_specs=(
            P(("dp", "opt"), None),
            P(("dp", "opt"), None),
            P(("dp", "opt"), None),
            P(("dp", "opt"), None),
            P(("dp", "opt"), None, None),
            P(("dp", "opt"), None, None, None),
            P(("dp", "opt"), None, None),
            P(("dp", "opt")),
            P(("dp", "opt")),
            P(("dp", "opt")),
        ),
        check_vma=False,
    )
```

```python
import functools

import jax
import jax.numpy as jnp
import numpy as np
from jax import lax
from jax.experimental import pallas as pl
from jax.experimental.pallas import tpu as pltpu
from jax.sharding import PartitionSpec as P

D = 768
H = 12
HD = 64
FF = 3072
NB = 32
MAXD = 128
BLK = 128
PASS_SLOT = 512
PASS_EX = 3
ALEN = 20
EX_DEV = 1
AROWS = 32
PAIRS = H // 2
STRIP = 7 * BLK
EXTRA = 16
SURE = 248

exact_prec = lax.Precision.HIGHEST
neg_fill = -1000000000.0
stat_decay = 0.95
block_rate = 0.5
moment_decay = 0.9
small_rate = 0.002
MESH = pl.DeviceIdType.MESH
VMEM_CAP = 60 << 20
f32 = jnp.float32
bf16 = jnp.bfloat16

ENC_QKV, ENC_OUT, ENC_UP, ENC_DOWN = 0, 108, 144, 288
DEC_QKV, DEC_OUT, CROSS_Q, CROSS_KV, CROSS_OUT, DEC_UP, DEC_DOWN = 432, 540, 576, 612, 684, 720, 864


def dot(left, right):
    return jnp.dot(left, right, preferred_element_type=f32)


def dot_nt(left, right):
    return lax.dot_general(left, right, (((1,), (1,)), ((), ())), preferred_element_type=f32)


def dot_tn(left, right):
    return lax.dot_general(left, right, (((0,), (0,)), ((), ())), preferred_element_type=f32)


def to_low(values):
    return values.astype(bf16)


def rms_factor(values):
    return lax.rsqrt(jnp.mean(values * values, axis=-1, keepdims=True) + 1e-06)


def rms_scale(values, gain):
    return values * rms_factor(values) * gain


def norm_back(values, gain, upstream):
    factor = rms_factor(values)
    scaled = values * factor
    lifted = upstream * gain
    inner = jnp.mean(lifted * scaled, axis=-1, keepdims=True)
    rows = factor * (lifted - scaled * inner)
    return rows, jnp.sum(upstream * scaled, axis=0, keepdims=True)


GATE_A = float(np.sqrt(2.0 / np.pi))
GATE_B = 0.044715


def gate(values):
    return 0.5 * values * (1.0 + jnp.tanh(GATE_A * (values + GATE_B * values * values * values)))


def gate_both(values):
    square = values * values
    bend = jnp.tanh(GATE_A * values * (1.0 + GATE_B * square))
    half = 0.5 * (1.0 + bend)
    slope = half + 0.5 * values * (1.0 - bend * bend) * (GATE_A * (1.0 + 3.0 * GATE_B * square))
    return values * half, slope


def bucket_of(offsets, both_sides):
    if both_sides:
        halves = NB // 2
        bucket_base = (offsets > 0) * halves
        distance = np.abs(offsets)
    else:
        halves = NB
        bucket_base = offsets * 0
        distance = np.maximum(-offsets, 0)
    exact_count = halves // 2
    widened = np.maximum(distance, 1) * 1.0
    far_bucket = exact_count + np.floor(
        np.log(widened / exact_count) / np.log(MAXD / exact_count) * (halves - exact_count)
    ).astype(np.int32)
    far_bucket = np.minimum(far_bucket, halves - 1)
    return (bucket_base + np.where(distance < exact_count, distance, far_bucket)).astype(np.int32)


def strip_buckets():
    rho = np.arange(2 * BLK, 5 * BLK)[:, None]
    return bucket_of(rho - 3 * BLK - np.arange(BLK)[None, :], True)


def start_blocks(rows_ref, gathered, first, rows, cols, dest, sem):
    across = cols // BLK

    def body(b, carry):
        i = b // across
        j = b - i * across
        source = pl.multiple_of(rows_ref[first + b], 16)
        pltpu.make_async_copy(
            gathered.at[pl.ds(source, BLK)],
            dest.at[pl.ds(pl.multiple_of(i * BLK, BLK), BLK), pl.ds(pl.multiple_of(j * BLK, BLK), BLK)],
            sem,
        ).start()
        return carry

    lax.fori_loop(0, rows // BLK * across, body, 0)


def wait_whole(dest, sem):
    pltpu.make_async_copy(dest, dest, sem).wait()


def head_lanes(rows, head):
    lane = lax.broadcasted_iota(jnp.int32, (rows, BLK), 1)
    return (lane < HD) if head == 0 else (lane >= HD)


ORDERS = {"A": (3, 2, 0, 1), "B": (3, 2, 1, 0), "C": (0, 1, 3, 2), "D": (1, 0, 3, 2)}


def chunk_plan(rows, nbits, names, shares):
    if nbits != 4:
        return [(0, rows, tuple(range(nbits - 1, -1, -1)))]
    total = sum(shares)
    plan, first = [], 0
    for k, name in enumerate(names):
        size = rows - first if k == len(names) - 1 else rows * shares[k] // total // 16 * 16
        plan.append((first, size, ORDERS[name]))
        first += size
    return plan


class Tree:
    def __init__(self, order):
        self.order, self.nbits = order, len(order)

    def last(self, m):
        return max([t for t, b in enumerate(self.order) if m >> b & 1], default=-1)

    def rank(self, m):
        t = self.last(m)
        peers = [x for x in range(1 << self.nbits) if self.last(x) == t]
        return (peers.index(m) + 0.5) / len(peers)

    def children(self, m):
        return [m | 1 << self.order[t] for t in range(self.last(m) + 1, self.nbits)]

    def bit(self, m):
        return 1 << self.order[self.last(m)]


def enter_tree(nbits):
    me, core = lax.axis_index("dp"), lax.axis_index("opt")
    barrier = pltpu.get_barrier_semaphore()
    for b in range(nbits):
        pl.semaphore_signal(barrier, inc=1, device_id=(me ^ (1 << b), core), device_id_type=MESH)
    pl.semaphore_signal(barrier, inc=1, device_id=(me, 1 - core), device_id_type=MESH)
    pl.semaphore_wait(barrier, nbits + 1)


def spread_steps(plan, nbits, rows, source, out_ref, sems):
    ssem, rsem, ssib, rsib, lsem = sems
    me, core = lax.axis_index("dp"), lax.axis_index("opt")
    masks = range(1 << nbits)
    trees = [Tree(order) for _, _, order in plan]

    def region(c, m, o):
        first, size, _ = plan[c]
        return out_ref.at[pl.ds(pl.multiple_of(((me ^ m) * 2 + o) * rows + first, 16), size)]

    def down(c, m):
        parent = m ^ trees[c].bit(m)
        return lambda sending: pltpu.make_async_remote_copy(
            (source(c) if parent == 0 else region(c, parent, core)) if sending else region(c, m, core),
            region(c, parent, core) if sending else region(c, m, core),
            ssem.at[c, m], rsem.at[c, m], device_id=(me ^ trees[c].bit(m), core), device_id_type=MESH,
        )

    def across(c, m):
        return pltpu.make_async_remote_copy(
            region(c, m, core) if m else source(c), region(c, m, core),
            ssib.at[c, m], rsib.at[c, m], device_id=(me, 1 - core), device_id_type=MESH,
        )

    def arrived(c, m):
        ref = region(c, m, 1 - core)
        return pltpu.make_async_remote_copy(
            ref, ref, ssib.at[c, m], rsib.at[c, m], device_id=(me, 1 - core), device_id_type=MESH
        )

    def keep(c):
        return pltpu.make_async_copy(source(c), region(c, 0, core), lsem.at[c, 0])

    def step(c, m):
        if m:
            down(c, m)(False).wait_recv()
        for child in trees[c].children(m):
            down(c, child)(True).start()
        across(c, m).start()
        if m == 0:
            keep(c).start()

    def end():
        for c in range(len(plan)):
            for m in masks:
                arrived(c, m).wait_recv()
                across(c, m).wait_send()
                if m:
                    down(c, m)(True).wait_send()
            keep(c).wait()

    keys = sorted((trees[c].last(m) * 100 + trees[c].rank(m) * (trees[c].last(m) + 2), c, m) for c in range(len(plan)) for m in masks)
    return [functools.partial(step, c, m) for _, c, m in keys], end


def sum_steps(plan, nbits, rows, terms_ref, put, own, sib, land, sems):
    ssem, rsem, ssib, rsib, lsem = sems
    me, core = lax.axis_index("dp"), lax.axis_index("opt")
    trees = [Tree(order) for _, _, order in plan]

    def span(c):
        return pl.ds(plan[c][0], plan[c][1])

    def source(c, m, o):
        first, size, _ = plan[c]
        return terms_ref.at[pl.ds(pl.multiple_of(((me ^ m) * 2 + o) * rows + first, 16), size)]

    def load(c, m):
        return pltpu.make_async_copy(source(c, m, core), own.at[m, span(c)], lsem.at[c, m])

    def across(c, m):
        return pltpu.make_async_remote_copy(
            source(c, m, 1 - core), sib.at[m, span(c)], ssib.at[c, m], rsib.at[c, m],
            device_id=(me, 1 - core), device_id_type=MESH,
        )

    def up(c, m):
        return pltpu.make_async_remote_copy(
            own.at[m, span(c)], land.at[m - 1, span(c)], ssem.at[c, m], rsem.at[c, m],
            device_id=(me ^ trees[c].bit(m), core), device_id_type=MESH,
        )

    def step(c, m):
        first, size, _ = plan[c]
        load(c, m).wait()
        across(c, m).wait_recv()
        arrived = [child - 1 for child in trees[c].children(m)]
        for child in reversed(trees[c].children(m)):
            up(c, child).wait_recv()

        def add(i, count):
            at = pl.ds(pl.multiple_of(first + i * BLK, 16), count)
            total = own[m, at, :].astype(f32) + sib[m, at, :].astype(f32)
            for child in arrived:
                total = total + land[child, at, :].astype(f32)
            if m:
                own[m, at, :] = to_low(total)
            else:
                put(at, total)

        def body(i, carry):
            add(i, BLK)
            return carry

        lax.fori_loop(0, size // BLK, body, 0)
        if size % BLK:
            add(size // BLK, size % BLK)
        if m:
            up(c, m).start()

    stages = lambda c, m: nbits - 1 - trees[c].last(m)
    keys = sorted(
        (stages(c, m) * 8 + trees[c].rank(m) * 8 + 2 * c, c, m) for c in range(len(plan)) for m in range(1 << nbits)
    )

    def begin():
        for _, c, m in keys:
            load(c, m).start()
            across(c, m).start()

    def end():
        for _, c, m in keys:
            across(c, m).wait_send()
            if m:
                up(c, m).wait_send()

    return begin, [functools.partial(step, c, m) for _, c, m in keys], end


def tree_sems(plan, nbits):
    return [pltpu.SemaphoreType.DMA((len(plan), 1 << nbits))] * 5


def sum_scratch(rows, nbits):
    many = 1 << nbits
    return [pltpu.VMEM((count, rows, BLK), bf16) for count in (many, many, many - 1)]


def gather_kernel(plan, nbits, rows, shard, out_ref, *sems):
    enter_tree(nbits)
    steps, end = spread_steps(plan, nbits, rows, lambda c: shard.at[pl.ds(plan[c][0], plan[c][1])], out_ref, sems)
    for step in steps:
        step()
    end()


def gather_rows(shard, dp_count, cid):
    rows = shard.shape[0]
    nbits = dp_count.bit_length() - 1
    plan = chunk_plan(rows, nbits, "ABABABCD", (1,) * 8)
    return pl.pallas_call(
        functools.partial(gather_kernel, plan, nbits, rows),
        out_shape=jax.ShapeDtypeStruct((dp_count * 2 * rows, BLK), shard.dtype),
        in_specs=[pl.BlockSpec(memory_space=pl.ANY)],
        out_specs=pl.BlockSpec(memory_space=pl.ANY),
        scratch_shapes=tree_sems(plan, nbits),
        compiler_params=pltpu.CompilerParams(collective_id=cid, has_side_effects=True),
        name="gather_rows",
    )(shard)


def total_kernel(plan, nbits, rows, terms, out_ref, own, sib, land, *sems):
    enter_tree(nbits)

    def put(at, total):
        own[0, at, :] = to_low(total)

    begin, steps, end = sum_steps(plan, nbits, rows, terms, put, own, sib, land, sems[:5])
    begin()
    for step in steps:
        step()
    more, last = spread_steps(plan, nbits, rows, lambda c: own.at[0, pl.ds(plan[c][0], plan[c][1])], out_ref, sems[5:])
    for step in more:
        step()
    end()
    last()


def total_rows_all(terms, dp_count, cid):
    rows = terms.shape[0] // (dp_count * 2)
    nbits = dp_count.bit_length() - 1
    plan = chunk_plan(rows, nbits, "ABCD", (3, 3, 1, 1))
    return pl.pallas_call(
        functools.partial(total_kernel, plan, nbits, rows),
        out_shape=jax.ShapeDtypeStruct(terms.shape, bf16),
        in_specs=[pl.BlockSpec(memory_space=pl.ANY)],
        out_specs=pl.BlockSpec(memory_space=pl.ANY),
        scratch_shapes=sum_scratch(rows, nbits) + tree_sems(plan, nbits) * 2,
        compiler_params=pltpu.CompilerParams(collective_id=cid, has_side_effects=True, vmem_limit_bytes=VMEM_CAP),
        name="total_rows",
    )(terms)


def strip_kernel(table, buckets, out):
    head = pl.program_id(0)
    which = buckets[...]
    total = jnp.zeros((3 * BLK, BLK), f32)
    for b in range(NB):
        total = jnp.where(which == b, table[b * H + head], total)
    out[0, 0 : 2 * BLK, :] = jnp.full((2 * BLK, BLK), table[(NB // 2 - 1) * H + head], f32)
    out[0, 2 * BLK : 5 * BLK, :] = total
    out[0, 5 * BLK :, :] = jnp.full((2 * BLK, BLK), table[(NB - 1) * H + head], f32)


def bias_strips(table):
    return pl.pallas_call(
        strip_kernel,
        grid=(H,),
        in_specs=[
            pl.BlockSpec(memory_space=pltpu.SMEM),
            pl.BlockSpec((3 * BLK, BLK), lambda h: (0, 0)),
        ],
        out_specs=pl.BlockSpec((1, STRIP, BLK), lambda h: (h, 0, 0)),
        out_shape=jax.ShapeDtypeStruct((H, STRIP, BLK), f32),
        name="bias_strips",
    )(table, jnp.asarray(strip_buckets()))


def masked_scores(keys, queries, strip, offset, length):
    rows = keys.shape[0]
    scores = dot_nt(keys, queries)
    bias = jnp.concatenate(
        [strip[(3 - n) * BLK : (3 - n) * BLK + rows, :] for n in (offset, offset + 1)], axis=1
    )
    key_at = lax.broadcasted_iota(jnp.int32, scores.shape, 0)
    scores = scores + bias
    return jnp.concatenate([scores[:SURE], jnp.where(key_at[SURE:] < length, scores[SURE:], neg_fill)], axis=0)


def attend_kernel(rows_ref, lengths, x_ref, gathered, gains, strips, qkv, lse, mixed, hidden, wqkv, wout, sems):
    step = pl.program_id(0)

    @pl.when(step == 0)
    def _():
        for m in range(3):
            start_blocks(rows_ref, gathered, ENC_QKV + 36 * m, D, D, wqkv.at[m], sems.at[m])
        start_blocks(rows_ref, gathered, ENC_OUT, D, D, wout, sems.at[3])

    values = x_ref[...].astype(f32)
    normed = to_low(rms_scale(values, gains[0:1, :]))
    for m in range(3):

        @pl.when(step == 0)
        def _(m=m):
            wait_whole(wqkv.at[m], sems.at[m])

        qkv[:, m * D : (m + 1) * D] = to_low(dot(normed, wqkv[m]))
    length = lengths[step]

    def one_pair(pair, carry):
        at = pl.multiple_of(pair * BLK, BLK)
        queries = qkv[:, pl.ds(at, BLK)]
        keys = qkv[:, pl.ds(pl.multiple_of(at + D, BLK), BLK)]
        turned = qkv[:, pl.ds(pl.multiple_of(at + 2 * D, BLK), BLK)].T
        for n in range(2):
            part = queries[n * 256 : (n + 1) * 256]
            outs = []
            for head in range(2):
                only = jnp.where(head_lanes(256, head), part, jnp.zeros_like(part))
                scores = masked_scores(keys, only, strips.at[2 * pair + head], 2 * n, length)
                peak = jnp.max(scores, axis=0, keepdims=True)
                expos = jnp.exp(scores - peak)
                total = jnp.sum(expos, axis=0, keepdims=True)
                lse[0, pl.ds(2 * pair + head, 1), n * 256 : (n + 1) * 256] = peak + jnp.log(total)
                outs.append(dot(turned, to_low(expos)) * (1.0 / total))
            lane = lax.broadcasted_iota(jnp.int32, (BLK, 256), 0)
            both = jnp.where(lane < HD, outs[0], outs[1])
            mixed[n * 256 : (n + 1) * 256, pl.ds(at, BLK)] = to_low(both.T)
        return carry

    lax.fori_loop(0, PAIRS, one_pair, 0)

    @pl.when(step == 0)
    def _():
        wait_whole(wout, sems.at[3])

    hidden[...] = x_ref[...].astype(f32) + dot(mixed[...], wout[...])


def encoder_attend(rows, lengths, enc_in, gathered, gains, strips):
    count = lengths.shape[0]
    total = count * PASS_SLOT
    by_row = lambda p, *_: (p, 0)
    return pl.pallas_call(
        attend_kernel,
        grid_spec=pltpu.PrefetchScalarGridSpec(
            num_scalar_prefetch=2,
            grid=(count,),
            in_specs=[
                pl.BlockSpec((PASS_SLOT, D), by_row),
                pl.BlockSpec(memory_space=pl.ANY),
                pl.BlockSpec((8, D), lambda p, *_: (0, 0)),
                pl.BlockSpec((H, STRIP, BLK), lambda p, *_: (0, 0, 0)),
            ],
            out_specs=[
                pl.BlockSpec((PASS_SLOT, 3 * D), by_row),
                pl.BlockSpec((1, 16, PASS_SLOT), lambda p, *_: (p, 0, 0)),
                pl.BlockSpec((PASS_SLOT, D), by_row),
                pl.BlockSpec((PASS_SLOT, D), by_row),
            ],
            scratch_shapes=[
                pltpu.VMEM((3, D, D), bf16),
                pltpu.VMEM((D, D), bf16),
                pltpu.SemaphoreType.DMA((4,)),
            ],
        ),
        out_shape=[
            jax.ShapeDtypeStruct((total, 3 * D), bf16),
            jax.ShapeDtypeStruct((count, 16, PASS_SLOT), f32),
            jax.ShapeDtypeStruct((total, D), bf16),
            jax.ShapeDtypeStruct((total, D), f32),
        ],
        compiler_params=pltpu.CompilerParams(vmem_limit_bytes=VMEM_CAP),
        name="encoder_attend",
    )(rows, lengths, enc_in, gathered, gains, strips)


FCHUNK = 1024


def feed_kernel(rows_ref, hidden, gathered, gains, inner, output, encoded, cross, wup, wdown, wkv, sems):
    step = pl.program_id(0)

    @pl.when(step == 0)
    def _():
        start_blocks(rows_ref, gathered, ENC_UP, D, FF, wup, sems.at[0])
        start_blocks(rows_ref, gathered, ENC_DOWN, FF, D, wdown, sems.at[1])
        for m in range(2):
            start_blocks(rows_ref, gathered, CROSS_KV + 36 * m, D, D, wkv.at[m], sems.at[2 + m])

    normed = to_low(rms_scale(hidden[...], gains[1:2, :]))

    @pl.when(step == 0)
    def _():
        wait_whole(wup, sems.at[0])
        wait_whole(wdown, sems.at[1])

    total = hidden[...]
    for c in range(FF // FCHUNK):
        cols = slice(c * FCHUNK, (c + 1) * FCHUNK)
        act = dot(normed, wup[:, cols])
        inner[:, cols] = to_low(act)
        total = total + dot(to_low(gate(act)), wdown[cols, :])
    output[...] = total
    low = to_low(rms_scale(total, gains[2:3, :]))
    encoded[...] = low
    for m in range(2):

        @pl.when(step == 0)
        def _(m=m):
            wait_whole(wkv.at[m], sems.at[2 + m])

        cross[:, m * D : (m + 1) * D] = to_low(dot(low, wkv[m]))


def encoder_feed(rows, hidden, gathered, gains):
    total = hidden.shape[0]
    tile = 512
    by_row = lambda p, *_: (p, 0)
    return pl.pallas_call(
        feed_kernel,
        grid_spec=pltpu.PrefetchScalarGridSpec(
            num_scalar_prefetch=1,
            grid=(total // tile,),
            in_specs=[
                pl.BlockSpec((tile, D), by_row),
                pl.BlockSpec(memory_space=pl.ANY),
                pl.BlockSpec((8, D), lambda p, *_: (0, 0)),
            ],
            out_specs=[
                pl.BlockSpec((tile, FF), by_row),
                pl.BlockSpec((tile, D), by_row),
                pl.BlockSpec((tile, D), by_row),
                pl.BlockSpec((tile, 2 * D), by_row),
            ],
            scratch_shapes=[
                pltpu.VMEM((D, FF), bf16),
                pltpu.VMEM((FF, D), bf16),
                pltpu.VMEM((2, D, D), bf16),
                pltpu.SemaphoreType.DMA((4,)),
            ],
        ),
        out_shape=[
            jax.ShapeDtypeStruct((total, FF), bf16),
            jax.ShapeDtypeStruct((total, D), f32),
            jax.ShapeDtypeStruct((total, D), bf16),
            jax.ShapeDtypeStruct((total, 2 * D), bf16),
        ],
        compiler_params=pltpu.CompilerParams(vmem_limit_bytes=VMEM_CAP),
        name="encoder_feed",
    )(rows, hidden, gathered, gains)


def feed_back_kernel(
    rows_ref, output, hidden, inner, upstream, gathered, gains,
    act_low, inner_grad, branch, normed, hidden_grad, attn_grad, mixed_grad, gain_sums,
    wup, wdown, wout, sems,
):
    step = pl.program_id(0)

    @pl.when(step == 0)
    def _():
        start_blocks(rows_ref, gathered, ENC_DOWN, FF, D, wdown, sems.at[0])
        start_blocks(rows_ref, gathered, ENC_UP, D, FF, wup, sems.at[1])
        start_blocks(rows_ref, gathered, ENC_OUT, D, D, wout, sems.at[2])
        gain_sums[...] = jnp.zeros_like(gain_sums)

    output_grad, final_gain = norm_back(output[...], gains[2:3, :], upstream[...])
    low = to_low(output_grad)
    branch[...] = low

    @pl.when(step == 0)
    def _():
        wait_whole(wdown, sems.at[0])
        wait_whole(wup, sems.at[1])

    total = jnp.zeros(hidden.shape, f32)
    for c in range(FF // FCHUNK):
        cols = slice(c * FCHUNK, (c + 1) * FCHUNK)
        value, slope = gate_both(inner[:, cols].astype(f32))
        act_low[:, cols] = to_low(value)
        grad = to_low(slope * dot_nt(low, wdown[cols, :]))
        inner_grad[:, cols] = grad
        total = total + dot_nt(grad, wup[:, cols])
    values = hidden[...]
    normed[...] = to_low(rms_scale(values, gains[1:2, :]))
    part, second_gain = norm_back(values, gains[1:2, :], total)
    grad = output_grad + part
    hidden_grad[...] = grad
    low = to_low(grad)
    attn_grad[...] = low

    @pl.when(step == 0)
    def _():
        wait_whole(wout, sems.at[2])

    mixed_grad[...] = to_low(dot_nt(low, wout[...]))
    gain_sums[0:1, :] += second_gain
    gain_sums[1:2, :] += final_gain


def feed_back(rows, output, hidden, inner, upstream, gathered, gains):
    total = hidden.shape[0]
    tile = 256
    by_row = lambda p, *_: (p, 0)
    fixed = lambda p, *_: (0, 0)
    row = pl.BlockSpec((tile, D), by_row)
    wide = pl.BlockSpec((tile, FF), by_row)
    return pl.pallas_call(
        feed_back_kernel,
        grid_spec=pltpu.PrefetchScalarGridSpec(
            num_scalar_prefetch=1,
            grid=(total // tile,),
            in_specs=[row, row, wide, row, pl.BlockSpec(memory_space=pl.ANY), pl.BlockSpec((8, D), fixed)],
            out_specs=[wide, wide, row, row, row, row, row, pl.BlockSpec((8, D), fixed)],
            scratch_shapes=[
                pltpu.VMEM((D, FF), bf16),
                pltpu.VMEM((FF, D), bf16),
                pltpu.VMEM((D, D), bf16),
                pltpu.SemaphoreType.DMA((3,)),
            ],
        ),
        out_shape=[
            jax.ShapeDtypeStruct((total, FF), bf16),
            jax.ShapeDtypeStruct((total, FF), bf16),
            jax.ShapeDtypeStruct((total, D), bf16),
            jax.ShapeDtypeStruct((total, D), bf16),
            jax.ShapeDtypeStruct((total, D), f32),
            jax.ShapeDtypeStruct((total, D), bf16),
            jax.ShapeDtypeStruct((total, D), bf16),
            jax.ShapeDtypeStruct((8, D), f32),
        ],
        compiler_params=pltpu.CompilerParams(vmem_limit_bytes=VMEM_CAP),
        name="feed_back",
    )(rows, output, hidden, inner, upstream, gathered, gains)


def attend_back_kernel(
    plan, nbits, rows, lengths, q_ref, k_ref, v_ref, go_ref, lse, strips, *refs
):
    if plan is None:
        gq_ref, gk_ref, gv_ref, bias_sums = refs
    else:
        terms, gq_ref, gk_ref, gv_ref, bias_sums, reduced, own, sib, land, *sems = refs
    pair = pl.program_id(0)
    step = pl.program_id(1)
    at = pair * pl.num_programs(1) + step
    total_steps = PAIRS * PASS_EX

    if plan is not None:

        def put(where, total):
            reduced[where, :] = to_low(total)

        begin, steps, end = sum_steps(plan, nbits, rows, terms, put, own, sib, land, sems)

        @pl.when(at == 0)
        def _():
            enter_tree(nbits)
            begin()

        for k in range(1, total_steps):
            some = steps[len(steps) * (k - 1) // (total_steps - 1) : len(steps) * k // (total_steps - 1)]

            @pl.when(at == k)
            def _(some=some):
                for one in some:
                    one()

    @pl.when(step == 0)
    def _():
        bias_sums[...] = jnp.zeros_like(bias_sums)

    length = lengths[step]
    keys = k_ref[...]
    values = v_ref[...]
    turned = keys.T
    lane = lax.broadcasted_iota(jnp.int32, turned.shape, 0)
    halves = [
        jnp.where(lane < HD, turned, jnp.zeros_like(turned)),
        jnp.where(lane >= HD, turned, jnp.zeros_like(turned)),
    ]
    key_grad = jnp.zeros((PASS_SLOT, BLK), f32)
    value_grad = jnp.zeros((PASS_SLOT, BLK), f32)
    for n in range(2):
        span = slice(n * 256, (n + 1) * 256)
        query_grad = jnp.zeros((BLK, 256), f32)
        for head in range(2):
            mask = head_lanes(256, head)
            queries = jnp.where(mask, q_ref[span, :], jnp.zeros((256, BLK), bf16))
            grads = jnp.where(mask, go_ref[span, :], jnp.zeros((256, BLK), bf16))
            scores = masked_scores(keys, queries, strips.at[head], 2 * n, length)
            probs = jnp.exp(scores - lse[0, pl.ds(2 * pair + head, 1), span])
            prob_grad = dot_nt(values, grads)
            inner = jnp.sum(probs * prob_grad, axis=0, keepdims=True)
            score_grad = to_low(probs * (prob_grad - inner))
            wide = score_grad.astype(f32)
            for m in range(2):
                first = (3 - 2 * n - m) * BLK
                bias_sums[head, first : first + PASS_SLOT, :] += wide[:, m * BLK : (m + 1) * BLK]
            value_grad = value_grad + dot(to_low(probs), grads)
            key_grad = key_grad + dot(score_grad, queries)
            query_grad = query_grad + dot(halves[head], score_grad)
        gq_ref[span, :] = to_low(query_grad.T)
    gk_ref[...] = to_low(key_grad)
    gv_ref[...] = to_low(value_grad)

    if plan is not None:

        @pl.when(at == total_steps - 1)
        def _():
            end()


def attend_back(lengths, qkv, mixed_grad, lse, strips, terms, dp_count, cid):
    count = lengths.shape[0]
    total = count * PASS_SLOT
    block = (PASS_SLOT, BLK)
    place = pl.BlockSpec(block, lambda a, p, *_: (p, a))
    strip = pl.BlockSpec((2, STRIP, BLK), lambda a, p, *_: (a, 0, 0))
    in_specs = [
        place,
        pl.BlockSpec(block, lambda a, p, *_: (p, a + PAIRS)),
        pl.BlockSpec(block, lambda a, p, *_: (p, a + 2 * PAIRS)),
        place,
        pl.BlockSpec((1, 16, PASS_SLOT), lambda a, p, *_: (p, 0, 0)),
        strip,
    ]
    out_specs = [place, place, place, strip]
    out_shape = [jax.ShapeDtypeStruct((total, D), bf16)] * 3 + [jax.ShapeDtypeStruct((H, STRIP, BLK), f32)]
    operands = [qkv, qkv, qkv, mixed_grad, lse, strips]
    scratch = []
    plan, nbits, rows = None, 0, 0
    params = dict(vmem_limit_bytes=VMEM_CAP)
    if dp_count == 16:
        rows = terms.shape[0] // (2 * dp_count)
        nbits = dp_count.bit_length() - 1
        plan = chunk_plan(rows, nbits, "ABCDAB", (3, 3, 2, 2, 3, 3))
        in_specs.append(pl.BlockSpec(memory_space=pl.ANY))
        out_specs.append(pl.BlockSpec((rows, BLK), lambda a, p, *_: (0, 0)))
        out_shape.append(jax.ShapeDtypeStruct((rows, BLK), bf16))
        operands.append(terms)
        scratch = sum_scratch(rows, nbits) + tree_sems(plan, nbits)
        params.update(collective_id=cid, has_side_effects=True)
    results = pl.pallas_call(
        functools.partial(attend_back_kernel, plan, nbits, rows),
        grid_spec=pltpu.PrefetchScalarGridSpec(
            num_scalar_prefetch=1,
            grid=(PAIRS, count),
            in_specs=in_specs,
            out_specs=out_specs,
            scratch_shapes=scratch,
        ),
        out_shape=out_shape,
        compiler_params=pltpu.CompilerParams(**params),
        name="attend_back",
    )(lengths, *operands)
    if plan is None:
        return *results, lax.psum_scatter(terms, ("dp", "opt"), scatter_dimension=0, tiled=True)
    return results


def input_back_kernel(
    rows_ref, x_ref, gq, gk, gv, hidden_grad, gathered, gains, result, normed, gain_sums, wqkv, sems
):
    step = pl.program_id(0)

    @pl.when(step == 0)
    def _():
        for m in range(3):
            start_blocks(rows_ref, gathered, ENC_QKV + 36 * m, D, D, wqkv.at[m], sems.at[m])
        gain_sums[...] = jnp.zeros_like(gain_sums)

    values = x_ref[...].astype(f32)
    normed[...] = to_low(rms_scale(values, gains[0:1, :]))
    total = jnp.zeros(values.shape, f32)
    for m, grads in enumerate((gq, gk, gv)):

        @pl.when(step == 0)
        def _(m=m):
            wait_whole(wqkv.at[m], sems.at[m])

        total = total + dot_nt(grads[...], wqkv[m])
    part, first_gain = norm_back(values, gains[0:1, :], total)
    result[...] = hidden_grad[...] + part
    gain_sums[0:1, :] += first_gain


def input_back(rows, enc_in, gq, gk, gv, hidden_grad, gathered, gains):
    total = enc_in.shape[0]
    tile = 256
    fixed = lambda p, *_: (0, 0)
    row = pl.BlockSpec((tile, D), lambda p, *_: (p, 0))
    return pl.pallas_call(
        input_back_kernel,
        grid_spec=pltpu.PrefetchScalarGridSpec(
            num_scalar_prefetch=1,
            grid=(total // tile,),
            in_specs=[row, row, row, row, row, pl.BlockSpec(memory_space=pl.ANY), pl.BlockSpec((8, D), fixed)],
            out_specs=[row, row, pl.BlockSpec((8, D), fixed)],
            scratch_shapes=[pltpu.VMEM((3, D, D), bf16), pltpu.SemaphoreType.DMA((3,))],
        ),
        out_shape=[
            jax.ShapeDtypeStruct((total, D), f32),
            jax.ShapeDtypeStruct((total, D), bf16),
            jax.ShapeDtypeStruct((8, D), f32),
        ],
        compiler_params=pltpu.CompilerParams(vmem_limit_bytes=VMEM_CAP),
        name="input_back",
    )(rows, enc_in, gq, gk, gv, hidden_grad, gathered, gains)


HROWS = H * AROWS
SIDE = D + 2 * BLK


def spread_heads(rows):
    lane = lax.broadcasted_iota(jnp.int32, rows.shape, 1)
    zero = jnp.zeros_like(rows)
    return jnp.concatenate(
        [jnp.where((lane >= h * HD) & (lane < (h + 1) * HD), rows, zero) for h in range(H)], axis=0
    )


def gather_heads(spread):
    lane = lax.broadcasted_iota(jnp.int32, (AROWS, D), 1)
    total = jnp.zeros((AROWS, D), f32)
    for h in range(H):
        total = jnp.where(
            (lane >= h * HD) & (lane < (h + 1) * HD), spread[h * AROWS : (h + 1) * AROWS], total
        )
    return total


def heads_to_lanes(column):
    lane = lax.broadcasted_iota(jnp.int32, (AROWS, BLK), 1)
    total = jnp.zeros((AROWS, BLK), f32)
    for h in range(H):
        total = jnp.where(lane == h, column[h * AROWS : (h + 1) * AROWS], total)
    return total


def lanes_to_heads(lanes):
    return jnp.concatenate([lanes[:, h : h + 1] for h in range(H)], axis=0)


def lanes_over_heads(lanes):
    lane = lax.broadcasted_iota(jnp.int32, (AROWS, D), 1)
    total = jnp.zeros((AROWS, D), f32)
    for h in range(H):
        total = jnp.where((lane >= h * HD) & (lane < (h + 1) * HD), lanes[:, h : h + 1], total)
    return total


def causal_scores(queries, keys, bias):
    scores = dot_nt(spread_heads(queries), keys) + bias
    row = lax.broadcasted_iota(jnp.int32, scores.shape, 0)
    key_at = lax.broadcasted_iota(jnp.int32, scores.shape, 1)
    return jnp.where(key_at <= row % AROWS, scores, neg_fill)


def self_kernel(rows_ref, dec_ref, gathered, gains, bias, qkv, mixed, first, normed, normed_two, cross, wqkv, wout, wcq, sems):
    for m in range(3):
        start_blocks(rows_ref, gathered, DEC_QKV + 36 * m, D, D, wqkv.at[m], sems.at[m])
    start_blocks(rows_ref, gathered, DEC_OUT, D, D, wout, sems.at[3])
    start_blocks(rows_ref, gathered, CROSS_Q, D, D, wcq, sems.at[4])
    values = dec_ref[...].astype(f32)
    low = to_low(rms_scale(values, gains[3:4, :]))
    normed[...] = low
    for m in range(3):
        wait_whole(wqkv.at[m], sems.at[m])
        qkv[:, m * D : (m + 1) * D] = to_low(dot(low, wqkv[m]))
    scores = causal_scores(qkv[:, 0:D], qkv[:, D : 2 * D], bias[...])
    peak = jnp.max(scores, axis=1, keepdims=True)
    expos = jnp.exp(scores - peak)
    probs = to_low(expos / jnp.sum(expos, axis=1, keepdims=True))
    heads = to_low(gather_heads(dot(probs, qkv[:, 2 * D : 3 * D])))
    mixed[...] = heads
    wait_whole(wout, sems.at[3])
    after = values + dot(heads, wout[...])
    first[...] = after
    low = to_low(rms_scale(after, gains[4:5, :]))
    normed_two[...] = low
    wait_whole(wcq, sems.at[4])
    cross[...] = to_low(dot(low, wcq[...]))


def whole_spec(shape):
    return pl.BlockSpec(shape, lambda *_: (0,) * len(shape))


def decoder_call(body, name, rows, ins, outs, scratch):
    specs = [pl.BlockSpec(memory_space=pl.ANY) if x.shape[0] > 65536 else whole_spec(x.shape) for x in ins]
    return pl.pallas_call(
        body,
        grid_spec=pltpu.PrefetchScalarGridSpec(
            num_scalar_prefetch=1,
            grid=(1,),
            in_specs=specs,
            out_specs=[whole_spec(shape) for shape, kind in outs],
            scratch_shapes=scratch,
        ),
        out_shape=[jax.ShapeDtypeStruct(shape, kind) for shape, kind in outs],
        compiler_params=pltpu.CompilerParams(vmem_limit_bytes=VMEM_CAP),
        name=name,
    )(rows, *ins)


def decoder_self(rows, dec_rows, gathered, gains, bias):
    low, full = ((AROWS, D), bf16), ((AROWS, D), f32)
    square = pltpu.VMEM((D, D), bf16)
    return decoder_call(
        self_kernel, "decoder_self", rows, (dec_rows, gathered, gains, bias),
        [((AROWS, 3 * D), bf16), low, full, low, low, low],
        [pltpu.VMEM((3, D, D), bf16), square, square, pltpu.SemaphoreType.DMA((5,))],
    )


def cross_kernel(lengths, offsets, queries, memory, result):
    length = lengths[pl.program_id(0)]
    scores = dot_nt(spread_heads(queries[0]), memory[:, 0:D])
    key_at = lax.broadcasted_iota(jnp.int32, scores.shape, 1)
    scores = jnp.where(key_at < length, scores, neg_fill)
    peak = jnp.max(scores, axis=1, keepdims=True)
    expos = jnp.exp(scores - peak)
    result[0, :, 0:D] = gather_heads(dot(to_low(expos), memory[:, D : 2 * D]))
    result[0, :, D : D + BLK] = heads_to_lanes(peak)
    result[0, :, D + BLK :] = heads_to_lanes(jnp.sum(expos, axis=1, keepdims=True))


def cross_attend(lengths, offsets, queries, memory):
    count = lengths.shape[0]
    at_offset = lambda p, lens, offs: (offs[p], 0, 0)
    return pl.pallas_call(
        cross_kernel,
        grid_spec=pltpu.PrefetchScalarGridSpec(
            num_scalar_prefetch=2,
            grid=(count,),
            in_specs=[
                pl.BlockSpec((1, AROWS, D), at_offset),
                pl.BlockSpec((PASS_SLOT, 2 * D), lambda p, *_: (p, 0)),
            ],
            out_specs=pl.BlockSpec((1, AROWS, SIDE), at_offset),
        ),
        out_shape=jax.ShapeDtypeStruct((count, AROWS, SIDE), f32),
        compiler_params=pltpu.CompilerParams(vmem_limit_bytes=VMEM_CAP),
        name="cross_attend",
    )(lengths, offsets, queries, memory)


def feed_decoder_kernel(
    rows_ref, parts, first, dec_cot, valid, gathered, gains,
    result, mixed, normed, act_low, inner_grad, branch, cross_grad, back, second_grad, gain_sums,
    wout, wup, wdown, sems,
):
    start_blocks(rows_ref, gathered, CROSS_OUT, D, D, wout, sems.at[0])
    start_blocks(rows_ref, gathered, DEC_UP, D, FF, wup, sems.at[1])
    start_blocks(rows_ref, gathered, DEC_DOWN, FF, D, wdown, sems.at[2])
    peaks = [parts[k, :, D : D + BLK] for k in range(PASS_EX)]
    peak = functools.reduce(jnp.maximum, peaks)
    scales = [jnp.exp(one - peak) for one in peaks]
    total = sum(parts[k, :, D + BLK :] * scales[k] for k in range(PASS_EX))
    lane = lax.broadcasted_iota(jnp.int32, total.shape, 1)
    total = jnp.where(lane < H, total, 1.0)
    heads = sum(parts[k, :, 0:D] * lanes_over_heads(scales[k] / total) for k in range(PASS_EX))
    low = to_low(heads)
    mixed[...] = low
    wait_whole(wout, sems.at[0])
    second = first[...] + dot(low, wout[...])
    low = to_low(rms_scale(second, gains[5:6, :]))
    normed[...] = low
    output_grad = dec_cot[...].astype(f32) * valid[:, 0:1]
    grad_low = to_low(output_grad)
    branch[...] = grad_low
    wait_whole(wup, sems.at[1])
    wait_whole(wdown, sems.at[2])
    after = second
    back_sum = jnp.zeros((AROWS, D), f32)
    for c in range(FF // D):
        cols = slice(c * D, (c + 1) * D)
        value, slope = gate_both(dot(low, wup[:, cols]))
        value = to_low(value)
        act_low[:, cols] = value
        after = after + dot(value, wdown[cols, :])
        grad = to_low(slope * dot_nt(grad_low, wdown[cols, :]))
        inner_grad[:, cols] = grad
        back_sum = back_sum + dot_nt(grad, wup[:, cols])
    result[...] = to_low(after)
    part, gain_grad = norm_back(second, gains[5:6, :], back_sum)
    grad = output_grad + part
    second_grad[...] = grad
    gain_sums[...] = jnp.broadcast_to(gain_grad, gain_sums.shape)
    low = to_low(grad)
    cross_grad[...] = low
    head_grad = to_low(dot_nt(low, wout[...])).astype(f32)
    back[:, 0:D] = head_grad
    back[:, D : D + BLK] = peak + jnp.log(total)
    product = head_grad * heads
    at = lax.broadcasted_iota(jnp.int32, (AROWS, D), 1)
    inner = jnp.zeros((AROWS, BLK), f32)
    for h in range(H):
        one = jnp.where((at >= h * HD) & (at < (h + 1) * HD), product, 0.0)
        inner = jnp.where(lane == h, jnp.sum(one, axis=1, keepdims=True), inner)
    back[:, D + BLK :] = inner


def decoder_feed(rows, parts, first, dec_cot, valid, gathered, gains):
    low, full, wide = ((AROWS, D), bf16), ((AROWS, D), f32), ((AROWS, FF), bf16)
    return decoder_call(
        feed_decoder_kernel, "decoder_feed", rows, (parts, first, dec_cot, valid, gathered, gains),
        [low, low, low, wide, wide, low, low, ((AROWS, SIDE), f32), full, ((8, D), f32)],
        [pltpu.VMEM((D, D), bf16), pltpu.VMEM((D, FF), bf16), pltpu.VMEM((FF, D), bf16), pltpu.SemaphoreType.DMA((3,))],
    )


def cross_back_kernel(
    rows_ref, lengths, offsets, queries, back, memory, enc_cot, gathered,
    memory_grad, query_grad, upstream, wkv, sems,
):
    step = pl.program_id(0)

    @pl.when(step == 0)
    def _():
        for m in range(2):
            start_blocks(rows_ref, gathered, CROSS_KV + 36 * m, D, D, wkv.at[m], sems.at[m])

    length = lengths[step]
    spread = spread_heads(queries[0])
    grads = spread_heads(to_low(back[0, :, 0:D]))
    keys = memory[:, 0:D]
    scores = dot_nt(spread, keys)
    key_at = lax.broadcasted_iota(jnp.int32, scores.shape, 1)
    scores = jnp.where(key_at < length, scores, neg_fill)
    probs = jnp.exp(scores - lanes_to_heads(back[0, :, D : D + BLK]))
    prob_grad = dot_nt(grads, memory[:, D : 2 * D])
    score_grad = to_low(probs * (prob_grad - lanes_to_heads(back[0, :, D + BLK :])))
    query_grad[0] = gather_heads(dot(score_grad, keys))
    key_low = to_low(dot_tn(score_grad, spread))
    value_low = to_low(dot_tn(to_low(probs), grads))
    memory_grad[:, 0:D] = key_low
    memory_grad[:, D : 2 * D] = value_low

    @pl.when(step == 0)
    def _():
        for m in range(2):
            wait_whole(wkv.at[m], sems.at[m])

    total = to_low(dot_nt(key_low, wkv[0]) + dot_nt(value_low, wkv[1])).astype(f32)
    row = lax.broadcasted_iota(jnp.int32, total.shape, 0)
    upstream[...] = total + jnp.where(row < length, enc_cot[...].astype(f32), 0.0)


def cross_back(rows, lengths, offsets, queries, back, memory, enc_cot, gathered):
    count = lengths.shape[0]
    total = count * PASS_SLOT
    at_offset = lambda p, rows, lens, offs: (offs[p], 0, 0)
    by_row = lambda p, *_: (p, 0)
    return pl.pallas_call(
        cross_back_kernel,
        grid_spec=pltpu.PrefetchScalarGridSpec(
            num_scalar_prefetch=3,
            grid=(count,),
            in_specs=[
                pl.BlockSpec((1, AROWS, D), at_offset),
                pl.BlockSpec((1, AROWS, SIDE), at_offset),
                pl.BlockSpec((PASS_SLOT, 2 * D), by_row),
                pl.BlockSpec((PASS_SLOT, D), by_row),
                pl.BlockSpec(memory_space=pl.ANY),
            ],
            out_specs=[
                pl.BlockSpec((PASS_SLOT, 2 * D), by_row),
                pl.BlockSpec((1, AROWS, D), at_offset),
                pl.BlockSpec((PASS_SLOT, D), by_row),
            ],
            scratch_shapes=[pltpu.VMEM((2, D, D), bf16), pltpu.SemaphoreType.DMA((2,))],
        ),
        out_shape=[
            jax.ShapeDtypeStruct((total, 2 * D), bf16),
            jax.ShapeDtypeStruct((count, AROWS, D), f32),
            jax.ShapeDtypeStruct((total, D), f32),
        ],
        compiler_params=pltpu.CompilerParams(vmem_limit_bytes=VMEM_CAP),
        name="cross_back",
    )(rows, lengths, offsets, queries, back, memory, enc_cot, gathered)


def self_back_kernel(
    rows_ref, parts, second_grad, first, dec_ref, qkv, gathered, gains, bias,
    result, cross_grad, out_grad, qkv_grad, score_grads, gain_sums, wqkv, wout, wcq, sems,
):
    start_blocks(rows_ref, gathered, CROSS_Q, D, D, wcq, sems.at[4])
    start_blocks(rows_ref, gathered, DEC_OUT, D, D, wout, sems.at[3])
    for m in range(3):
        start_blocks(rows_ref, gathered, DEC_QKV + 36 * m, D, D, wqkv.at[m], sems.at[m])
    low = to_low(parts[0] + parts[1] + parts[2])
    cross_grad[...] = low
    wait_whole(wcq, sems.at[4])
    part, second_gain = norm_back(first[...], gains[4:5, :], dot_nt(low, wcq[...]))
    first_grad = second_grad[...] + part
    low = to_low(first_grad)
    out_grad[...] = low
    wait_whole(wout, sems.at[3])
    heads_grad = spread_heads(to_low(dot_nt(low, wout[...])))
    queries = qkv[:, 0:D]
    keys = qkv[:, D : 2 * D]
    scores = causal_scores(queries, keys, bias[...])
    peak = jnp.max(scores, axis=1, keepdims=True)
    expos = jnp.exp(scores - peak)
    probs = expos / jnp.sum(expos, axis=1, keepdims=True)
    prob_grad = dot_nt(heads_grad, qkv[:, 2 * D : 3 * D])
    inner = jnp.sum(probs * prob_grad, axis=1, keepdims=True)
    score_grad = to_low(probs * (prob_grad - inner))
    score_grads[...] = score_grad.astype(f32)
    grads = (
        gather_heads(dot(score_grad, keys)),
        dot_tn(score_grad, spread_heads(queries)),
        dot_tn(to_low(probs), heads_grad),
    )
    total = jnp.zeros((AROWS, D), f32)
    for m in range(3):
        low = to_low(grads[m])
        qkv_grad[:, m * D : (m + 1) * D] = low
        wait_whole(wqkv.at[m], sems.at[m])
        total = total + dot_nt(low, wqkv[m])
    part, first_gain = norm_back(dec_ref[...].astype(f32), gains[3:4, :], total)
    result[...] = first_grad + part
    gain_sums[0:1, :] = first_gain
    gain_sums[1:2, :] = second_gain


def decoder_self_back(rows, parts, second_grad, first, dec_rows, qkv, gathered, gains, bias):
    low, full = ((AROWS, D), bf16), ((AROWS, D), f32)
    square = pltpu.VMEM((D, D), bf16)
    return decoder_call(
        self_back_kernel, "decoder_self_back", rows,
        (parts, second_grad, first, dec_rows, qkv, gathered, gains, bias),
        [full, low, low, ((AROWS, 3 * D), bf16), ((HROWS, AROWS), f32), ((8, D), f32)],
        [pltpu.VMEM((3, D, D), bf16), square, square, pltpu.SemaphoreType.DMA((5,))],
    )


def shift_kernel(way, one, two, got_one, got_two, ssem, rsem):
    size = lax.axis_size("dp")
    me = lax.axis_index("dp")
    core = lax.axis_index("opt")
    bar = pltpu.get_barrier_semaphore()
    for k in (1, 2):
        pl.semaphore_signal(bar, inc=1, device_id=((me - way * k + size) % size, core), device_id_type=MESH)
    pl.semaphore_wait(bar, 2)
    copies = []
    for k, source, dest in ((1, one, got_one), (2, two, got_two)):
        copies.append(
            pltpu.make_async_remote_copy(
                src_ref=source, dst_ref=dest, send_sem=ssem.at[k - 1], recv_sem=rsem.at[k - 1],
                device_id=((me + way * k + size) % size, core), device_id_type=MESH,
            )
        )
    for copy in copies:
        copy.start()
    for copy in copies:
        copy.wait()


def shifted(one, two, way, cid):
    vmem = pl.BlockSpec(memory_space=pltpu.VMEM)
    return pl.pallas_call(
        functools.partial(shift_kernel, way),
        in_specs=[vmem, vmem],
        out_specs=[vmem, vmem],
        out_shape=[jax.ShapeDtypeStruct(one.shape, one.dtype), jax.ShapeDtypeStruct(two.shape, two.dtype)],
        scratch_shapes=[pltpu.SemaphoreType.DMA((2,)), pltpu.SemaphoreType.DMA((2,))],
        compiler_params=pltpu.CompilerParams(collective_id=cid, has_side_effects=True),
        name="shift_rows",
    )(one, two)


SQUARE = D * D // BLK
GROUP_ONE = 2 * D * FF // BLK + 3 * SQUARE
SMALL_ROWS = 512
GROUP_TWO = 3 * SQUARE + SMALL_ROWS


def put_blocks(out_ref, values, at=0):
    down, across = values.shape[0] // BLK, values.shape[1] // BLK
    for i in range(down):
        for j in range(across):
            out_ref[pl.ds(at + (i * across + j) * BLK, BLK), :] = to_low(
                values[i * BLK : (i + 1) * BLK, j * BLK : (j + 1) * BLK]
            )


def up_weight_kernel(left, right, out_ref):
    put_blocks(out_ref, dot_tn(left[...], right[...]))


def up_weight(left, right):
    count = left.shape[0]
    tile = 256
    return pl.pallas_call(
        up_weight_kernel,
        grid=(D // tile,),
        in_specs=[pl.BlockSpec((count, tile), lambda p: (0, p)), pl.BlockSpec((count, FF), lambda p: (0, 0))],
        out_specs=pl.BlockSpec((tile * FF // BLK, BLK), lambda p: (p, 0)),
        out_shape=jax.ShapeDtypeStruct((GROUP_ONE, BLK), bf16),
        compiler_params=pltpu.CompilerParams(vmem_limit_bytes=VMEM_CAP),
        name="up_weight",
    )(left, right)


def down_weight_kernel(left, right, into, out_ref):
    put_blocks(out_ref, dot_tn(left[...], right[...]))


def down_weight(left, right, into):
    count = left.shape[0]
    first = D * FF // BLK // SQUARE
    return pl.pallas_call(
        down_weight_kernel,
        grid=(FF // D,),
        in_specs=[
            pl.BlockSpec((count, D), lambda p: (0, p)),
            pl.BlockSpec((count, D), lambda p: (0, 0)),
            pl.BlockSpec(memory_space=pl.ANY),
        ],
        out_specs=pl.BlockSpec((SQUARE, BLK), lambda p: (first + p, 0)),
        out_shape=jax.ShapeDtypeStruct(into.shape, bf16),
        input_output_aliases={2: 0},
        compiler_params=pltpu.CompilerParams(vmem_limit_bytes=VMEM_CAP),
        name="down_weight",
    )(left, right, into)


def square_weight_kernel(pairs, has_into, *refs):
    sources, refs = refs[: len(pairs[0])], refs[len(pairs[0]) + has_into :]
    out_ref, held, sems = refs
    step = pl.program_id(0)
    columns, products = pairs

    def fetch(k):
        source, col = columns[k]
        return pltpu.make_async_copy(sources[k].at[:, pl.ds(col, D)], held.at[k], sems.at[k])

    @pl.when(step == 0)
    def _():
        for k in range(len(columns)):
            fetch(k).start()

    seen = set()
    for m, (a, b) in enumerate(products):
        fresh = [k for k in (a, b) if k not in seen]
        seen.update(fresh)

        @pl.when(step == m)
        def _(a=a, b=b, fresh=fresh):
            for k in fresh:
                fetch(k).wait()
            put_blocks(out_ref, dot_tn(held[a], held[b]))


def square_weight(operands, products, into, first, total):
    any_space = pl.BlockSpec(memory_space=pl.ANY)
    arrays = [array for array, _ in operands]
    columns = [(k, col) for k, (_, col) in enumerate(operands)]
    count = arrays[0].shape[0]
    extra = [] if into is None else [into]
    return pl.pallas_call(
        functools.partial(square_weight_kernel, (columns, products), len(extra)),
        grid=(len(products),),
        in_specs=[any_space] * (len(arrays) + len(extra)),
        out_specs=pl.BlockSpec((SQUARE, BLK), lambda p: (first + p, 0)),
        scratch_shapes=[pltpu.VMEM((len(arrays), count, D), bf16), pltpu.SemaphoreType.DMA((len(arrays),))],
        out_shape=jax.ShapeDtypeStruct((total, BLK), bf16),
        input_output_aliases={len(arrays): 0} if extra else {},
        compiler_params=pltpu.CompilerParams(vmem_limit_bytes=VMEM_CAP),
        name="square_weight",
    )(*arrays, *extra)


HELD = 16
REST = ALEN - HELD


def pack_rows(groups):
    sides = [jnp.concatenate(group, axis=1) if len(group) > 1 else group[0] for group in groups]
    main = jnp.concatenate([side[:HELD] for side in sides], axis=1)
    width = max(side.shape[1] for side in sides)
    rest = jnp.concatenate([jnp.pad(side[HELD:ALEN], ((0, 0), (0, width - side.shape[1]))) for side in sides], axis=0)
    return jnp.concatenate([main, pad_rows(rest, HELD)], axis=1)


def block_table():
    table = np.zeros((1009, 8), np.int32)
    wide = D // BLK
    early, late = 3 * wide, 5 * wide
    rows = (
        (DEC_QKV, 108, 1, 0, 0, early, late, 0),
        (DEC_OUT, 36, 1, wide, 3 * wide, early, late, 1),
        (CROSS_Q, 36, 1, 2 * wide, 4 * wide, early, late, 2),
        (DEC_UP, 144, 4, 0, wide, 12 * wide, 13 * wide, 0),
        (DEC_DOWN, 144, 4, 5 * wide, 9 * wide, 12 * wide, 16 * wide, 1),
        (CROSS_OUT, 36, 4, 10 * wide, 11 * wide, 12 * wide, 13 * wide, 2),
    )
    for first, count, kind, left, right, rest_left, rest_right, group in rows:
        for b in range(count):
            if first == DEC_QKV:
                m, k = divmod(b, 36)
                i, j = divmod(k, wide)
                j = j + wide * m
            else:
                i, j = divmod(b, 4 * wide if first == DEC_UP else wide)
            table[first + b] = (kind, 0, left + i, right + j, rest_left + i, rest_right + j, group, 0)
    for first, count, at in ((ENC_UP, 144, 0), (ENC_DOWN, 144, 144), (CROSS_KV, 72, 288), (ENC_OUT, 36, 360)):
        for b in range(count):
            table[first + b, :2] = (2, at + b)
    for b in range(108):
        table[b, :2] = (3, b)
    return table


def update_kernel(
    slots, info, early, middle, late, one, two, master, stats, roots,
    grads, new_stats, new_master, sides, held, summed, sems,
):
    step = pl.program_id(0)
    steps = pl.num_programs(0)

    def each(step, action):
        buffer = lax.rem(step, 2)
        for s in range(slots):
            at = (step * slots + s) * 8
            kind = info[at]

            def copy(source, dest, k, s=s):
                return pltpu.make_async_copy(source, dest, sems.at[buffer, s, k])

            def rows_of(left, right, s=s, at=at, copy=copy):
                for k, source in enumerate((left, right, left, right)):
                    col = pl.multiple_of(info[at + 2 + k] * BLK, BLK)
                    action(copy(source.at[:, pl.ds(col, BLK)], sides.at[buffer, s, k], k))

            def block_of(source, s=s, at=at, copy=copy):
                row = pl.multiple_of(info[at + 1] * BLK, BLK)
                action(copy(source.at[pl.ds(row, BLK)], held.at[buffer, s], 4))

            pl.when(kind == 1)(functools.partial(rows_of, early, late))
            pl.when(kind == 4)(functools.partial(rows_of, middle, middle))
            pl.when(kind == 2)(functools.partial(block_of, one))
            pl.when(kind == 3)(functools.partial(block_of, two))

    @pl.when(step == 0)
    def _():
        each(step, lambda copy: copy.start())

    @pl.when(step + 1 < steps)
    def _():
        each(step + 1, lambda copy: copy.start())

    each(step, lambda copy: copy.wait())
    buffer = lax.rem(step, 2)
    for s in range(slots):
        at = (step * slots + s) * 8
        kind = info[at]
        group = info[at + 6]

        @pl.when((kind == 1) | (kind == 4))
        def _(s=s, group=group):
            rest = sides[buffer, s, 2]
            row = lax.broadcasted_iota(jnp.int32, rest.shape, 0)
            mine = jnp.where(row % HELD // REST == group, rest, jnp.zeros_like(rest))
            summed[s] = dot_tn(sides[buffer, s, 0], sides[buffer, s, 1]) + dot_tn(mine, sides[buffer, s, 3])

        @pl.when((kind == 2) | (kind == 3))
        def _(s=s):
            summed[s] = held[buffer, s].astype(f32)

        @pl.when(kind == 0)
        def _(s=s):
            summed[s] = jnp.zeros((BLK, BLK), f32)

    for s in range(slots):
        grad = summed[s]
        low = to_low(grad)
        grads[s] = grad
        new_stats[s, 0] = stat_decay * stats[s, 0] + (1.0 - stat_decay) * dot_nt(low, low)
        new_stats[s, 1] = stat_decay * stats[s, 1] + (1.0 - stat_decay) * dot_tn(low, low)
        shaped = dot(to_low(roots[s, 0]), low)
        shaped = dot(to_low(shaped), to_low(roots[s, 1]))
        old = master[s]
        shaped_rms = jnp.sqrt(jnp.mean(shaped * shaped) + 1e-06)
        weight_rms = jnp.sqrt(jnp.mean(old * old) + 1e-06)
        new_master[s] = old - (block_rate * weight_rms / shaped_rms) * shaped


def update_blocks(info, early, middle, late, one, two, master, kron_stats, inverse_roots):
    count = master.shape[0]
    slots = min(4, count)
    depth = early.shape[0]
    any_space = pl.BlockSpec(memory_space=pl.ANY)
    block = pl.BlockSpec((slots, BLK, BLK), lambda p, *_: (p, 0, 0))
    pair = pl.BlockSpec((slots, 2, BLK, BLK), lambda p, *_: (p, 0, 0, 0))
    return pl.pallas_call(
        functools.partial(update_kernel, slots),
        grid_spec=pltpu.PrefetchScalarGridSpec(
            num_scalar_prefetch=1,
            grid=(count // slots,),
            in_specs=[any_space] * 5 + [block, pair, pair],
            out_specs=[block, pair, block],
            scratch_shapes=[
                pltpu.VMEM((2, slots, 4, depth, BLK), bf16),
                pltpu.VMEM((2, slots, BLK, BLK), bf16),
                pltpu.VMEM((slots, BLK, BLK), f32),
                pltpu.SemaphoreType.DMA((2, slots, 5)),
            ],
        ),
        out_shape=[
            jax.ShapeDtypeStruct(master.shape, f32),
            jax.ShapeDtypeStruct(kron_stats.shape, f32),
            jax.ShapeDtypeStruct(master.shape, f32),
        ],
        compiler_params=pltpu.CompilerParams(vmem_limit_bytes=VMEM_CAP),
        name="update_blocks",
    )(info, early, middle, late, one, two, master, kron_stats, inverse_roots)


def gather_all(shard, dp_count):
    if dp_count == 16:
        return gather_rows(shard, dp_count, 0)
    return lax.all_gather(shard, ("dp", "opt"), axis=0, tiled=True)


def total_all(terms, dp_count):
    if dp_count == 16:
        return total_rows_all(terms, dp_count, 1)
    return lax.psum(terms, ("dp", "opt"))


def gather_low(rows):
    return lax.all_gather(rows, ("dp", "opt"), axis=0, tiled=True)


def pad_rows(array, rows):
    return jnp.pad(array, ((0, rows - array.shape[0]),) + ((0, 0),) * (array.ndim - 1))


def per_device(
    enc_in,
    enc_cot,
    dec_in,
    dec_cot,
    passage_lengths,
    passage_example,
    answer_tokens,
    owner_slot,
    master,
    kron_stats,
    inverse_roots,
    small_params,
    small_moment,
):
    dp_count = lax.axis_size("dp")
    pair_count = lax.axis_size("opt")
    devices = dp_count * pair_count
    slot_dev = master.shape[0]
    small_dev = small_params.shape[0]
    dev_rows = slot_dev * BLK + EXTRA
    total_rows = devices * dev_rows
    table_size = NB * H

    padded = jnp.pad(to_low(small_params), (0, EXTRA * BLK - small_dev)).reshape(EXTRA, BLK)
    gathered = gather_all(
        jnp.concatenate([to_low(master).reshape(slot_dev * BLK, BLK), padded], axis=0), dp_count
    )
    small_all = gathered.reshape(devices, dev_rows, BLK)[:, slot_dev * BLK :]
    small_all = small_all.reshape(devices, EXTRA * BLK)[:, :small_dev].reshape(-1).astype(f32)
    gains = pad_rows(small_all[: 6 * D].reshape(6, D), 8)
    rows = (owner_slot // slot_dev * dev_rows + owner_slot % slot_dev * BLK).astype(jnp.int32)
    strips = bias_strips(small_all[6 * D : 6 * D + table_size])
    answer_at = np.arange(AROWS)
    dec_buckets = bucket_of(np.minimum(answer_at, ALEN - 1)[None, :] - np.minimum(answer_at, ALEN - 1)[:, None], False)
    dec_onehot = jnp.asarray((dec_buckets[..., None] == np.arange(NB)).reshape(-1, NB).astype(np.float32))
    dec_bias = jnp.dot(
        small_all[6 * D + table_size :].reshape(NB, H).T, dec_onehot.T, precision=exact_prec, preferred_element_type=f32
    ).reshape(HROWS, AROWS)

    dec_rows = pad_rows(dec_in, AROWS)
    dec_qkv, dec_mixed, first, dec_normed, dec_normed_two, cross_queries = decoder_self(
        rows, dec_rows, gathered, gains, dec_bias
    )
    from_one, from_two = shifted(cross_queries, cross_queries, 1, 2)
    early, enc_rows = lax.optimization_barrier(
        (pack_rows(((dec_normed,), (dec_mixed,), (dec_normed_two,))), enc_in)
    )
    early = gather_low(early)
    queries = jnp.stack([cross_queries, from_one, from_two])

    owner_dp = passage_example // EX_DEV // pair_count
    offsets = ((lax.axis_index("dp") - owner_dp) % dp_count).astype(jnp.int32)
    qkv, log_total, mixed, hidden = encoder_attend(rows, passage_lengths, enc_rows, gathered, gains, strips)
    inner, output, encoded, memory = encoder_feed(rows, hidden, gathered, gains)

    parts = cross_attend(passage_lengths, offsets, queries, memory)
    part_one, part_two = shifted(parts[1], parts[2], -1, 3)
    valid = (pad_rows(answer_tokens.reshape(ALEN, 1), AROWS) != 0).astype(f32)
    dec_out, cross_mixed, dec_normed_three, dec_act, dec_inner_grad, dec_branch, cross_out_grad, back, second_grad, gain_six = (
        decoder_feed(
            rows, jnp.stack([parts[0], part_one, part_two]), first, pad_rows(dec_cot, AROWS),
            jnp.broadcast_to(valid, (AROWS, BLK)), gathered, gains,
        )
    )
    middle = pack_rows(
        ((dec_normed_three, dec_inner_grad), (dec_act, dec_branch), (cross_mixed, cross_out_grad))
    )
    middle, back, early = lax.optimization_barrier((middle, back, early))
    middle = gather_low(middle)
    back_one, back_two = shifted(back, back, 1, 4)
    memory_grad, query_parts, upstream = cross_back(
        rows, passage_lengths, offsets, queries, jnp.stack([back, back_one, back_two]), memory, enc_cot, gathered
    )
    query_one, query_two = shifted(query_parts[1], query_parts[2], -1, 5)
    dec_in_grad, cross_query_grad, dec_out_grad, dec_qkv_grad, dec_scores, gain_four = decoder_self_back(
        rows, jnp.stack([query_parts[0], query_one, query_two]), second_grad, first, dec_rows, dec_qkv, gathered, gains, dec_bias
    )

    late = pack_rows(((dec_qkv_grad,), (dec_out_grad,), (cross_query_grad,)))
    late, upstream = lax.optimization_barrier((late, upstream))

    act, inner_grad, branch, normed_two, hidden_grad, attn_grad, mixed_grad, gain_two = feed_back(
        rows, output, hidden, inner, upstream, gathered, gains
    )
    late, middle, inner_grad = lax.optimization_barrier((late, middle, inner_grad))
    late = gather_low(late)
    one = up_weight(normed_two, inner_grad)
    one = down_weight(act, branch, one)
    one = square_weight(
        [(encoded, 0), (memory_grad, 0), (memory_grad, D), (mixed, 0), (attn_grad, 0)],
        [(0, 1), (0, 2), (3, 4)], one, 2 * D * FF // BLK // SQUARE, GROUP_ONE,
    )
    grad_query, grad_key, grad_value, bias_sums, one = attend_back(
        passage_lengths, qkv, mixed_grad, log_total, strips, one, dp_count, 6
    )
    one, late = lax.optimization_barrier((one, late))
    one = gather_low(one)
    enc_in_grad, normed, gain_one = input_back(
        rows, enc_in, grad_query, grad_key, grad_value, hidden_grad, gathered, gains
    )
    two = square_weight(
        [(normed, 0), (grad_query, 0), (grad_key, 0), (grad_value, 0)], [(0, 1), (0, 2), (0, 3)], None, 0, GROUP_TWO
    )

    inner_strip = bias_sums[:, 2 * BLK : 5 * BLK].reshape(H, -1)
    strip_onehot = jnp.asarray(strip_buckets().reshape(-1, 1) == np.arange(NB)[None, :]).astype(f32)
    enc_table = jnp.dot(inner_strip, strip_onehot, precision=exact_prec, preferred_element_type=f32).T
    enc_table = enc_table.at[NB // 2 - 1].add(jnp.sum(bias_sums[:, : 2 * BLK], axis=(1, 2)))
    enc_table = enc_table.at[NB - 1].add(jnp.sum(bias_sums[:, 5 * BLK :], axis=(1, 2)))
    dec_table = jnp.dot(
        dec_scores.reshape(H, AROWS * AROWS), dec_onehot, precision=exact_prec, preferred_element_type=f32
    ).T
    small_terms = jnp.concatenate(
        [gain_one[0], gain_two[0], gain_two[1], gain_four[0], gain_four[1], gain_six[0], enc_table.reshape(-1), dec_table.reshape(-1)]
    )
    small_rows = pad_rows(to_low(small_terms).reshape(-1, BLK), SMALL_ROWS)
    two = total_all(lax.dynamic_update_slice(two, small_rows, (3 * SQUARE, 0)), dp_count)

    device = lax.axis_index("dp") * pair_count + lax.axis_index("opt")
    small_grads = lax.dynamic_slice(two[3 * SQUARE :].reshape(-1), (device * small_dev,), (small_dev,)).astype(f32)
    here = device * slot_dev + jnp.arange(slot_dev)
    place = jnp.where(owner_slot[None, :] == here[:, None], jnp.arange(owner_slot.shape[0])[None, :] + 1, 0)
    block_at = jnp.sum(place, axis=1)
    info = jnp.asarray(np.roll(block_table(), 1, axis=0))[block_at].reshape(-1)
    block_grads, new_stats, new_master = update_blocks(info, early, middle, late, one, two, master, kron_stats, inverse_roots)
    new_moment = moment_decay * small_moment + small_grads
    new_small = small_params - small_rate * new_moment
    return (
        dec_out[:ALEN],
        encoded,
        enc_in_grad,
        dec_in_grad[:ALEN],
        block_grads,
        new_stats,
        new_master,
        small_grads,
        new_moment,
        new_small,
    )


def solution(mesh):
    placed = (
        P(("dp", "opt"), None),
        P(("dp", "opt"), None),
        P(("dp", "opt"), None),
        P(("dp", "opt"), None),
        P(("dp", "opt")),
        P(("dp", "opt")),
        P(("dp", "opt"), None),
        P(),
        P(("dp", "opt"), None, None),
        P(("dp", "opt"), None, None, None),
        P(("dp", "opt"), None, None, None),
        P(("dp", "opt")),
        P(("dp", "opt")),
    )
    return jax.shard_map(
        per_device,
        mesh=mesh,
        in_specs=placed,
        out_specs=(
            P(("dp", "opt"), None),
            P(("dp", "opt"), None),
            P(("dp", "opt"), None),
            P(("dp", "opt"), None),
            P(("dp", "opt"), None, None),
            P(("dp", "opt"), None, None, None),
            P(("dp", "opt"), None, None),
            P(("dp", "opt")),
            P(("dp", "opt")),
            P(("dp", "opt")),
        ),
        check_vma=False,
    )
```

```python
import functools

import jax
import jax.numpy as jnp
import numpy as np
from jax import lax
from jax.experimental import pallas as pl
from jax.experimental.pallas import tpu as pltpu
from jax.sharding import PartitionSpec as P

D = 768
H = 12
HD = 64
FF = 3072
NB = 32
MAXD = 128
BLK = 128
PASS_SLOT = 512
PASS_EX = 3
ALEN = 20
EX_DEV = 1
AROWS = 32
PAIRS = H // 2
STRIP = 7 * BLK
EXTRA = 16
SURE = 248
EARLY_SLOTS = 22

exact_prec = lax.Precision.HIGHEST
neg_fill = -1000000000.0
stat_decay = 0.95
block_rate = 0.5
moment_decay = 0.9
small_rate = 0.002
MESH = pl.DeviceIdType.MESH
VMEM_CAP = 60 << 20
f32 = jnp.float32
bf16 = jnp.bfloat16

ENC_QKV, ENC_OUT, ENC_UP, ENC_DOWN = 0, 108, 144, 288
DEC_QKV, DEC_OUT, CROSS_Q, CROSS_KV, CROSS_OUT, DEC_UP, DEC_DOWN = 432, 540, 576, 612, 684, 720, 864


def dot(left, right):
    return jnp.dot(left, right, preferred_element_type=f32)


def dot_nt(left, right):
    return lax.dot_general(left, right, (((1,), (1,)), ((), ())), preferred_element_type=f32)


def dot_tn(left, right):
    return lax.dot_general(left, right, (((0,), (0,)), ((), ())), preferred_element_type=f32)


def to_low(values):
    return values.astype(bf16)


def rms_factor(values):
    return lax.rsqrt(jnp.mean(values * values, axis=-1, keepdims=True) + 1e-06)


def rms_scale(values, gain):
    return values * rms_factor(values) * gain


def norm_back(values, gain, upstream):
    factor = rms_factor(values)
    scaled = values * factor
    lifted = upstream * gain
    inner = jnp.mean(lifted * scaled, axis=-1, keepdims=True)
    rows = factor * (lifted - scaled * inner)
    return rows, jnp.sum(upstream * scaled, axis=0, keepdims=True)


GATE_A = float(np.sqrt(2.0 / np.pi))
GATE_B = 0.044715


def gate(values):
    return 0.5 * values * (1.0 + jnp.tanh(GATE_A * (values + GATE_B * values * values * values)))


def gate_both(values):
    square = values * values
    bend = jnp.tanh(GATE_A * values * (1.0 + GATE_B * square))
    half = 0.5 * (1.0 + bend)
    slope = half + 0.5 * values * (1.0 - bend * bend) * (GATE_A * (1.0 + 3.0 * GATE_B * square))
    return values * half, slope


def bucket_of(offsets, both_sides):
    if both_sides:
        halves = NB // 2
        bucket_base = (offsets > 0) * halves
        distance = np.abs(offsets)
    else:
        halves = NB
        bucket_base = offsets * 0
        distance = np.maximum(-offsets, 0)
    exact_count = halves // 2
    widened = np.maximum(distance, 1) * 1.0
    far_bucket = exact_count + np.floor(
        np.log(widened / exact_count) / np.log(MAXD / exact_count) * (halves - exact_count)
    ).astype(np.int32)
    far_bucket = np.minimum(far_bucket, halves - 1)
    return (bucket_base + np.where(distance < exact_count, distance, far_bucket)).astype(np.int32)


def strip_buckets():
    rho = np.arange(2 * BLK, 5 * BLK)[:, None]
    return bucket_of(rho - 3 * BLK - np.arange(BLK)[None, :], True)


def start_blocks(rows_ref, gathered, first, rows, cols, dest, sem):
    across = cols // BLK

    def body(b, carry):
        i = b // across
        j = b - i * across
        row = rows_ref[first + b]
        place = dest.at[pl.ds(pl.multiple_of(i * BLK, BLK), BLK), pl.ds(pl.multiple_of(j * BLK, BLK), BLK)]

        @pl.when(row >= 0)
        def _():
            pltpu.make_async_copy(gathered[0].at[pl.ds(pl.multiple_of(row, 16), BLK)], place, sem).start()

        @pl.when(row < 0)
        def _():
            pltpu.make_async_copy(gathered[1].at[pl.ds(pl.multiple_of(-1 - row, 16), BLK)], place, sem).start()

        return carry

    lax.fori_loop(0, rows // BLK * across, body, 0)


def wait_whole(dest, sem):
    pltpu.make_async_copy(dest, dest, sem).wait()


def head_lanes(rows, head):
    lane = lax.broadcasted_iota(jnp.int32, (rows, BLK), 1)
    return (lane < HD) if head == 0 else (lane >= HD)


ORDERS = {"A": (3, 2, 0, 1), "B": (3, 2, 1, 0), "C": (0, 1, 3, 2), "D": (1, 0, 3, 2)}


def chunk_plan(rows, nbits, names, shares):
    if nbits != 4:
        return [(0, rows, tuple(range(nbits - 1, -1, -1)))]
    total = sum(shares)
    plan, first = [], 0
    for k, name in enumerate(names):
        size = rows - first if k == len(names) - 1 else rows * shares[k] // total // 16 * 16
        plan.append((first, size, ORDERS[name]))
        first += size
    return plan


class Tree:
    def __init__(self, order):
        self.order, self.nbits = order, len(order)

    def last(self, m):
        return max([t for t, b in enumerate(self.order) if m >> b & 1], default=-1)

    def rank(self, m):
        t = self.last(m)
        peers = [x for x in range(1 << self.nbits) if self.last(x) == t]
        return (peers.index(m) + 0.5) / len(peers)

    def children(self, m):
        return [m | 1 << self.order[t] for t in range(self.last(m) + 1, self.nbits)]

    def bit(self, m):
        return 1 << self.order[self.last(m)]


def enter_tree(nbits):
    me, core = lax.axis_index("dp"), lax.axis_index("opt")
    barrier = pltpu.get_barrier_semaphore()
    for b in range(nbits):
        pl.semaphore_signal(barrier, inc=1, device_id=(me ^ (1 << b), core), device_id_type=MESH)
    pl.semaphore_signal(barrier, inc=1, device_id=(me, 1 - core), device_id_type=MESH)
    pl.semaphore_wait(barrier, nbits + 1)


def spread_steps(plan, nbits, rows, source, out_ref, sems):
    ssem, rsem, ssib, rsib, lsem = sems
    me, core = lax.axis_index("dp"), lax.axis_index("opt")
    masks = range(1 << nbits)
    trees = [Tree(order) for _, _, order in plan]

    def region(c, m, o):
        first, size, _ = plan[c]
        return out_ref.at[pl.ds(pl.multiple_of(((me ^ m) * 2 + o) * rows + first, 16), size)]

    def down(c, m):
        parent = m ^ trees[c].bit(m)
        return lambda sending: pltpu.make_async_remote_copy(
            (source(c) if parent == 0 else region(c, parent, core)) if sending else region(c, m, core),
            region(c, parent, core) if sending else region(c, m, core),
            ssem.at[c, m], rsem.at[c, m], device_id=(me ^ trees[c].bit(m), core), device_id_type=MESH,
        )

    def across(c, m):
        return pltpu.make_async_remote_copy(
            region(c, m, core) if m else source(c), region(c, m, core),
            ssib.at[c, m], rsib.at[c, m], device_id=(me, 1 - core), device_id_type=MESH,
        )

    def arrived(c, m):
        ref = region(c, m, 1 - core)
        return pltpu.make_async_remote_copy(
            ref, ref, ssib.at[c, m], rsib.at[c, m], device_id=(me, 1 - core), device_id_type=MESH
        )

    def keep(c):
        return pltpu.make_async_copy(source(c), region(c, 0, core), lsem.at[c, 0])

    def step(c, m):
        if m:
            down(c, m)(False).wait_recv()
        for child in trees[c].children(m):
            down(c, child)(True).start()
        across(c, m).start()
        if m == 0:
            keep(c).start()

    def end():
        for c in range(len(plan)):
            for m in masks:
                arrived(c, m).wait_recv()
                across(c, m).wait_send()
                if m:
                    down(c, m)(True).wait_send()
            keep(c).wait()

    keys = sorted((trees[c].last(m) * 100 + trees[c].rank(m) * (trees[c].last(m) + 2), c, m) for c in range(len(plan)) for m in masks)
    return [functools.partial(step, c, m) for _, c, m in keys], end


def sum_steps(plan, nbits, rows, terms_ref, put, own, sib, land, sems):
    ssem, rsem, ssib, rsib, lsem = sems
    me, core = lax.axis_index("dp"), lax.axis_index("opt")
    trees = [Tree(order) for _, _, order in plan]

    def span(c):
        return pl.ds(plan[c][0], plan[c][1])

    def source(c, m, o):
        first, size, _ = plan[c]
        return terms_ref.at[pl.ds(pl.multiple_of(((me ^ m) * 2 + o) * rows + first, 16), size)]

    def load(c, m):
        return pltpu.make_async_copy(source(c, m, core), own.at[m, span(c)], lsem.at[c, m])

    def across(c, m):
        return pltpu.make_async_remote_copy(
            source(c, m, 1 - core), sib.at[m, span(c)], ssib.at[c, m], rsib.at[c, m],
            device_id=(me, 1 - core), device_id_type=MESH,
        )

    def up(c, m):
        return pltpu.make_async_remote_copy(
            own.at[m, span(c)], land.at[m - 1, span(c)], ssem.at[c, m], rsem.at[c, m],
            device_id=(me ^ trees[c].bit(m), core), device_id_type=MESH,
        )

    def step(c, m):
        first, size, _ = plan[c]
        load(c, m).wait()
        across(c, m).wait_recv()
        arrived = [child - 1 for child in trees[c].children(m)]
        for child in reversed(trees[c].children(m)):
            up(c, child).wait_recv()

        def add(i, count):
            at = pl.ds(pl.multiple_of(first + i * BLK, 16), count)
            total = own[m, at, :].astype(f32) + sib[m, at, :].astype(f32)
            for child in arrived:
                total = total + land[child, at, :].astype(f32)
            if m:
                own[m, at, :] = to_low(total)
            else:
                put(at, total)

        def body(i, carry):
            add(i, BLK)
            return carry

        lax.fori_loop(0, size // BLK, body, 0)
        if size % BLK:
            add(size // BLK, size % BLK)
        if m:
            up(c, m).start()

    stages = lambda c, m: nbits - 1 - trees[c].last(m)
    keys = sorted(
        (stages(c, m) * 8 + trees[c].rank(m) * 8 + 2 * c, c, m) for c in range(len(plan)) for m in range(1 << nbits)
    )

    def begin():
        for _, c, m in keys:
            load(c, m).start()
            across(c, m).start()

    def end():
        for _, c, m in keys:
            across(c, m).wait_send()
            if m:
                up(c, m).wait_send()

    return begin, [functools.partial(step, c, m) for _, c, m in keys], end


def tree_sems(plan, nbits):
    return [pltpu.SemaphoreType.DMA((len(plan), 1 << nbits))] * 5


def sum_scratch(rows, nbits):
    many = 1 << nbits
    return [pltpu.VMEM((count, rows, BLK), bf16) for count in (many, many, many - 1)]


def together(steps, more):
    placed = [(k / len(steps), 0, k, step) for k, step in enumerate(steps)]
    placed += [(k / len(more), 1, k, step) for k, step in enumerate(more)]
    return [step for _, _, _, step in sorted(placed, key=lambda entry: entry[:3])]


def gather_kernel(plan, nbits, rows, shard, out_ref, *sems):
    enter_tree(nbits)
    steps, end = spread_steps(plan, nbits, rows, lambda c: shard.at[pl.ds(plan[c][0], plan[c][1])], out_ref, sems)
    for step in steps:
        step()
    end()


def gather_rows(shard, rows, dp_count, cid):
    nbits = dp_count.bit_length() - 1
    plan = chunk_plan(rows, nbits, "ABABABCD", (1,) * 8)
    any_space = pl.BlockSpec(memory_space=pl.ANY)
    return pl.pallas_call(
        functools.partial(gather_kernel, plan, nbits, rows),
        out_shape=jax.ShapeDtypeStruct((dp_count * 2 * rows, BLK), shard.dtype),
        in_specs=[any_space],
        out_specs=any_space,
        scratch_shapes=tree_sems(plan, nbits),
        compiler_params=pltpu.CompilerParams(collective_id=cid, has_side_effects=True),
        name="gather_rows",
    )(shard)


def total_kernel(plan, nbits, rows, terms, out_ref, own, sib, land, *sems):
    enter_tree(nbits)

    def put(at, total):
        own[0, at, :] = to_low(total)

    begin, steps, end = sum_steps(plan, nbits, rows, terms, put, own, sib, land, sems[:5])
    begin()
    for step in steps:
        step()
    more, last = spread_steps(plan, nbits, rows, lambda c: own.at[0, pl.ds(plan[c][0], plan[c][1])], out_ref, sems[5:])
    for step in more:
        step()
    end()
    last()


def total_rows_all(terms, dp_count, cid):
    rows = terms.shape[0] // (dp_count * 2)
    nbits = dp_count.bit_length() - 1
    plan = chunk_plan(rows, nbits, "ABCD", (3, 3, 1, 1))
    return pl.pallas_call(
        functools.partial(total_kernel, plan, nbits, rows),
        out_shape=jax.ShapeDtypeStruct(terms.shape, bf16),
        in_specs=[pl.BlockSpec(memory_space=pl.ANY)],
        out_specs=pl.BlockSpec(memory_space=pl.ANY),
        scratch_shapes=sum_scratch(rows, nbits) + tree_sems(plan, nbits) * 2,
        compiler_params=pltpu.CompilerParams(collective_id=cid, has_side_effects=True, vmem_limit_bytes=VMEM_CAP),
        name="total_rows",
    )(terms)


def strip_kernel(table, buckets, out):
    head = pl.program_id(0)
    which = buckets[...]
    total = jnp.zeros((3 * BLK, BLK), f32)
    for b in range(NB):
        total = jnp.where(which == b, table[b * H + head], total)
    out[0, 0 : 2 * BLK, :] = jnp.full((2 * BLK, BLK), table[(NB // 2 - 1) * H + head], f32)
    out[0, 2 * BLK : 5 * BLK, :] = total
    out[0, 5 * BLK :, :] = jnp.full((2 * BLK, BLK), table[(NB - 1) * H + head], f32)


def bias_strips(table):
    return pl.pallas_call(
        strip_kernel,
        grid=(H,),
        in_specs=[
            pl.BlockSpec(memory_space=pltpu.SMEM),
            pl.BlockSpec((3 * BLK, BLK), lambda h: (0, 0)),
        ],
        out_specs=pl.BlockSpec((1, STRIP, BLK), lambda h: (h, 0, 0)),
        out_shape=jax.ShapeDtypeStruct((H, STRIP, BLK), f32),
        name="bias_strips",
    )(table, jnp.asarray(strip_buckets()))


def masked_scores(keys, queries, strip, offset, length):
    rows = keys.shape[0]
    scores = dot_nt(keys, queries)
    bias = jnp.concatenate(
        [strip[(3 - n) * BLK : (3 - n) * BLK + rows, :] for n in range(offset, offset + queries.shape[0] // BLK)], axis=1
    )
    key_at = lax.broadcasted_iota(jnp.int32, scores.shape, 0)
    scores = scores + bias
    return jnp.concatenate([scores[:SURE], jnp.where(key_at[SURE:] < length, scores[SURE:], neg_fill)], axis=0)


def attend_kernel(
    rows_ref, lengths, x_ref, near, far, gains, strips, qkv, lse, mixed, hidden, whole, wqkv, sems, out_sem
):
    step = pl.program_id(0)
    keep = pltpu.make_async_copy(wqkv, whole, out_sem.at[0])

    @pl.when(step == 0)
    def _():
        for m in range(4):
            start_blocks(rows_ref, (near, far), 36 * m, D, D, wqkv.at[m], sems.at[m])

    values = x_ref[...].astype(f32)
    normed = to_low(rms_scale(values, gains[0:1, :]))
    for m in range(3):

        @pl.when(step == 0)
        def _(m=m):
            wait_whole(wqkv.at[m], sems.at[m])

        qkv[:, m * D : (m + 1) * D] = to_low(dot(normed, wqkv[m]))

    @pl.when(step == 0)
    def _():
        wait_whole(wqkv.at[3], sems.at[3])
        keep.start()

    length = lengths[step]

    def one_pair(pair, carry):
        at = pl.multiple_of(pair * BLK, BLK)
        queries = qkv[:, pl.ds(at, BLK)]
        keys = qkv[:, pl.ds(pl.multiple_of(at + D, BLK), BLK)]
        turned = qkv[:, pl.ds(pl.multiple_of(at + 2 * D, BLK), BLK)].T
        outs = []
        for head in range(2):
            only = jnp.where(head_lanes(PASS_SLOT, head), queries, jnp.zeros_like(queries))
            scores = masked_scores(keys, only, strips.at[2 * pair + head], 0, length)
            peak = jnp.max(scores, axis=0, keepdims=True)
            expos = jnp.exp(scores - peak)
            total = jnp.sum(expos, axis=0, keepdims=True)
            lse[0, pl.ds(2 * pair + head, 1), :] = peak + jnp.log(total)
            outs.append(dot(turned, to_low(expos)) * (1.0 / total))
        lane = lax.broadcasted_iota(jnp.int32, (BLK, PASS_SLOT), 0)
        mixed[:, pl.ds(at, BLK)] = to_low(jnp.where(lane < HD, outs[0], outs[1]).T)
        return carry

    lax.fori_loop(0, PAIRS, one_pair, 0)
    hidden[...] = x_ref[...].astype(f32) + dot(mixed[...], wqkv[3])
    pl.when(step == pl.num_programs(0) - 1)(lambda: keep.wait())


def encoder_attend(rows, lengths, enc_in, gathered, gains, strips):
    count = lengths.shape[0]
    total = count * PASS_SLOT
    by_row = lambda p, *_: (p, 0)
    any_space = pl.BlockSpec(memory_space=pl.ANY)
    return pl.pallas_call(
        attend_kernel,
        grid_spec=pltpu.PrefetchScalarGridSpec(
            num_scalar_prefetch=2,
            grid=(count,),
            in_specs=[
                pl.BlockSpec((PASS_SLOT, D), by_row),
                any_space,
                any_space,
                pl.BlockSpec((8, D), lambda p, *_: (0, 0)),
                pl.BlockSpec((H, STRIP, BLK), lambda p, *_: (0, 0, 0)),
            ],
            out_specs=[
                pl.BlockSpec((PASS_SLOT, 3 * D), by_row),
                pl.BlockSpec((1, 16, PASS_SLOT), lambda p, *_: (p, 0, 0)),
                pl.BlockSpec((PASS_SLOT, D), by_row),
                pl.BlockSpec((PASS_SLOT, D), by_row),
                any_space,
            ],
            scratch_shapes=[
                pltpu.VMEM((4, D, D), bf16),
                pltpu.SemaphoreType.DMA((4,)),
                pltpu.SemaphoreType.DMA((1,)),
            ],
        ),
        out_shape=[
            jax.ShapeDtypeStruct((total, 3 * D), bf16),
            jax.ShapeDtypeStruct((count, 16, PASS_SLOT), f32),
            jax.ShapeDtypeStruct((total, D), bf16),
            jax.ShapeDtypeStruct((total, D), f32),
            jax.ShapeDtypeStruct((4, D, D), bf16),
        ],
        compiler_params=pltpu.CompilerParams(vmem_limit_bytes=VMEM_CAP),
        name="encoder_attend",
    )(rows, lengths, enc_in, *gathered, gains, strips)


FEED_CHUNK = 1536
FCHUNK = 768


def feed_kernel(rows_ref, hidden, near, far, gains, inner, output, encoded, up, down, wup, wdown, sems, out_sems):
    step = pl.program_id(0)
    keeps = [pltpu.make_async_copy(wup, up, out_sems.at[0]), pltpu.make_async_copy(wdown, down, out_sems.at[1])]

    @pl.when(step == 0)
    def _():
        start_blocks(rows_ref, (near, far), ENC_UP, D, FF, wup, sems.at[0])
        start_blocks(rows_ref, (near, far), ENC_DOWN, FF, D, wdown, sems.at[1])

    normed = to_low(rms_scale(hidden[...], gains[1:2, :]))
    total = hidden[...]

    @pl.when(step == 0)
    def _():
        wait_whole(wup, sems.at[0])
        wait_whole(wdown, sems.at[1])
        for keep in keeps:
            keep.start()

    for c in range(FF // FEED_CHUNK):
        cols = slice(c * FEED_CHUNK, (c + 1) * FEED_CHUNK)
        act = dot(normed, wup[:, cols])
        inner[:, cols] = to_low(act)
        total = total + dot(to_low(gate(act)), wdown[cols, :])
    output[...] = total
    encoded[...] = to_low(rms_scale(total, gains[2:3, :]))

    @pl.when(step == pl.num_programs(0) - 1)
    def _():
        for keep in keeps:
            keep.wait()


def encoder_feed(rows, hidden, gathered, gains):
    total = hidden.shape[0]
    tile = 512
    by_row = lambda p, *_: (p, 0)
    any_space = pl.BlockSpec(memory_space=pl.ANY)
    return pl.pallas_call(
        feed_kernel,
        grid_spec=pltpu.PrefetchScalarGridSpec(
            num_scalar_prefetch=1,
            grid=(total // tile,),
            in_specs=[
                pl.BlockSpec((tile, D), by_row),
                any_space,
                any_space,
                pl.BlockSpec((8, D), lambda p, *_: (0, 0)),
            ],
            out_specs=[
                pl.BlockSpec((tile, FF), by_row),
                pl.BlockSpec((tile, D), by_row),
                pl.BlockSpec((tile, D), by_row),
                any_space,
                any_space,
            ],
            scratch_shapes=[
                pltpu.VMEM((D, FF), bf16),
                pltpu.VMEM((FF, D), bf16),
                pltpu.SemaphoreType.DMA((2,)),
                pltpu.SemaphoreType.DMA((2,)),
            ],
        ),
        out_shape=[
            jax.ShapeDtypeStruct((total, FF), bf16),
            jax.ShapeDtypeStruct((total, D), f32),
            jax.ShapeDtypeStruct((total, D), bf16),
            jax.ShapeDtypeStruct((D, FF), bf16),
            jax.ShapeDtypeStruct((FF, D), bf16),
        ],
        compiler_params=pltpu.CompilerParams(vmem_limit_bytes=VMEM_CAP),
        name="encoder_feed",
    )(rows, hidden, *gathered, gains)


def feed_back_kernel(
    output, hidden, inner, upstream, down, up, out, gains,
    act_low, inner_grad, branch, normed, hidden_grad, attn_grad, mixed_grad, gain_sums,
    wup, wdown, wout, sems,
):
    step = pl.program_id(0)

    @pl.when(step == 0)
    def _():
        pltpu.make_async_copy(down, wdown, sems.at[0]).start()
        pltpu.make_async_copy(up, wup, sems.at[1]).start()
        pltpu.make_async_copy(out.at[3], wout, sems.at[2]).start()
        gain_sums[...] = jnp.zeros_like(gain_sums)

    output_grad, final_gain = norm_back(output[...], gains[2:3, :], upstream[...])
    low = to_low(output_grad)
    branch[...] = low

    @pl.when(step == 0)
    def _():
        wait_whole(wdown, sems.at[0])
        wait_whole(wup, sems.at[1])

    total = jnp.zeros(hidden.shape, f32)
    for c in range(FF // FCHUNK):
        cols = slice(c * FCHUNK, (c + 1) * FCHUNK)
        value, slope = gate_both(inner[:, cols].astype(f32))
        act_low[:, cols] = to_low(value)
        grad = to_low(slope * dot_nt(low, wdown[cols, :]))
        inner_grad[:, cols] = grad
        total = total + dot_nt(grad, wup[:, cols])
    values = hidden[...]
    normed[...] = to_low(rms_scale(values, gains[1:2, :]))
    part, second_gain = norm_back(values, gains[1:2, :], total)
    grad = output_grad + part
    hidden_grad[...] = grad
    low = to_low(grad)
    attn_grad[...] = low

    @pl.when(step == 0)
    def _():
        wait_whole(wout, sems.at[2])

    mixed_grad[...] = to_low(dot_nt(low, wout[...]))
    gain_sums[0:1, :] += second_gain
    gain_sums[1:2, :] += final_gain


def feed_back(output, hidden, inner, upstream, down, up, out, gains):
    total = hidden.shape[0]
    tile = 256
    by_row = lambda p, *_: (p, 0)
    fixed = lambda p, *_: (0, 0)
    row = pl.BlockSpec((tile, D), by_row)
    wide = pl.BlockSpec((tile, FF), by_row)
    return pl.pallas_call(
        feed_back_kernel,
        grid_spec=pltpu.PrefetchScalarGridSpec(
            num_scalar_prefetch=0,
            grid=(total // tile,),
            in_specs=[row, row, wide, row, *[pl.BlockSpec(memory_space=pl.ANY)] * 3, pl.BlockSpec((8, D), fixed)],
            out_specs=[wide, wide, row, row, row, row, row, pl.BlockSpec((8, D), fixed)],
            scratch_shapes=[
                pltpu.VMEM((D, FF), bf16),
                pltpu.VMEM((FF, D), bf16),
                pltpu.VMEM((D, D), bf16),
                pltpu.SemaphoreType.DMA((3,)),
            ],
        ),
        out_shape=[
            jax.ShapeDtypeStruct((total, FF), bf16),
            jax.ShapeDtypeStruct((total, FF), bf16),
            jax.ShapeDtypeStruct((total, D), bf16),
            jax.ShapeDtypeStruct((total, D), bf16),
            jax.ShapeDtypeStruct((total, D), f32),
            jax.ShapeDtypeStruct((total, D), bf16),
            jax.ShapeDtypeStruct((total, D), bf16),
            jax.ShapeDtypeStruct((8, D), f32),
        ],
        compiler_params=pltpu.CompilerParams(vmem_limit_bytes=VMEM_CAP),
        name="feed_back",
    )(output, hidden, inner, upstream, down, up, out, gains)


def attend_back_kernel(
    plan, shard_plan, nbits, rows, lengths, q_ref, k_ref, v_ref, go_ref, lse, strips, buckets, *refs
):
    if plan is None:
        gq_ref, gk_ref, gv_ref, table, bias_sums = refs
    else:
        terms, shard, gq_ref, gk_ref, gv_ref, table, reduced, spread, bias_sums, own, sib, land, *sems = refs
    pair = pl.program_id(0)
    step = pl.program_id(1)
    at = pair * pl.num_programs(1) + step
    total_steps = PAIRS * PASS_EX

    if plan is not None:

        def put(where, total):
            reduced[where, :] = to_low(total)

        begin, steps, end = sum_steps(plan, nbits, rows, terms, put, own, sib, land, sems[:5])
        more, more_end = spread_steps(
            shard_plan, nbits, shard.shape[0], lambda c: shard.at[pl.ds(shard_plan[c][0], shard_plan[c][1])], spread, sems[5:]
        )
        steps = together(steps, more)

        @pl.when(at == 0)
        def _():
            enter_tree(nbits)
            begin()

        cuts = [round(len(steps) * (k / (total_steps - 1)) ** 0.8) for k in range(total_steps)]
        for k in range(1, total_steps):
            some = steps[cuts[k - 1] : cuts[k]]

            @pl.when(at == k)
            def _(some=some):
                for one in some:
                    one()

    @pl.when(step == 0)
    def _():
        bias_sums[...] = jnp.zeros_like(bias_sums)

    length = lengths[step]
    keys = k_ref[...]
    values = v_ref[...]
    turned = keys.T
    lane = lax.broadcasted_iota(jnp.int32, turned.shape, 0)
    halves = [
        jnp.where(lane < HD, turned, jnp.zeros_like(turned)),
        jnp.where(lane >= HD, turned, jnp.zeros_like(turned)),
    ]
    key_grad = jnp.zeros((PASS_SLOT, BLK), f32)
    value_grad = jnp.zeros((PASS_SLOT, BLK), f32)
    query_grad = jnp.zeros((BLK, PASS_SLOT), f32)
    for head in range(2):
        mask = head_lanes(PASS_SLOT, head)
        queries = jnp.where(mask, q_ref[...], jnp.zeros((PASS_SLOT, BLK), bf16))
        grads = jnp.where(mask, go_ref[...], jnp.zeros((PASS_SLOT, BLK), bf16))
        scores = masked_scores(keys, queries, strips.at[head], 0, length)
        probs = jnp.exp(scores - lse[0, pl.ds(2 * pair + head, 1), :])
        prob_grad = dot_nt(values, grads)
        inner = jnp.sum(probs * prob_grad, axis=0, keepdims=True)
        score_grad = to_low(probs * (prob_grad - inner))
        wide = score_grad.astype(f32)
        for m in range(PASS_SLOT // BLK):
            first = (3 - m) * BLK
            bias_sums[head, first : first + PASS_SLOT, :] += wide[:, m * BLK : (m + 1) * BLK]
        value_grad = value_grad + dot(to_low(probs), grads)
        key_grad = key_grad + dot(score_grad, queries)
        query_grad = query_grad + dot(halves[head], score_grad)
    gq_ref[...] = to_low(query_grad.T)
    gk_ref[...] = to_low(key_grad)
    gv_ref[...] = to_low(value_grad)

    @pl.when(step == pl.num_programs(1) - 1)
    def _():
        which = buckets[...]
        lane = lax.broadcasted_iota(jnp.int32, (1, BLK), 1)
        for head in range(2):
            near = bias_sums[head, 2 * BLK : 5 * BLK, :]
            sums = jnp.zeros((1, BLK), f32)
            for b in range(NB):
                part = jnp.sum(jnp.where(which == b, near, 0.0), axis=0, keepdims=True)
                if b % (NB // 2) == NB // 2 - 1:
                    ends = slice(0, 2 * BLK) if b < NB // 2 else slice(5 * BLK, STRIP)
                    part = part + jnp.sum(bias_sums[head, ends, :], axis=0, keepdims=True)
                sums = jnp.where(lane == b, jnp.sum(part, axis=1, keepdims=True), sums)
            table[0, head : head + 1, :] = sums

    if plan is not None:

        @pl.when(at == total_steps - 1)
        def _():
            end()
            more_end()


def attend_back(lengths, qkv, mixed_grad, lse, strips, terms, shard, dp_count, cid):
    count = lengths.shape[0]
    total = count * PASS_SLOT
    block = (PASS_SLOT, BLK)
    place = pl.BlockSpec(block, lambda a, p, *_: (p, a))
    strip = pl.BlockSpec((2, STRIP, BLK), lambda a, p, *_: (a, 0, 0))
    in_specs = [
        place,
        pl.BlockSpec(block, lambda a, p, *_: (p, a + PAIRS)),
        pl.BlockSpec(block, lambda a, p, *_: (p, a + 2 * PAIRS)),
        place,
        pl.BlockSpec((1, 16, PASS_SLOT), lambda a, p, *_: (p, 0, 0)),
        strip,
        pl.BlockSpec((3 * BLK, BLK), lambda *_: (0, 0)),
    ]
    out_specs = [place, place, place, pl.BlockSpec((1, 8, BLK), lambda a, p, *_: (a, 0, 0))]
    out_shape = [jax.ShapeDtypeStruct((total, D), bf16)] * 3 + [jax.ShapeDtypeStruct((PAIRS, 8, BLK), f32)]
    operands = [qkv, qkv, qkv, mixed_grad, lse, strips, jnp.asarray(strip_buckets())]
    scratch = [pltpu.VMEM((2, STRIP, BLK), f32)]
    plan, shard_plan, nbits, rows = None, None, 0, 0
    params = dict(vmem_limit_bytes=VMEM_CAP)
    if dp_count == 16:
        rows = terms.shape[0] // (2 * dp_count)
        nbits = dp_count.bit_length() - 1
        plan = chunk_plan(rows, nbits, "ABCDABAB", (2, 2, 2, 2, 3, 3, 1, 1))
        shard_plan = chunk_plan(shard.shape[0], nbits, "ABCD", (3, 3, 1, 1))
        any_space = pl.BlockSpec(memory_space=pl.ANY)
        in_specs += [any_space, any_space]
        out_specs += [pl.BlockSpec((rows, BLK), lambda a, p, *_: (0, 0)), any_space]
        out_shape += [
            jax.ShapeDtypeStruct((rows, BLK), bf16),
            jax.ShapeDtypeStruct((2 * dp_count * shard.shape[0], BLK), bf16),
        ]
        operands += [terms, shard]
        scratch = scratch + sum_scratch(rows, nbits) + tree_sems(plan, nbits) + tree_sems(shard_plan, nbits)
        params.update(collective_id=cid, has_side_effects=True)
    results = pl.pallas_call(
        functools.partial(attend_back_kernel, plan, shard_plan, nbits, rows),
        grid_spec=pltpu.PrefetchScalarGridSpec(
            num_scalar_prefetch=1,
            grid=(PAIRS, count),
            in_specs=in_specs,
            out_specs=out_specs,
            scratch_shapes=scratch,
        ),
        out_shape=out_shape,
        compiler_params=pltpu.CompilerParams(**params),
        name="attend_back",
    )(lengths, *operands)
    if plan is None:
        return (
            *results,
            lax.psum_scatter(terms, ("dp", "opt"), scatter_dimension=0, tiled=True),
            lax.all_gather(shard, ("dp", "opt"), axis=0, tiled=True),
        )
    return results


def input_back_kernel(
    x_ref, gq, gk, gv, hidden_grad, whole, gains, result, normed, gain_sums, wqkv, sems
):
    step = pl.program_id(0)

    @pl.when(step == 0)
    def _():
        for m in range(3):
            pltpu.make_async_copy(whole.at[m], wqkv.at[m], sems.at[m]).start()
        gain_sums[...] = jnp.zeros_like(gain_sums)

    values = x_ref[...].astype(f32)
    normed[...] = to_low(rms_scale(values, gains[0:1, :]))
    total = jnp.zeros(values.shape, f32)
    for m, grads in enumerate((gq, gk, gv)):

        @pl.when(step == 0)
        def _(m=m):
            wait_whole(wqkv.at[m], sems.at[m])

        total = total + dot_nt(grads[...], wqkv[m])
    part, first_gain = norm_back(values, gains[0:1, :], total)
    result[...] = hidden_grad[...] + part
    gain_sums[0:1, :] += first_gain


def input_back(enc_in, gq, gk, gv, hidden_grad, whole, gains):
    total = enc_in.shape[0]
    tile = 256
    fixed = lambda p, *_: (0, 0)
    row = pl.BlockSpec((tile, D), lambda p, *_: (p, 0))
    return pl.pallas_call(
        input_back_kernel,
        grid_spec=pltpu.PrefetchScalarGridSpec(
            num_scalar_prefetch=0,
            grid=(total // tile,),
            in_specs=[row, row, row, row, row, pl.BlockSpec(memory_space=pl.ANY), pl.BlockSpec((8, D), fixed)],
            out_specs=[row, row, pl.BlockSpec((8, D), fixed)],
            scratch_shapes=[pltpu.VMEM((3, D, D), bf16), pltpu.SemaphoreType.DMA((3,))],
        ),
        out_shape=[
            jax.ShapeDtypeStruct((total, D), f32),
            jax.ShapeDtypeStruct((total, D), bf16),
            jax.ShapeDtypeStruct((8, D), f32),
        ],
        compiler_params=pltpu.CompilerParams(vmem_limit_bytes=VMEM_CAP),
        name="input_back",
    )(enc_in, gq, gk, gv, hidden_grad, whole, gains)


HROWS = H * AROWS
SIDE = D + 2 * BLK


HELD = 16
REST = ALEN - HELD


def pack_rows(sides):
    main = jnp.concatenate([side[:HELD] for side in sides], axis=1)
    width = max(side.shape[1] for side in sides)
    rest = jnp.zeros((HELD, width), f32)
    for k, side in enumerate(sides):
        rows = side[HELD:ALEN].astype(f32)
        if side.shape[1] < width:
            rows = jnp.concatenate([rows, jnp.zeros((REST, width - side.shape[1]), f32)], axis=1)
        above, below = REST * k, HELD - REST * (k + 1)
        rows = [jnp.zeros((above, width), f32)] * (above > 0) + [rows] + [jnp.zeros((below, width), f32)] * (below > 0)
        rest = rest + jnp.concatenate(rows, axis=0)
    return jnp.concatenate([main, to_low(rest)], axis=1)


def spread_heads(rows):
    lane = lax.broadcasted_iota(jnp.int32, rows.shape, 1)
    zero = jnp.zeros_like(rows)
    return jnp.concatenate(
        [jnp.where((lane >= h * HD) & (lane < (h + 1) * HD), rows, zero) for h in range(H)], axis=0
    )


def gather_heads(spread):
    lane = lax.broadcasted_iota(jnp.int32, (AROWS, D), 1)
    total = jnp.zeros((AROWS, D), f32)
    for h in range(H):
        total = jnp.where(
            (lane >= h * HD) & (lane < (h + 1) * HD), spread[h * AROWS : (h + 1) * AROWS], total
        )
    return total


def heads_to_lanes(column):
    lane = lax.broadcasted_iota(jnp.int32, (AROWS, BLK), 1)
    total = jnp.zeros((AROWS, BLK), f32)
    for h in range(H):
        total = jnp.where(lane == h, column[h * AROWS : (h + 1) * AROWS], total)
    return total


def lanes_to_heads(lanes):
    return jnp.concatenate([lanes[:, h : h + 1] for h in range(H)], axis=0)


def lanes_over_heads(lanes):
    lane = lax.broadcasted_iota(jnp.int32, (AROWS, D), 1)
    total = jnp.zeros((AROWS, D), f32)
    for h in range(H):
        total = jnp.where((lane >= h * HD) & (lane < (h + 1) * HD), lanes[:, h : h + 1], total)
    return total


def causal_scores(queries, keys, bias):
    scores = dot_nt(spread_heads(queries), keys) + bias
    row = lax.broadcasted_iota(jnp.int32, scores.shape, 0)
    key_at = lax.broadcasted_iota(jnp.int32, scores.shape, 1)
    return jnp.where(key_at <= row % AROWS, scores, neg_fill)


def self_kernel(rows_ref, dec_ref, near, far, gains, bias, qkv, first, cross, early, wqkv, wout, wcq, sems):
    for m in range(3):
        start_blocks(rows_ref, (near, far), DEC_QKV + 36 * m, D, D, wqkv.at[m], sems.at[m])
    start_blocks(rows_ref, (near, far), DEC_OUT, D, D, wout, sems.at[3])
    start_blocks(rows_ref, (near, far), CROSS_Q, D, D, wcq, sems.at[4])
    values = dec_ref[...].astype(f32)
    low = normed = to_low(rms_scale(values, gains[3:4, :]))
    for m in range(3):
        wait_whole(wqkv.at[m], sems.at[m])
        qkv[:, m * D : (m + 1) * D] = to_low(dot(low, wqkv[m]))
    scores = causal_scores(qkv[:, 0:D], qkv[:, D : 2 * D], bias[...])
    peak = jnp.max(scores, axis=1, keepdims=True)
    expos = jnp.exp(scores - peak)
    probs = to_low(expos / jnp.sum(expos, axis=1, keepdims=True))
    heads = to_low(gather_heads(dot(probs, qkv[:, 2 * D : 3 * D])))
    wait_whole(wout, sems.at[3])
    after = values + dot(heads, wout[...])
    first[...] = after
    low = to_low(rms_scale(after, gains[4:5, :]))
    wait_whole(wcq, sems.at[4])
    cross[...] = to_low(dot(low, wcq[...]))
    early[...] = pack_rows((normed, heads, low))


def whole_spec(shape):
    return pl.BlockSpec(shape, lambda *_: (0,) * len(shape))


def decoder_call(body, name, rows, ins, outs, scratch):
    specs = [pl.BlockSpec(memory_space=pl.ANY) if x.shape[0] > 8192 else whole_spec(x.shape) for x in ins]
    return pl.pallas_call(
        body,
        grid_spec=pltpu.PrefetchScalarGridSpec(
            num_scalar_prefetch=1,
            grid=(1,),
            in_specs=specs,
            out_specs=[whole_spec(shape) for shape, kind in outs],
            scratch_shapes=scratch,
        ),
        out_shape=[jax.ShapeDtypeStruct(shape, kind) for shape, kind in outs],
        compiler_params=pltpu.CompilerParams(vmem_limit_bytes=VMEM_CAP),
        name=name,
    )(rows, *ins)


def decoder_self(rows, dec_rows, gathered, gains, bias):
    low, full = ((AROWS, D), bf16), ((AROWS, D), f32)
    square = pltpu.VMEM((D, D), bf16)
    return decoder_call(
        self_kernel, "decoder_self", rows, (dec_rows, *gathered, gains, bias),
        [((AROWS, 3 * D), bf16), full, low, ((HELD, 4 * D), bf16)],
        [pltpu.VMEM((3, D, D), bf16), square, square, pltpu.SemaphoreType.DMA((5,))],
    )


def memory_kernel(rows_ref, encoded, near, far, memory, wkv, sems):
    step = pl.program_id(0)

    @pl.when(step == 0)
    def _():
        for m in range(2):
            start_blocks(rows_ref, (near, far), CROSS_KV + 36 * m, D, D, wkv.at[m], sems.at[m])

    for m in range(2):

        @pl.when(step == 0)
        def _(m=m):
            wait_whole(wkv.at[m], sems.at[m])

        memory[:, m * D : (m + 1) * D] = to_low(dot(encoded[...], wkv[m]))


def cross_memory(rows, encoded, gathered):
    total = encoded.shape[0]
    return pl.pallas_call(
        memory_kernel,
        grid_spec=pltpu.PrefetchScalarGridSpec(
            num_scalar_prefetch=1,
            grid=(total // PASS_SLOT,),
            in_specs=[pl.BlockSpec((PASS_SLOT, D), lambda p, *_: (p, 0)), *[pl.BlockSpec(memory_space=pl.ANY)] * 2],
            out_specs=pl.BlockSpec((PASS_SLOT, 2 * D), lambda p, *_: (p, 0)),
            scratch_shapes=[pltpu.VMEM((2, D, D), bf16), pltpu.SemaphoreType.DMA((2,))],
        ),
        out_shape=jax.ShapeDtypeStruct((total, 2 * D), bf16),
        compiler_params=pltpu.CompilerParams(vmem_limit_bytes=VMEM_CAP),
        name="cross_memory",
    )(rows, encoded, *gathered)


def cross_kernel(lengths, offsets, queries, memory, result):
    length = lengths[pl.program_id(0)]
    scores = dot_nt(spread_heads(queries[0]), memory[:, 0:D])
    key_at = lax.broadcasted_iota(jnp.int32, scores.shape, 1)
    scores = jnp.where(key_at < length, scores, neg_fill)
    peak = jnp.max(scores, axis=1, keepdims=True)
    expos = jnp.exp(scores - peak)
    result[0, :, 0:D] = gather_heads(dot(to_low(expos), memory[:, D : 2 * D]))
    result[0, :, D : D + BLK] = heads_to_lanes(peak)
    result[0, :, D + BLK :] = heads_to_lanes(jnp.sum(expos, axis=1, keepdims=True))


def cross_attend(lengths, offsets, queries, memory):
    count = lengths.shape[0]
    at_offset = lambda p, lens, offs: (offs[p], 0, 0)
    return pl.pallas_call(
        cross_kernel,
        grid_spec=pltpu.PrefetchScalarGridSpec(
            num_scalar_prefetch=2,
            grid=(count,),
            in_specs=[
                pl.BlockSpec((1, AROWS, D), at_offset),
                pl.BlockSpec((PASS_SLOT, 2 * D), lambda p, *_: (p, 0)),
            ],
            out_specs=pl.BlockSpec((1, AROWS, SIDE), at_offset),
        ),
        out_shape=jax.ShapeDtypeStruct((count, AROWS, SIDE), f32),
        compiler_params=pltpu.CompilerParams(vmem_limit_bytes=VMEM_CAP),
        name="cross_attend",
    )(lengths, offsets, queries, memory)


def feed_decoder_kernel(
    rows_ref, parts, first, dec_cot, valid, early, near, far, gains,
    result, middle, back, second_grad, gain_sums, wout, wup, wdown, sems,
):
    start_blocks(rows_ref, (near, far), CROSS_OUT, D, D, wout, sems.at[0])
    start_blocks(rows_ref, (near, far), DEC_UP, D, FF, wup, sems.at[1])
    start_blocks(rows_ref, (near, far), DEC_DOWN, FF, D, wdown, sems.at[2])
    peaks = [parts[k, :, D : D + BLK] for k in range(PASS_EX)]
    peak = functools.reduce(jnp.maximum, peaks)
    scales = [jnp.exp(one - peak) for one in peaks]
    total = sum(parts[k, :, D + BLK :] * scales[k] for k in range(PASS_EX))
    lane = lax.broadcasted_iota(jnp.int32, total.shape, 1)
    total = jnp.where(lane < H, total, 1.0)
    heads = sum(parts[k, :, 0:D] * lanes_over_heads(scales[k] / total) for k in range(PASS_EX))
    low = mixed = to_low(heads)
    wait_whole(wout, sems.at[0])
    second = first[...] + dot(low, wout[...])
    low = to_low(rms_scale(second, gains[5:6, :]))
    output_grad = dec_cot[...].astype(f32) * valid[:, 0:1]
    grad_low = to_low(output_grad)
    acts, inner_grads = [], []
    wait_whole(wup, sems.at[1])
    wait_whole(wdown, sems.at[2])
    after = second
    back_sum = jnp.zeros((AROWS, D), f32)
    for c in range(FF // D):
        cols = slice(c * D, (c + 1) * D)
        value, slope = gate_both(dot(low, wup[:, cols]))
        value = to_low(value)
        acts.append(value)
        after = after + dot(value, wdown[cols, :])
        grad = to_low(slope * dot_nt(grad_low, wdown[cols, :]))
        inner_grads.append(grad)
        back_sum = back_sum + dot_nt(grad, wup[:, cols])
    result[...] = to_low(after)
    part, gain_grad = norm_back(second, gains[5:6, :], back_sum)
    grad = output_grad + part
    second_grad[...] = grad
    gain_sums[...] = jnp.broadcast_to(gain_grad, gain_sums.shape)
    normed, low = low, to_low(grad)
    middle[:, : 17 * D] = pack_rows(
        (
            jnp.concatenate([normed] + inner_grads, axis=1),
            jnp.concatenate(acts + [grad_low], axis=1),
            jnp.concatenate([mixed, low], axis=1),
        )
    )
    middle[:, 17 * D :] = early[...]
    head_grad = to_low(dot_nt(low, wout[...])).astype(f32)
    back[:, 0:D] = head_grad
    back[:, D : D + BLK] = peak + jnp.log(total)
    product = head_grad * heads
    at = lax.broadcasted_iota(jnp.int32, (AROWS, D), 1)
    inner = jnp.zeros((AROWS, BLK), f32)
    for h in range(H):
        one = jnp.where((at >= h * HD) & (at < (h + 1) * HD), product, 0.0)
        inner = jnp.where(lane == h, jnp.sum(one, axis=1, keepdims=True), inner)
    back[:, D + BLK :] = inner


def decoder_feed(rows, parts, first, dec_cot, valid, early, gathered, gains):
    low, full = ((AROWS, D), bf16), ((AROWS, D), f32)
    return decoder_call(
        feed_decoder_kernel, "decoder_feed", rows, (parts, first, dec_cot, valid, early, *gathered, gains),
        [low, ((HELD, 21 * D), bf16), ((AROWS, SIDE), f32), full, ((8, D), f32)],
        [pltpu.VMEM((D, D), bf16), pltpu.VMEM((D, FF), bf16), pltpu.VMEM((FF, D), bf16), pltpu.SemaphoreType.DMA((3,))],
    )


def cross_back_kernel(
    rows_ref, lengths, offsets, queries, back, memory, enc_cot, near, far,
    memory_grad, query_grad, upstream, wkv, sems,
):
    step = pl.program_id(0)

    @pl.when(step == 0)
    def _():
        for m in range(2):
            start_blocks(rows_ref, (near, far), CROSS_KV + 36 * m, D, D, wkv.at[m], sems.at[m])

    length = lengths[step]
    spread = spread_heads(queries[0])
    grads = spread_heads(to_low(back[0, :, 0:D]))
    keys = memory[:, 0:D]
    scores = dot_nt(spread, keys)
    key_at = lax.broadcasted_iota(jnp.int32, scores.shape, 1)
    scores = jnp.where(key_at < length, scores, neg_fill)
    probs = jnp.exp(scores - lanes_to_heads(back[0, :, D : D + BLK]))
    prob_grad = dot_nt(grads, memory[:, D : 2 * D])
    score_grad = to_low(probs * (prob_grad - lanes_to_heads(back[0, :, D + BLK :])))
    query_grad[0] = gather_heads(dot(score_grad, keys))
    key_low = to_low(dot_tn(score_grad, spread))
    value_low = to_low(dot_tn(to_low(probs), grads))
    memory_grad[:, 0:D] = key_low
    memory_grad[:, D : 2 * D] = value_low

    @pl.when(step == 0)
    def _():
        for m in range(2):
            wait_whole(wkv.at[m], sems.at[m])

    total = to_low(dot_nt(key_low, wkv[0]) + dot_nt(value_low, wkv[1])).astype(f32)
    row = lax.broadcasted_iota(jnp.int32, total.shape, 0)
    upstream[...] = total + jnp.where(row < length, enc_cot[...].astype(f32), 0.0)


def cross_back(rows, lengths, offsets, queries, back, memory, enc_cot, gathered):
    count = lengths.shape[0]
    total = count * PASS_SLOT
    at_offset = lambda p, rows, lens, offs: (offs[p], 0, 0)
    by_row = lambda p, *_: (p, 0)
    return pl.pallas_call(
        cross_back_kernel,
        grid_spec=pltpu.PrefetchScalarGridSpec(
            num_scalar_prefetch=3,
            grid=(count,),
            in_specs=[
                pl.BlockSpec((1, AROWS, D), at_offset),
                pl.BlockSpec((1, AROWS, SIDE), at_offset),
                pl.BlockSpec((PASS_SLOT, 2 * D), by_row),
                pl.BlockSpec((PASS_SLOT, D), by_row),
                *[pl.BlockSpec(memory_space=pl.ANY)] * 2,
            ],
            out_specs=[
                pl.BlockSpec((PASS_SLOT, 2 * D), by_row),
                pl.BlockSpec((1, AROWS, D), at_offset),
                pl.BlockSpec((PASS_SLOT, D), by_row),
            ],
            scratch_shapes=[pltpu.VMEM((2, D, D), bf16), pltpu.SemaphoreType.DMA((2,))],
        ),
        out_shape=[
            jax.ShapeDtypeStruct((total, 2 * D), bf16),
            jax.ShapeDtypeStruct((count, AROWS, D), f32),
            jax.ShapeDtypeStruct((total, D), f32),
        ],
        compiler_params=pltpu.CompilerParams(vmem_limit_bytes=VMEM_CAP),
        name="cross_back",
    )(rows, lengths, offsets, queries, back, memory, enc_cot, *gathered)


def self_back_kernel(
    rows_ref, part_zero, part_one, part_two, second_grad, first, dec_ref, qkv, near, far, gains, bias,
    result, late, score_grads, gain_sums, wqkv, wout, wcq, sems,
):
    start_blocks(rows_ref, (near, far), CROSS_Q, D, D, wcq, sems.at[4])
    start_blocks(rows_ref, (near, far), DEC_OUT, D, D, wout, sems.at[3])
    for m in range(3):
        start_blocks(rows_ref, (near, far), DEC_QKV + 36 * m, D, D, wqkv.at[m], sems.at[m])
    low = cross_grad = to_low(part_zero[...] + part_one[...] + part_two[...])
    wait_whole(wcq, sems.at[4])
    part, second_gain = norm_back(first[...], gains[4:5, :], dot_nt(low, wcq[...]))
    first_grad = second_grad[...] + part
    low = out_grad = to_low(first_grad)
    wait_whole(wout, sems.at[3])
    heads_grad = spread_heads(to_low(dot_nt(low, wout[...])))
    queries = qkv[:, 0:D]
    keys = qkv[:, D : 2 * D]
    scores = causal_scores(queries, keys, bias[...])
    peak = jnp.max(scores, axis=1, keepdims=True)
    expos = jnp.exp(scores - peak)
    probs = expos / jnp.sum(expos, axis=1, keepdims=True)
    prob_grad = dot_nt(heads_grad, qkv[:, 2 * D : 3 * D])
    inner = jnp.sum(probs * prob_grad, axis=1, keepdims=True)
    score_grad = to_low(probs * (prob_grad - inner))
    score_grads[...] = score_grad.astype(f32)
    grads = (
        gather_heads(dot(score_grad, keys)),
        dot_tn(score_grad, spread_heads(queries)),
        dot_tn(to_low(probs), heads_grad),
    )
    total = jnp.zeros((AROWS, D), f32)
    lows = [to_low(grad) for grad in grads]
    packed = pack_rows((jnp.concatenate(lows, axis=1), out_grad, cross_grad))
    for j in range(LATE_COLS):
        late[j * HELD : (j + 1) * HELD, :] = packed[:, j * BLK : (j + 1) * BLK]
    for m in range(3):
        low = lows[m]
        wait_whole(wqkv.at[m], sems.at[m])
        total = total + dot_nt(low, wqkv[m])
    part, first_gain = norm_back(dec_ref[...].astype(f32), gains[3:4, :], total)
    result[...] = first_grad + part
    gain_sums[0:1, :] = first_gain
    gain_sums[1:2, :] = second_gain


LATE_COLS = 8 * D // BLK


def decoder_self_back(rows, parts, second_grad, first, dec_rows, qkv, gathered, gains, bias):
    full = ((AROWS, D), f32)
    square = pltpu.VMEM((D, D), bf16)
    return decoder_call(
        self_back_kernel, "decoder_self_back", rows,
        (*parts, second_grad, first, dec_rows, qkv, *gathered, gains, bias),
        [full, ((LATE_COLS * HELD, BLK), bf16), ((HROWS, AROWS), f32), ((8, D), f32)],
        [pltpu.VMEM((3, D, D), bf16), square, square, pltpu.SemaphoreType.DMA((5,))],
    )


def shift_kernel(way, apart, source, got, ssem, rsem, lsem):
    size = lax.axis_size("dp")
    me = lax.axis_index("dp")
    core = lax.axis_index("opt")
    bar = pltpu.get_barrier_semaphore()
    for k in (1, 2):
        pl.semaphore_signal(bar, inc=1, device_id=((me - way * k + size) % size, core), device_id_type=MESH)
    own = pltpu.make_async_copy(source.at[0] if apart else source, got.at[0], lsem.at[0])
    own.start()
    pl.semaphore_wait(bar, 2)
    copies = [
        pltpu.make_async_remote_copy(
            src_ref=source.at[k] if apart else source, dst_ref=got.at[k], send_sem=ssem.at[k - 1], recv_sem=rsem.at[k - 1],
            device_id=((me + way * k + size) % size, core), device_id_type=MESH,
        )
        for k in (1, 2)
    ]
    for copy in copies:
        copy.start()
    own.wait()
    for copy in copies:
        copy.wait()


def shifted(source, way, apart, cid):
    shape = source.shape if apart else (PASS_EX,) + source.shape
    vmem = pl.BlockSpec(memory_space=pltpu.VMEM)
    return pl.pallas_call(
        functools.partial(shift_kernel, way, apart),
        in_specs=[vmem],
        out_specs=vmem,
        out_shape=jax.ShapeDtypeStruct(shape, source.dtype),
        scratch_shapes=[
            pltpu.SemaphoreType.DMA((2,)),
            pltpu.SemaphoreType.DMA((2,)),
            pltpu.SemaphoreType.DMA((1,)),
        ],
        compiler_params=pltpu.CompilerParams(collective_id=cid, has_side_effects=True),
        name="shift_rows",
    )(source)


def passed_along(values, by):
    size = lax.axis_size("dp")
    return lax.ppermute(values, "dp", [(i, (i + by) % size) for i in range(size)])


SQUARE = D * D // BLK
GROUP_ONE = 2 * D * FF // BLK + 3 * SQUARE
SMALL_ROWS = 512
GROUP_TWO = 3 * SQUARE + SMALL_ROWS


def put_blocks(out_ref, values, at=0):
    down, across = values.shape[0] // BLK, values.shape[1] // BLK
    for i in range(down):
        for j in range(across):
            out_ref[pl.ds(at + (i * across + j) * BLK, BLK), :] = to_low(
                values[i * BLK : (i + 1) * BLK, j * BLK : (j + 1) * BLK]
            )


def square_weight_kernel(columns, products, *refs):
    count = len(columns)
    sources, (out_ref, held, sems) = refs[:count], refs[count:]
    step = pl.program_id(0)

    def fetch(k):
        return pltpu.make_async_copy(sources[k].at[:, pl.ds(columns[k], D)], held.at[k], sems.at[k])

    @pl.when(step == 0)
    def _():
        for k in range(count):
            fetch(k).start()

    seen = set()
    for m, (a, b) in enumerate(products):
        fresh = [k for k in (a, b) if k not in seen]
        seen.update(fresh)

        @pl.when(step == m)
        def _(a=a, b=b, fresh=fresh):
            for k in fresh:
                fetch(k).wait()
            put_blocks(out_ref, dot_tn(held[a], held[b]))


def square_weight(operands, products, total):
    any_space = pl.BlockSpec(memory_space=pl.ANY)
    arrays = [array for array, _ in operands]
    columns = [col for _, col in operands]
    count = arrays[0].shape[0]
    return pl.pallas_call(
        functools.partial(square_weight_kernel, columns, products),
        grid=(len(products),),
        in_specs=[any_space] * len(arrays),
        out_specs=pl.BlockSpec((SQUARE, BLK), lambda p: (p, 0)),
        scratch_shapes=[pltpu.VMEM((len(arrays), count, D), bf16), pltpu.SemaphoreType.DMA((len(arrays),))],
        out_shape=jax.ShapeDtypeStruct((total, BLK), bf16),
        compiler_params=pltpu.CompilerParams(vmem_limit_bytes=VMEM_CAP),
        name="square_weight",
    )(*arrays)


def block_table():
    table = np.zeros((1009, 8), np.int32)
    wide = D // BLK
    early, late = 20 * wide, 5 * wide
    rows = (
        (DEC_QKV, 108, 1, 17 * wide, 0, early, late, 0),
        (DEC_OUT, 36, 1, 18 * wide, 3 * wide, early, late, 1),
        (CROSS_Q, 36, 1, 19 * wide, 4 * wide, early, late, 2),
        (DEC_UP, 144, 4, 0, wide, 12 * wide, 13 * wide, 0),
        (DEC_DOWN, 144, 4, 5 * wide, 9 * wide, 12 * wide, 16 * wide, 1),
        (CROSS_OUT, 36, 4, 10 * wide, 11 * wide, 12 * wide, 13 * wide, 2),
    )
    for first, count, kind, left, right, rest_left, rest_right, group in rows:
        for b in range(count):
            if first == DEC_QKV:
                m, k = divmod(b, 36)
                i, j = divmod(k, wide)
                j = j + wide * m
            else:
                i, j = divmod(b, 4 * wide if first == DEC_UP else wide)
            table[first + b] = (kind, 0, left + i, right + j, rest_left + i, rest_right + j, group, 0)
    for first, count, at in ((ENC_DOWN, 144, 144), (CROSS_KV, 72, 288), (ENC_OUT, 36, 360)):
        for b in range(count):
            table[first + b, :2] = (2, at + b)
    for b in range(144):
        i, j = divmod(b, 4 * wide)
        table[ENC_UP + b, :2] = (2, j // wide * 36 + i * wide + j % wide)
    for b in range(108):
        table[b, :2] = (3, b)
    return table


def update_kernel(
    slots, info, middle, late, one, two, master, stats, roots,
    grads, new_stats, new_master, sides, held, summed, sems,
):
    step = pl.program_id(0)
    steps = pl.num_programs(0)

    def each(step, action):
        buffer = lax.rem(step, 2)
        for s in range(slots):
            at = (step * slots + s) * 8
            kind = info[at]

            def copy(source, dest, k, s=s):
                return pltpu.make_async_copy(source, dest, sems.at[buffer, s, k])

            def rows_of(left, right, s=s, at=at, copy=copy):
                for k, source in enumerate((left, right, left, right)):
                    col = info[at + 2 + k]
                    if source is late:
                        part = source.at[:, pl.ds(pl.multiple_of(col * HELD, HELD), HELD)]
                    else:
                        part = source.at[:, :, pl.ds(pl.multiple_of(col * BLK, BLK), BLK)]
                    action(copy(part, sides.at[buffer, s, k], k))

            def block_of(source, s=s, at=at, copy=copy):
                row = pl.multiple_of(info[at + 1] * BLK, BLK)
                action(copy(source.at[pl.ds(row, BLK)], held.at[buffer, s], 4))

            pl.when(kind == 1)(functools.partial(rows_of, middle, late))
            pl.when(kind == 4)(functools.partial(rows_of, middle, middle))
            pl.when(kind == 2)(functools.partial(block_of, one))
            pl.when(kind == 3)(functools.partial(block_of, two))

    @pl.when(step == 0)
    def _():
        each(step, lambda copy: copy.start())

    @pl.when(step + 1 < steps)
    def _():
        each(step + 1, lambda copy: copy.start())

    each(step, lambda copy: copy.wait())
    buffer = lax.rem(step, 2)
    for s in range(slots):
        at = (step * slots + s) * 8
        kind = info[at]
        group = info[at + 6]

        @pl.when((kind == 1) | (kind == 4))
        def _(s=s, group=group):
            left, right, rest, rest_right = [sides[buffer, s, k].reshape(-1, BLK) for k in range(4)]
            row = lax.broadcasted_iota(jnp.int32, rest.shape, 0)
            mine = jnp.where(row % HELD // REST == group, rest, jnp.zeros_like(rest))
            summed[s] = dot_tn(left, right) + dot_tn(mine, rest_right)

        @pl.when((kind == 2) | (kind == 3))
        def _(s=s):
            summed[s] = held[buffer, s].astype(f32)

        @pl.when(kind == 0)
        def _(s=s):
            summed[s] = jnp.zeros((BLK, BLK), f32)

    for s in range(slots):
        grad = summed[s]
        low = to_low(grad)
        grads[s] = grad
        new_stats[s, 0] = stat_decay * stats[s, 0] + (1.0 - stat_decay) * dot_nt(low, low)
        new_stats[s, 1] = stat_decay * stats[s, 1] + (1.0 - stat_decay) * dot_tn(low, low)
        shaped = dot(to_low(roots[s, 0]), low)
        shaped = dot(to_low(shaped), to_low(roots[s, 1]))
        old = master[s]
        shaped_rms = jnp.sqrt(jnp.mean(shaped * shaped) + 1e-06)
        weight_rms = jnp.sqrt(jnp.mean(old * old) + 1e-06)
        new_master[s] = old - (block_rate * weight_rms / shaped_rms) * shaped


def update_blocks(info, middle, late, one, two, master, kron_stats, inverse_roots):
    count = master.shape[0]
    slots = min(4, count)
    devices = late.shape[0]
    any_space = pl.BlockSpec(memory_space=pl.ANY)
    block = pl.BlockSpec((slots, BLK, BLK), lambda p, *_: (p, 0, 0))
    pair = pl.BlockSpec((slots, 2, BLK, BLK), lambda p, *_: (p, 0, 0, 0))
    return pl.pallas_call(
        functools.partial(update_kernel, slots),
        grid_spec=pltpu.PrefetchScalarGridSpec(
            num_scalar_prefetch=1,
            grid=(count // slots,),
            in_specs=[any_space] * 4 + [block, pair, pair],
            out_specs=[block, pair, block],
            scratch_shapes=[
                pltpu.VMEM((2, slots, 4, devices, HELD, BLK), bf16),
                pltpu.VMEM((2, slots, BLK, BLK), bf16),
                pltpu.VMEM((slots, BLK, BLK), f32),
                pltpu.SemaphoreType.DMA((2, slots, 5)),
            ],
        ),
        out_shape=[
            jax.ShapeDtypeStruct(master.shape, f32),
            jax.ShapeDtypeStruct(kron_stats.shape, f32),
            jax.ShapeDtypeStruct(master.shape, f32),
        ],
        compiler_params=pltpu.CompilerParams(vmem_limit_bytes=VMEM_CAP),
        name="update_blocks",
    )(info, middle, late, one, two, master, kron_stats, inverse_roots)


def order_kernel(order, master, small, near, far, held, sems):
    count = held.shape[0]
    for s in range(count):
        pltpu.make_async_copy(master.at[order[s]], held.at[s], sems.at[s]).start()
    near[0:EXTRA, :] = small[...]
    first = near.shape[0]
    for s in range(count):
        pltpu.make_async_copy(master.at[order[s]], held.at[s], sems.at[s]).wait()
        at = EXTRA + s * BLK
        if at < first:
            near[at : at + BLK, :] = to_low(held[s])
        else:
            far[at - first : at - first + BLK, :] = to_low(held[s])


def ordered_shards(order, master, small, near_rows):
    count = master.shape[0]
    shapes = [(near_rows, BLK), (max(EXTRA + count * BLK - near_rows, EXTRA), BLK)]
    return pl.pallas_call(
        order_kernel,
        grid_spec=pltpu.PrefetchScalarGridSpec(
            num_scalar_prefetch=1,
            grid=(1,),
            in_specs=[pl.BlockSpec(memory_space=pl.ANY), whole_spec(small.shape)],
            out_specs=[whole_spec(shape) for shape in shapes],
            scratch_shapes=[pltpu.VMEM((count, BLK, BLK), f32), pltpu.SemaphoreType.DMA((count,))],
        ),
        out_shape=[jax.ShapeDtypeStruct(shape, bf16) for shape in shapes],
        name="ordered_shards",
    )(order, master, small)


def total_all(terms, dp_count):
    if dp_count == 16:
        return total_rows_all(terms, dp_count, 1)
    return lax.psum(terms, ("dp", "opt"))


def gather_low(rows):
    return lax.all_gather(rows, ("dp", "opt"), axis=0, tiled=True)


def pad_rows(array, rows):
    return jnp.pad(array, ((0, rows - array.shape[0]),) + ((0, 0),) * (array.ndim - 1))


def per_device(
    enc_in,
    enc_cot,
    dec_in,
    dec_cot,
    passage_lengths,
    passage_example,
    answer_tokens,
    owner_slot,
    master,
    kron_stats,
    inverse_roots,
    small_params,
    small_moment,
):
    dp_count = lax.axis_size("dp")
    pair_count = lax.axis_size("opt")
    devices = dp_count * pair_count
    slot_dev = master.shape[0]
    small_dev = small_params.shape[0]
    dev_rows = slot_dev * BLK + EXTRA
    table_size = NB * H
    device = lax.axis_index("dp") * pair_count + lax.axis_index("opt")

    kinds = jnp.asarray((np.arange(owner_slot.shape[0]) >= DEC_QKV).astype(np.int32))
    owners, local = owner_slot // slot_dev, owner_slot % slot_dev
    keys = (owners * 4 + kinds) * slot_dev + local
    before = (keys[None, :] < keys[:, None]) & (owners[None, :] == owners[:, None])
    rank = jnp.sum(before.astype(jnp.int32), axis=1)
    split = dp_count == 16 and slot_dev > EARLY_SLOTS
    near_slots = EARLY_SLOTS if split else slot_dev
    near_rows, far_rows = EXTRA + near_slots * BLK, (slot_dev - near_slots) * BLK
    rows = jnp.where(
        rank < near_slots,
        owners * near_rows + EXTRA + rank * BLK,
        -1 - (owners * far_rows + (rank - near_slots) * BLK),
    ).astype(jnp.int32)
    mine = owner_slot[None, :] == (device * slot_dev + jnp.arange(slot_dev))[:, None]
    block_at = jnp.sum(jnp.where(mine, jnp.arange(owner_slot.shape[0])[None, :] + 1, 0), axis=1)
    own_kind = 2 - jnp.sum(jnp.where(mine, 2 - kinds[None, :], 0), axis=1)
    own_keys = own_kind * slot_dev + jnp.arange(slot_dev)
    own_rank = jnp.sum((own_keys[None, :] < own_keys[:, None]).astype(jnp.int32), axis=1)
    order = jnp.sum(
        jnp.where(own_rank[None, :] == jnp.arange(slot_dev)[:, None], jnp.arange(slot_dev)[None, :], 0), axis=1
    ).astype(jnp.int32)

    padded = jnp.pad(to_low(small_params), (0, EXTRA * BLK - small_dev)).reshape(EXTRA, BLK)
    near, later = ordered_shards(order, master, padded, near_rows)
    if split:
        near = gather_rows(near, near_rows, dp_count, 0)
        later, near = lax.optimization_barrier((later, near))
        far = gather_low(later)
    else:
        near = far = gather_low(near)
    small_all = near.reshape(devices, near_rows, BLK)[:, :EXTRA]
    small_all = small_all.reshape(devices, EXTRA * BLK)[:, :small_dev].reshape(-1).astype(f32)
    gains = pad_rows(small_all[: 6 * D].reshape(6, D), 8)
    strips = bias_strips(small_all[6 * D : 6 * D + table_size])

    def encoder(rows, gathered):
        qkv, log_total, mixed, hidden, whole = encoder_attend(rows, passage_lengths, enc_in, gathered, gains, strips)
        inner, output, encoded, up, down = encoder_feed(rows, hidden, gathered, gains)
        return qkv, log_total, mixed, hidden, whole, inner, output, encoded, up, down

    gathered = (near, far)
    if split:
        state = encoder(jnp.maximum(rows, 0), (near, near))
        far, state = lax.optimization_barrier((far, state))
        gathered = (near, far)
        late_blocks = jnp.any((kinds == 0) & (rank >= near_slots))

        def again(carry):
            count, fresh_rows = lax.optimization_barrier((carry[0], rows))
            return count + 1, encoder(fresh_rows, gathered)

        _, state = lax.while_loop(
            lambda carry: carry[0] < late_blocks.astype(jnp.int32), again, (jnp.int32(0), state)
        )
    else:
        state = encoder(rows, gathered)
    qkv, log_total, mixed, hidden, whole, inner, output, encoded, up, down = state
    answer_at = np.arange(AROWS)
    dec_buckets = bucket_of(np.minimum(answer_at, ALEN - 1)[None, :] - np.minimum(answer_at, ALEN - 1)[:, None], False)
    dec_onehot = jnp.asarray((dec_buckets[..., None] == np.arange(NB)).reshape(-1, NB).astype(np.float32))
    dec_bias = jnp.dot(
        small_all[6 * D + table_size :].reshape(NB, H).T, dec_onehot.T, precision=exact_prec, preferred_element_type=f32
    ).reshape(HROWS, AROWS)

    dec_rows, encoded = lax.optimization_barrier((pad_rows(dec_in, AROWS), encoded))
    dec_qkv, first, cross_queries, early = decoder_self(rows, dec_rows, gathered, gains, dec_bias)
    moved = [passed_along(cross_queries, k) for k in (1, 2)]
    memory = cross_memory(rows, encoded, gathered)
    moved, memory = lax.optimization_barrier((moved, memory))
    queries = jnp.stack([cross_queries] + moved)
    owner_dp = passage_example // EX_DEV // pair_count
    offsets = ((lax.axis_index("dp") - owner_dp) % dp_count).astype(jnp.int32)

    parts = cross_attend(passage_lengths, offsets, queries, memory)
    parts = shifted(parts, -1, True, 3)
    valid = (pad_rows(answer_tokens.reshape(ALEN, 1), AROWS) != 0).astype(f32)
    dec_out, middle, back, second_grad, gain_six = decoder_feed(
        rows, parts, first, pad_rows(dec_cot, AROWS), jnp.broadcast_to(valid, (AROWS, BLK)), early, gathered, gains
    )
    middle, back = lax.optimization_barrier((middle, back))
    middle = gather_low(middle)
    memory_grad, query_parts, upstream = cross_back(
        rows, passage_lengths, offsets, queries, shifted(back, 1, False, 4), memory, enc_cot, gathered
    )
    query_parts = [query_parts[0]] + [passed_along(query_parts[k], -k) for k in (1, 2)]

    act, inner_grad, branch, normed_two, hidden_grad, attn_grad, mixed_grad, gain_two = feed_back(
        output, hidden, inner, upstream, down, up, whole, gains
    )
    query_parts, inner_grad = lax.optimization_barrier((query_parts, inner_grad))
    dec_in_grad, late, dec_scores, gain_four = decoder_self_back(
        rows, query_parts, second_grad, first, dec_rows, dec_qkv, gathered, gains, dec_bias
    )
    one = square_weight(
        [(normed_two, 0)] + [(inner_grad, k * D) for k in range(4)]
        + [(branch, 0)] + [(act, k * D) for k in range(4)]
        + [(encoded, 0), (memory_grad, 0), (memory_grad, D), (mixed, 0), (attn_grad, 0)],
        [(0, 1 + k) for k in range(4)] + [(6 + k, 5) for k in range(4)] + [(10, 11), (10, 12), (13, 14)],
        GROUP_ONE,
    )
    grad_query, grad_key, grad_value, enc_table, one, late = attend_back(
        passage_lengths, qkv, mixed_grad, log_total, strips, one, late, dp_count, 6
    )
    one, middle = lax.optimization_barrier((one, middle))
    one = gather_low(one)
    enc_in_grad, normed, gain_one = input_back(
        enc_in, grad_query, grad_key, grad_value, hidden_grad, whole, gains
    )
    two = square_weight(
        [(normed, 0), (grad_query, 0), (grad_key, 0), (grad_value, 0)], [(0, 1), (0, 2), (0, 3)], GROUP_TWO
    )

    enc_table = enc_table[:, :2, :NB].reshape(H, NB).T
    dec_table = jnp.dot(
        dec_scores.reshape(H, AROWS * AROWS), dec_onehot, precision=exact_prec, preferred_element_type=f32
    ).T
    small_terms = jnp.concatenate(
        [gain_one[0], gain_two[0], gain_two[1], gain_four[0], gain_four[1], gain_six[0], enc_table.reshape(-1), dec_table.reshape(-1)]
    )
    small_rows = pad_rows(to_low(small_terms).reshape(-1, BLK), SMALL_ROWS)
    two = total_all(lax.dynamic_update_slice(two, small_rows, (3 * SQUARE, 0)), dp_count)

    small_grads = lax.dynamic_slice(two[3 * SQUARE :].reshape(-1), (device * small_dev,), (small_dev,)).astype(f32)
    info = jnp.asarray(np.roll(block_table(), 1, axis=0))[block_at].reshape(-1)
    middle, late = (part.reshape(devices, -1, part.shape[1]) for part in (middle, late))
    block_grads, new_stats, new_master = update_blocks(info, middle, late, one, two, master, kron_stats, inverse_roots)
    new_moment = moment_decay * small_moment + small_grads
    new_small = small_params - small_rate * new_moment
    return (
        dec_out[:ALEN],
        encoded,
        enc_in_grad,
        dec_in_grad[:ALEN],
        block_grads,
        new_stats,
        new_master,
        small_grads,
        new_moment,
        new_small,
    )


def solution(mesh):
    placed = (
        P(("dp", "opt"), None),
        P(("dp", "opt"), None),
        P(("dp", "opt"), None),
        P(("dp", "opt"), None),
        P(("dp", "opt")),
        P(("dp", "opt")),
        P(("dp", "opt"), None),
        P(),
        P(("dp", "opt"), None, None),
        P(("dp", "opt"), None, None, None),
        P(("dp", "opt"), None, None, None),
        P(("dp", "opt")),
        P(("dp", "opt")),
    )
    return jax.shard_map(
        per_device,
        mesh=mesh,
        in_specs=placed,
        out_specs=(
            P(("dp", "opt"), None),
            P(("dp", "opt"), None),
            P(("dp", "opt"), None),
            P(("dp", "opt"), None),
            P(("dp", "opt"), None, None),
            P(("dp", "opt"), None, None, None),
            P(("dp", "opt"), None, None),
            P(("dp", "opt")),
            P(("dp", "opt")),
            P(("dp", "opt")),
        ),
        check_vma=False,
    )
```

```python
import functools

import jax
import jax.numpy as jnp
import numpy as np
from jax import lax
from jax.experimental import pallas as pl
from jax.experimental.pallas import tpu as pltpu
from jax.sharding import PartitionSpec as P

D = 768
H = 12
HD = 64
FF = 3072
NB = 32
MAXD = 128
BLK = 128
PASS_SLOT = 512
PASS_EX = 3
ALEN = 20
EX_DEV = 1
AROWS = 32
PAIRS = H // 2
STRIP = 7 * BLK
EXTRA = 16
SURE = 248
EARLY_SLOTS = 22

exact_prec = lax.Precision.HIGHEST
neg_fill = -1000000000.0
stat_decay = 0.95
block_rate = 0.5
moment_decay = 0.9
small_rate = 0.002
MESH = pl.DeviceIdType.MESH
VMEM_CAP = 60 << 20
f32 = jnp.float32
bf16 = jnp.bfloat16

ENC_QKV, ENC_OUT, ENC_UP, ENC_DOWN = 0, 108, 144, 288
DEC_QKV, DEC_OUT, CROSS_Q, CROSS_KV, CROSS_OUT, DEC_UP, DEC_DOWN = 432, 540, 576, 612, 684, 720, 864


def dot(left, right):
    return jnp.dot(left, right, preferred_element_type=f32)


def dot_nt(left, right):
    return lax.dot_general(left, right, (((1,), (1,)), ((), ())), preferred_element_type=f32)


def dot_tn(left, right):
    return lax.dot_general(left, right, (((0,), (0,)), ((), ())), preferred_element_type=f32)


def to_low(values):
    return values.astype(bf16)


def rms_factor(values):
    return lax.rsqrt(jnp.mean(values * values, axis=-1, keepdims=True) + 1e-06)


def rms_scale(values, gain):
    return values * rms_factor(values) * gain


def norm_back(values, gain, upstream):
    factor = rms_factor(values)
    scaled = values * factor
    lifted = upstream * gain
    inner = jnp.mean(lifted * scaled, axis=-1, keepdims=True)
    rows = factor * (lifted - scaled * inner)
    return rows, jnp.sum(upstream * scaled, axis=0, keepdims=True)


GATE_A = float(np.sqrt(2.0 / np.pi))
GATE_B = 0.044715


def gate(values):
    return 0.5 * values * (1.0 + jnp.tanh(GATE_A * (values + GATE_B * values * values * values)))


def gate_both(values):
    square = values * values
    bend = jnp.tanh(GATE_A * values * (1.0 + GATE_B * square))
    half = 0.5 * (1.0 + bend)
    slope = half + 0.5 * values * (1.0 - bend * bend) * (GATE_A * (1.0 + 3.0 * GATE_B * square))
    return values * half, slope


def bucket_of(offsets, both_sides):
    if both_sides:
        halves = NB // 2
        bucket_base = (offsets > 0) * halves
        distance = np.abs(offsets)
    else:
        halves = NB
        bucket_base = offsets * 0
        distance = np.maximum(-offsets, 0)
    exact_count = halves // 2
    widened = np.maximum(distance, 1) * 1.0
    far_bucket = exact_count + np.floor(
        np.log(widened / exact_count) / np.log(MAXD / exact_count) * (halves - exact_count)
    ).astype(np.int32)
    far_bucket = np.minimum(far_bucket, halves - 1)
    return (bucket_base + np.where(distance < exact_count, distance, far_bucket)).astype(np.int32)


def strip_buckets():
    rho = np.arange(2 * BLK, 5 * BLK)[:, None]
    return bucket_of(rho - 3 * BLK - np.arange(BLK)[None, :], True)


def start_blocks(rows_ref, gathered, first, rows, cols, dest, sem):
    across = cols // BLK

    def body(b, carry):
        i = b // across
        j = b - i * across
        row = rows_ref[first + b]
        place = dest.at[pl.ds(pl.multiple_of(i * BLK, BLK), BLK), pl.ds(pl.multiple_of(j * BLK, BLK), BLK)]

        @pl.when(row >= 0)
        def _():
            pltpu.make_async_copy(gathered[0].at[pl.ds(pl.multiple_of(row, 16), BLK)], place, sem).start()

        @pl.when(row < 0)
        def _():
            pltpu.make_async_copy(gathered[1].at[pl.ds(pl.multiple_of(-1 - row, 16), BLK)], place, sem).start()

        return carry

    lax.fori_loop(0, rows // BLK * across, body, 0)


def wait_whole(dest, sem):
    pltpu.make_async_copy(dest, dest, sem).wait()


def head_lanes(rows, head):
    lane = lax.broadcasted_iota(jnp.int32, (rows, BLK), 1)
    return (lane < HD) if head == 0 else (lane >= HD)


ORDERS = {"A": (3, 2, 0, 1), "B": (3, 2, 1, 0), "C": (0, 1, 3, 2), "D": (1, 0, 3, 2)}


def chunk_plan(rows, nbits, names, shares):
    if nbits != 4:
        return [(0, rows, tuple(range(nbits - 1, -1, -1)))]
    total = sum(shares)
    plan, first = [], 0
    for k, name in enumerate(names):
        size = rows - first if k == len(names) - 1 else rows * shares[k] // total // 16 * 16
        plan.append((first, size, ORDERS[name]))
        first += size
    return plan


class Tree:
    def __init__(self, order):
        self.order, self.nbits = order, len(order)

    def last(self, m):
        return max([t for t, b in enumerate(self.order) if m >> b & 1], default=-1)

    def rank(self, m):
        t = self.last(m)
        peers = [x for x in range(1 << self.nbits) if self.last(x) == t]
        return (peers.index(m) + 0.5) / len(peers)

    def children(self, m):
        return [m | 1 << self.order[t] for t in range(self.last(m) + 1, self.nbits)]

    def bit(self, m):
        return 1 << self.order[self.last(m)]


def enter_tree(nbits):
    me, core = lax.axis_index("dp"), lax.axis_index("opt")
    barrier = pltpu.get_barrier_semaphore()
    for b in range(nbits):
        pl.semaphore_signal(barrier, inc=1, device_id=(me ^ (1 << b), core), device_id_type=MESH)
    pl.semaphore_signal(barrier, inc=1, device_id=(me, 1 - core), device_id_type=MESH)
    pl.semaphore_wait(barrier, nbits + 1)


def spread_steps(plan, nbits, rows, source, out_ref, sems):
    ssem, rsem, ssib, rsib, lsem = sems
    me, core = lax.axis_index("dp"), lax.axis_index("opt")
    masks = range(1 << nbits)
    trees = [Tree(order) for _, _, order in plan]

    def region(c, m, o):
        first, size, _ = plan[c]
        return out_ref.at[pl.ds(pl.multiple_of(((me ^ m) * 2 + o) * rows + first, 16), size)]

    def down(c, m):
        parent = m ^ trees[c].bit(m)
        return lambda sending: pltpu.make_async_remote_copy(
            (source(c) if parent == 0 else region(c, parent, core)) if sending else region(c, m, core),
            region(c, parent, core) if sending else region(c, m, core),
            ssem.at[c, m], rsem.at[c, m], device_id=(me ^ trees[c].bit(m), core), device_id_type=MESH,
        )

    def across(c, m):
        return pltpu.make_async_remote_copy(
            region(c, m, core) if m else source(c), region(c, m, core),
            ssib.at[c, m], rsib.at[c, m], device_id=(me, 1 - core), device_id_type=MESH,
        )

    def arrived(c, m):
        ref = region(c, m, 1 - core)
        return pltpu.make_async_remote_copy(
            ref, ref, ssib.at[c, m], rsib.at[c, m], device_id=(me, 1 - core), device_id_type=MESH
        )

    def keep(c):
        return pltpu.make_async_copy(source(c), region(c, 0, core), lsem.at[c, 0])

    def step(c, m):
        if m:
            down(c, m)(False).wait_recv()
        for child in trees[c].children(m):
            down(c, child)(True).start()
        across(c, m).start()
        if m == 0:
            keep(c).start()

    def end():
        for c in range(len(plan)):
            for m in masks:
                arrived(c, m).wait_recv()
                across(c, m).wait_send()
                if m:
                    down(c, m)(True).wait_send()
            keep(c).wait()

    keys = sorted((trees[c].last(m) * 100 + trees[c].rank(m) * (trees[c].last(m) + 2), c, m) for c in range(len(plan)) for m in masks)
    return [functools.partial(step, c, m) for _, c, m in keys], end


def sum_steps(plan, nbits, rows, terms_ref, put, own, sib, land, sems):
    ssem, rsem, ssib, rsib, lsem = sems
    me, core = lax.axis_index("dp"), lax.axis_index("opt")
    trees = [Tree(order) for _, _, order in plan]

    def span(c):
        return pl.ds(plan[c][0], plan[c][1])

    def source(c, m, o):
        first, size, _ = plan[c]
        return terms_ref.at[pl.ds(pl.multiple_of(((me ^ m) * 2 + o) * rows + first, 16), size)]

    def load(c, m):
        return pltpu.make_async_copy(source(c, m, core), own.at[m, span(c)], lsem.at[c, m])

    def across(c, m):
        return pltpu.make_async_remote_copy(
            source(c, m, 1 - core), sib.at[m, span(c)], ssib.at[c, m], rsib.at[c, m],
            device_id=(me, 1 - core), device_id_type=MESH,
        )

    def up(c, m):
        return pltpu.make_async_remote_copy(
            own.at[m, span(c)], land.at[m - 1, span(c)], ssem.at[c, m], rsem.at[c, m],
            device_id=(me ^ trees[c].bit(m), core), device_id_type=MESH,
        )

    def step(c, m):
        first, size, _ = plan[c]
        load(c, m).wait()
        across(c, m).wait_recv()
        arrived = [child - 1 for child in trees[c].children(m)]
        for child in reversed(trees[c].children(m)):
            up(c, child).wait_recv()

        def add(i, count):
            at = pl.ds(pl.multiple_of(first + i * BLK, 16), count)
            total = own[m, at, :].astype(f32) + sib[m, at, :].astype(f32)
            for child in arrived:
                total = total + land[child, at, :].astype(f32)
            if m:
                own[m, at, :] = to_low(total)
            else:
                put(at, total)

        def body(i, carry):
            add(i, BLK)
            return carry

        lax.fori_loop(0, size // BLK, body, 0)
        if size % BLK:
            add(size // BLK, size % BLK)
        if m:
            up(c, m).start()

    stages = lambda c, m: nbits - 1 - trees[c].last(m)
    keys = sorted(
        (stages(c, m) * 8 + trees[c].rank(m) * 8 + 2 * c, c, m) for c in range(len(plan)) for m in range(1 << nbits)
    )

    def begin():
        for _, c, m in keys:
            load(c, m).start()
            across(c, m).start()

    def end():
        for _, c, m in keys:
            across(c, m).wait_send()
            if m:
                up(c, m).wait_send()

    return begin, [functools.partial(step, c, m) for _, c, m in keys], end


def tree_sems(plan, nbits):
    return [pltpu.SemaphoreType.DMA((len(plan), 1 << nbits))] * 5


def sum_scratch(rows, nbits):
    many = 1 << nbits
    return [pltpu.VMEM((count, rows, BLK), bf16) for count in (many, many, many - 1)]


def together(steps, more):
    placed = [(k / len(steps), 0, k, step) for k, step in enumerate(steps)]
    placed += [(k / len(more), 1, k, step) for k, step in enumerate(more)]
    return [step for _, _, _, step in sorted(placed, key=lambda entry: entry[:3])]


def gather_kernel(plan, nbits, rows, shard, out_ref, *sems):
    enter_tree(nbits)
    steps, end = spread_steps(plan, nbits, rows, lambda c: shard.at[pl.ds(plan[c][0], plan[c][1])], out_ref, sems)
    for step in steps:
        step()
    end()


def gather_rows(shard, rows, dp_count, cid):
    nbits = dp_count.bit_length() - 1
    plan = chunk_plan(rows, nbits, "ABABABCD", (1,) * 8)
    any_space = pl.BlockSpec(memory_space=pl.ANY)
    return pl.pallas_call(
        functools.partial(gather_kernel, plan, nbits, rows),
        out_shape=jax.ShapeDtypeStruct((dp_count * 2 * rows, BLK), shard.dtype),
        in_specs=[any_space],
        out_specs=any_space,
        scratch_shapes=tree_sems(plan, nbits),
        compiler_params=pltpu.CompilerParams(collective_id=cid, has_side_effects=True),
        name="gather_rows",
    )(shard)


def total_kernel(plan, nbits, rows, terms, out_ref, own, sib, land, *sems):
    enter_tree(nbits)

    def put(at, total):
        own[0, at, :] = to_low(total)

    begin, steps, end = sum_steps(plan, nbits, rows, terms, put, own, sib, land, sems[:5])
    begin()
    for step in steps:
        step()
    more, last = spread_steps(plan, nbits, rows, lambda c: own.at[0, pl.ds(plan[c][0], plan[c][1])], out_ref, sems[5:])
    for step in more:
        step()
    end()
    last()


def total_rows_all(terms, dp_count, cid):
    rows = terms.shape[0] // (dp_count * 2)
    nbits = dp_count.bit_length() - 1
    plan = chunk_plan(rows, nbits, "ABCD", (3, 3, 1, 1))
    return pl.pallas_call(
        functools.partial(total_kernel, plan, nbits, rows),
        out_shape=jax.ShapeDtypeStruct(terms.shape, bf16),
        in_specs=[pl.BlockSpec(memory_space=pl.ANY)],
        out_specs=pl.BlockSpec(memory_space=pl.ANY),
        scratch_shapes=sum_scratch(rows, nbits) + tree_sems(plan, nbits) * 2,
        compiler_params=pltpu.CompilerParams(collective_id=cid, has_side_effects=True, vmem_limit_bytes=VMEM_CAP),
        name="total_rows",
    )(terms)


def strip_kernel(table, buckets, out):
    head = pl.program_id(0)
    which = buckets[...]
    total = jnp.zeros((3 * BLK, BLK), f32)
    for b in range(NB):
        total = jnp.where(which == b, table[b * H + head], total)
    out[0, 0 : 2 * BLK, :] = jnp.full((2 * BLK, BLK), table[(NB // 2 - 1) * H + head], f32)
    out[0, 2 * BLK : 5 * BLK, :] = total
    out[0, 5 * BLK :, :] = jnp.full((2 * BLK, BLK), table[(NB - 1) * H + head], f32)


def bias_strips(table):
    return pl.pallas_call(
        strip_kernel,
        grid=(H,),
        in_specs=[
            pl.BlockSpec(memory_space=pltpu.SMEM),
            pl.BlockSpec((3 * BLK, BLK), lambda h: (0, 0)),
        ],
        out_specs=pl.BlockSpec((1, STRIP, BLK), lambda h: (h, 0, 0)),
        out_shape=jax.ShapeDtypeStruct((H, STRIP, BLK), f32),
        name="bias_strips",
    )(table, jnp.asarray(strip_buckets()))


def masked_scores(keys, queries, strip, offset, length):
    rows = keys.shape[0]
    scores = dot_nt(keys, queries)
    bias = jnp.concatenate(
        [strip[(3 - n) * BLK : (3 - n) * BLK + rows, :] for n in range(offset, offset + queries.shape[0] // BLK)], axis=1
    )
    key_at = lax.broadcasted_iota(jnp.int32, scores.shape, 0)
    scores = scores + bias
    return jnp.concatenate([scores[:SURE], jnp.where(key_at[SURE:] < length, scores[SURE:], neg_fill)], axis=0)


def attend_kernel(
    rows_ref, lengths, x_ref, near, far, gains, strips, qkv, lse, mixed, hidden, whole, wqkv, sems, out_sem
):
    step = pl.program_id(0)
    keep = pltpu.make_async_copy(wqkv, whole, out_sem.at[0])

    @pl.when(step == 0)
    def _():
        for m in range(4):
            start_blocks(rows_ref, (near, far), 36 * m, D, D, wqkv.at[m], sems.at[m])

    values = x_ref[...].astype(f32)
    normed = to_low(rms_scale(values, gains[0:1, :]))
    for m in range(3):

        @pl.when(step == 0)
        def _(m=m):
            wait_whole(wqkv.at[m], sems.at[m])

        qkv[:, m * D : (m + 1) * D] = to_low(dot(normed, wqkv[m]))

    @pl.when(step == 0)
    def _():
        wait_whole(wqkv.at[3], sems.at[3])
        keep.start()

    length = lengths[step]

    def one_pair(pair, carry):
        at = pl.multiple_of(pair * BLK, BLK)
        queries = qkv[:, pl.ds(at, BLK)]
        keys = qkv[:, pl.ds(pl.multiple_of(at + D, BLK), BLK)]
        turned = qkv[:, pl.ds(pl.multiple_of(at + 2 * D, BLK), BLK)].T
        outs = []
        for head in range(2):
            only = jnp.where(head_lanes(PASS_SLOT, head), queries, jnp.zeros_like(queries))
            scores = masked_scores(keys, only, strips.at[2 * pair + head], 0, length)
            peak = jnp.max(scores, axis=0, keepdims=True)
            expos = jnp.exp(scores - peak)
            total = jnp.sum(expos, axis=0, keepdims=True)
            lse[0, pl.ds(2 * pair + head, 1), :] = peak + jnp.log(total)
            outs.append(dot(turned, to_low(expos)) * (1.0 / total))
        lane = lax.broadcasted_iota(jnp.int32, (BLK, PASS_SLOT), 0)
        mixed[:, pl.ds(at, BLK)] = to_low(jnp.where(lane < HD, outs[0], outs[1]).T)
        return carry

    lax.fori_loop(0, PAIRS, one_pair, 0, unroll=2)
    hidden[...] = x_ref[...].astype(f32) + dot(mixed[...], wqkv[3])
    pl.when(step == pl.num_programs(0) - 1)(lambda: keep.wait())


def encoder_attend(rows, lengths, enc_in, gathered, gains, strips):
    count = lengths.shape[0]
    total = count * PASS_SLOT
    by_row = lambda p, *_: (p, 0)
    any_space = pl.BlockSpec(memory_space=pl.ANY)
    return pl.pallas_call(
        attend_kernel,
        grid_spec=pltpu.PrefetchScalarGridSpec(
            num_scalar_prefetch=2,
            grid=(count,),
            in_specs=[
                pl.BlockSpec((PASS_SLOT, D), by_row),
                any_space,
                any_space,
                pl.BlockSpec((8, D), lambda p, *_: (0, 0)),
                pl.BlockSpec((H, STRIP, BLK), lambda p, *_: (0, 0, 0)),
            ],
            out_specs=[
                pl.BlockSpec((PASS_SLOT, 3 * D), by_row),
                pl.BlockSpec((1, 16, PASS_SLOT), lambda p, *_: (p, 0, 0)),
                pl.BlockSpec((PASS_SLOT, D), by_row),
                pl.BlockSpec((PASS_SLOT, D), by_row),
                any_space,
            ],
            scratch_shapes=[
                pltpu.VMEM((4, D, D), bf16),
                pltpu.SemaphoreType.DMA((4,)),
                pltpu.SemaphoreType.DMA((1,)),
            ],
        ),
        out_shape=[
            jax.ShapeDtypeStruct((total, 3 * D), bf16),
            jax.ShapeDtypeStruct((count, 16, PASS_SLOT), f32),
            jax.ShapeDtypeStruct((total, D), bf16),
            jax.ShapeDtypeStruct((total, D), f32),
            jax.ShapeDtypeStruct((4, D, D), bf16),
        ],
        compiler_params=pltpu.CompilerParams(vmem_limit_bytes=VMEM_CAP),
        name="encoder_attend",
    )(rows, lengths, enc_in, *gathered, gains, strips)


FEED_CHUNK = 1536
FCHUNK = 768


def feed_kernel(rows_ref, hidden, near, far, gains, inner, output, encoded, up, down, wup, wdown, sems, out_sems):
    step = pl.program_id(0)
    keeps = [pltpu.make_async_copy(wup, up, out_sems.at[0]), pltpu.make_async_copy(wdown, down, out_sems.at[1])]

    @pl.when(step == 0)
    def _():
        start_blocks(rows_ref, (near, far), ENC_UP, D, FF, wup, sems.at[0])
        start_blocks(rows_ref, (near, far), ENC_DOWN, FF, D, wdown, sems.at[1])

    normed = to_low(rms_scale(hidden[...], gains[1:2, :]))
    total = hidden[...]

    @pl.when(step == 0)
    def _():
        wait_whole(wup, sems.at[0])
        wait_whole(wdown, sems.at[1])
        for keep in keeps:
            keep.start()

    for c in range(FF // FEED_CHUNK):
        cols = slice(c * FEED_CHUNK, (c + 1) * FEED_CHUNK)
        act = dot(normed, wup[:, cols])
        inner[:, cols] = to_low(act)
        total = total + dot(to_low(gate(act)), wdown[cols, :])
    output[...] = total
    encoded[...] = to_low(rms_scale(total, gains[2:3, :]))

    @pl.when(step == pl.num_programs(0) - 1)
    def _():
        for keep in keeps:
            keep.wait()


def encoder_feed(rows, hidden, gathered, gains):
    total = hidden.shape[0]
    tile = 512
    by_row = lambda p, *_: (p, 0)
    any_space = pl.BlockSpec(memory_space=pl.ANY)
    return pl.pallas_call(
        feed_kernel,
        grid_spec=pltpu.PrefetchScalarGridSpec(
            num_scalar_prefetch=1,
            grid=(total // tile,),
            in_specs=[
                pl.BlockSpec((tile, D), by_row),
                any_space,
                any_space,
                pl.BlockSpec((8, D), lambda p, *_: (0, 0)),
            ],
            out_specs=[
                pl.BlockSpec((tile, FF), by_row),
                pl.BlockSpec((tile, D), by_row),
                pl.BlockSpec((tile, D), by_row),
                any_space,
                any_space,
            ],
            scratch_shapes=[
                pltpu.VMEM((D, FF), bf16),
                pltpu.VMEM((FF, D), bf16),
                pltpu.SemaphoreType.DMA((2,)),
                pltpu.SemaphoreType.DMA((2,)),
            ],
        ),
        out_shape=[
            jax.ShapeDtypeStruct((total, FF), bf16),
            jax.ShapeDtypeStruct((total, D), f32),
            jax.ShapeDtypeStruct((total, D), bf16),
            jax.ShapeDtypeStruct((D, FF), bf16),
            jax.ShapeDtypeStruct((FF, D), bf16),
        ],
        compiler_params=pltpu.CompilerParams(vmem_limit_bytes=VMEM_CAP),
        name="encoder_feed",
    )(rows, hidden, *gathered, gains)


def feed_back_kernel(
    output, hidden, inner, upstream, down, up, out, gains,
    act_low, inner_grad, branch, normed, hidden_grad, attn_grad, mixed_grad, gain_sums,
    wup, wdown, wout, sems,
):
    step = pl.program_id(0)

    @pl.when(step == 0)
    def _():
        pltpu.make_async_copy(down, wdown, sems.at[0]).start()
        pltpu.make_async_copy(up, wup, sems.at[1]).start()
        pltpu.make_async_copy(out.at[3], wout, sems.at[2]).start()
        gain_sums[...] = jnp.zeros_like(gain_sums)

    output_grad, final_gain = norm_back(output[...], gains[2:3, :], upstream[...])
    low = to_low(output_grad)
    branch[...] = low

    @pl.when(step == 0)
    def _():
        wait_whole(wdown, sems.at[0])
        wait_whole(wup, sems.at[1])

    total = jnp.zeros(hidden.shape, f32)
    for c in range(FF // FCHUNK):
        cols = slice(c * FCHUNK, (c + 1) * FCHUNK)
        value, slope = gate_both(inner[:, cols].astype(f32))
        act_low[:, cols] = to_low(value)
        grad = to_low(slope * dot_nt(low, wdown[cols, :]))
        inner_grad[:, cols] = grad
        total = total + dot_nt(grad, wup[:, cols])
    values = hidden[...]
    normed[...] = to_low(rms_scale(values, gains[1:2, :]))
    part, second_gain = norm_back(values, gains[1:2, :], total)
    grad = output_grad + part
    hidden_grad[...] = grad
    low = to_low(grad)
    attn_grad[...] = low

    @pl.when(step == 0)
    def _():
        wait_whole(wout, sems.at[2])

    mixed_grad[...] = to_low(dot_nt(low, wout[...]))
    gain_sums[0:1, :] += second_gain
    gain_sums[1:2, :] += final_gain


def feed_back(output, hidden, inner, upstream, down, up, out, gains):
    total = hidden.shape[0]
    tile = 256
    by_row = lambda p, *_: (p, 0)
    fixed = lambda p, *_: (0, 0)
    row = pl.BlockSpec((tile, D), by_row)
    wide = pl.BlockSpec((tile, FF), by_row)
    return pl.pallas_call(
        feed_back_kernel,
        grid_spec=pltpu.PrefetchScalarGridSpec(
            num_scalar_prefetch=0,
            grid=(total // tile,),
            in_specs=[row, row, wide, row, *[pl.BlockSpec(memory_space=pl.ANY)] * 3, pl.BlockSpec((8, D), fixed)],
            out_specs=[wide, wide, row, row, row, row, row, pl.BlockSpec((8, D), fixed)],
            scratch_shapes=[
                pltpu.VMEM((D, FF), bf16),
                pltpu.VMEM((FF, D), bf16),
                pltpu.VMEM((D, D), bf16),
                pltpu.SemaphoreType.DMA((3,)),
            ],
        ),
        out_shape=[
            jax.ShapeDtypeStruct((total, FF), bf16),
            jax.ShapeDtypeStruct((total, FF), bf16),
            jax.ShapeDtypeStruct((total, D), bf16),
            jax.ShapeDtypeStruct((total, D), bf16),
            jax.ShapeDtypeStruct((total, D), f32),
            jax.ShapeDtypeStruct((total, D), bf16),
            jax.ShapeDtypeStruct((total, D), bf16),
            jax.ShapeDtypeStruct((8, D), f32),
        ],
        compiler_params=pltpu.CompilerParams(vmem_limit_bytes=VMEM_CAP),
        name="feed_back",
    )(output, hidden, inner, upstream, down, up, out, gains)


def attend_back_kernel(
    plan, shard_plan, nbits, rows, lengths, q_ref, k_ref, v_ref, go_ref, lse, strips, buckets, *refs
):
    if plan is None:
        gq_ref, gk_ref, gv_ref, table, bias_sums = refs
    else:
        terms, shard, gq_ref, gk_ref, gv_ref, table, reduced, spread, bias_sums, own, sib, land, *sems = refs
    pair = pl.program_id(0)
    step = pl.program_id(1)
    at = pair * pl.num_programs(1) + step
    total_steps = PAIRS * PASS_EX

    if plan is not None:

        def put(where, total):
            reduced[where, :] = to_low(total)

        begin, steps, end = sum_steps(plan, nbits, rows, terms, put, own, sib, land, sems[:5])
        more, more_end = spread_steps(
            shard_plan, nbits, shard.shape[0], lambda c: shard.at[pl.ds(shard_plan[c][0], shard_plan[c][1])], spread, sems[5:]
        )
        steps = together(steps, more)

        @pl.when(at == 0)
        def _():
            enter_tree(nbits)
            begin()

        cuts = [round(len(steps) * (k / (total_steps - 1)) ** 0.8) for k in range(total_steps)]
        for k in range(1, total_steps):
            some = steps[cuts[k - 1] : cuts[k]]

            @pl.when(at == k)
            def _(some=some):
                for one in some:
                    one()

    @pl.when(step == 0)
    def _():
        bias_sums[...] = jnp.zeros_like(bias_sums)

    length = lengths[step]
    keys = k_ref[...]
    values = v_ref[...]
    turned = keys.T
    lane = lax.broadcasted_iota(jnp.int32, turned.shape, 0)
    halves = [
        jnp.where(lane < HD, turned, jnp.zeros_like(turned)),
        jnp.where(lane >= HD, turned, jnp.zeros_like(turned)),
    ]
    key_grad = jnp.zeros((PASS_SLOT, BLK), f32)
    value_grad = jnp.zeros((PASS_SLOT, BLK), f32)
    query_grad = jnp.zeros((BLK, PASS_SLOT), f32)
    for head in range(2):
        mask = head_lanes(PASS_SLOT, head)
        queries = jnp.where(mask, q_ref[...], jnp.zeros((PASS_SLOT, BLK), bf16))
        grads = jnp.where(mask, go_ref[...], jnp.zeros((PASS_SLOT, BLK), bf16))
        scores = masked_scores(keys, queries, strips.at[head], 0, length)
        probs = jnp.exp(scores - lse[0, pl.ds(2 * pair + head, 1), :])
        prob_grad = dot_nt(values, grads)
        inner = jnp.sum(probs * prob_grad, axis=0, keepdims=True)
        score_grad = to_low(probs * (prob_grad - inner))
        wide = score_grad.astype(f32)
        for m in range(PASS_SLOT // BLK):
            first = (3 - m) * BLK
            bias_sums[head, first : first + PASS_SLOT, :] += wide[:, m * BLK : (m + 1) * BLK]
        value_grad = value_grad + dot(to_low(probs), grads)
        key_grad = key_grad + dot(score_grad, queries)
        query_grad = query_grad + dot(halves[head], score_grad)
    gq_ref[...] = to_low(query_grad.T)
    gk_ref[...] = to_low(key_grad)
    gv_ref[...] = to_low(value_grad)

    @pl.when(step == pl.num_programs(1) - 1)
    def _():
        which = buckets[...]
        lane = lax.broadcasted_iota(jnp.int32, (1, BLK), 1)
        for head in range(2):
            near = bias_sums[head, 2 * BLK : 5 * BLK, :]
            sums = jnp.zeros((1, BLK), f32)
            for b in range(NB):
                part = jnp.sum(jnp.where(which == b, near, 0.0), axis=0, keepdims=True)
                if b % (NB // 2) == NB // 2 - 1:
                    ends = slice(0, 2 * BLK) if b < NB // 2 else slice(5 * BLK, STRIP)
                    part = part + jnp.sum(bias_sums[head, ends, :], axis=0, keepdims=True)
                sums = jnp.where(lane == b, jnp.sum(part, axis=1, keepdims=True), sums)
            table[0, head : head + 1, :] = sums

    if plan is not None:

        @pl.when(at == total_steps - 1)
        def _():
            end()
            more_end()


def attend_back(lengths, qkv, mixed_grad, lse, strips, terms, shard, dp_count, cid):
    count = lengths.shape[0]
    total = count * PASS_SLOT
    block = (PASS_SLOT, BLK)
    place = pl.BlockSpec(block, lambda a, p, *_: (p, a))
    strip = pl.BlockSpec((2, STRIP, BLK), lambda a, p, *_: (a, 0, 0))
    in_specs = [
        place,
        pl.BlockSpec(block, lambda a, p, *_: (p, a + PAIRS)),
        pl.BlockSpec(block, lambda a, p, *_: (p, a + 2 * PAIRS)),
        place,
        pl.BlockSpec((1, 16, PASS_SLOT), lambda a, p, *_: (p, 0, 0)),
        strip,
        pl.BlockSpec((3 * BLK, BLK), lambda *_: (0, 0)),
    ]
    out_specs = [place, place, place, pl.BlockSpec((1, 8, BLK), lambda a, p, *_: (a, 0, 0))]
    out_shape = [jax.ShapeDtypeStruct((total, D), bf16)] * 3 + [jax.ShapeDtypeStruct((PAIRS, 8, BLK), f32)]
    operands = [qkv, qkv, qkv, mixed_grad, lse, strips, jnp.asarray(strip_buckets())]
    scratch = [pltpu.VMEM((2, STRIP, BLK), f32)]
    plan, shard_plan, nbits, rows = None, None, 0, 0
    params = dict(vmem_limit_bytes=VMEM_CAP)
    if dp_count == 16:
        rows = terms.shape[0] // (2 * dp_count)
        nbits = dp_count.bit_length() - 1
        plan = chunk_plan(rows, nbits, "ABCDABAB", (2, 2, 2, 2, 3, 3, 1, 1))
        shard_plan = chunk_plan(shard.shape[0], nbits, "ABCD", (3, 3, 1, 1))
        any_space = pl.BlockSpec(memory_space=pl.ANY)
        in_specs += [any_space, any_space]
        out_specs += [pl.BlockSpec((rows, BLK), lambda a, p, *_: (0, 0)), any_space]
        out_shape += [
            jax.ShapeDtypeStruct((rows, BLK), bf16),
            jax.ShapeDtypeStruct((2 * dp_count * shard.shape[0], BLK), bf16),
        ]
        operands += [terms, shard]
        scratch = scratch + sum_scratch(rows, nbits) + tree_sems(plan, nbits) + tree_sems(shard_plan, nbits)
        params.update(collective_id=cid, has_side_effects=True)
    results = pl.pallas_call(
        functools.partial(attend_back_kernel, plan, shard_plan, nbits, rows),
        grid_spec=pltpu.PrefetchScalarGridSpec(
            num_scalar_prefetch=1,
            grid=(PAIRS, count),
            in_specs=in_specs,
            out_specs=out_specs,
            scratch_shapes=scratch,
        ),
        out_shape=out_shape,
        compiler_params=pltpu.CompilerParams(**params),
        name="attend_back",
    )(lengths, *operands)
    if plan is None:
        return (
            *results,
            lax.psum_scatter(terms, ("dp", "opt"), scatter_dimension=0, tiled=True),
            lax.all_gather(shard, ("dp", "opt"), axis=0, tiled=True),
        )
    return results


def input_back_kernel(
    x_ref, gq, gk, gv, hidden_grad, whole, gains, result, normed, gain_sums, wqkv, sems
):
    step = pl.program_id(0)

    @pl.when(step == 0)
    def _():
        for m in range(3):
            pltpu.make_async_copy(whole.at[m], wqkv.at[m], sems.at[m]).start()
        gain_sums[...] = jnp.zeros_like(gain_sums)

    values = x_ref[...].astype(f32)
    normed[...] = to_low(rms_scale(values, gains[0:1, :]))
    total = jnp.zeros(values.shape, f32)
    for m, grads in enumerate((gq, gk, gv)):

        @pl.when(step == 0)
        def _(m=m):
            wait_whole(wqkv.at[m], sems.at[m])

        total = total + dot_nt(grads[...], wqkv[m])
    part, first_gain = norm_back(values, gains[0:1, :], total)
    result[...] = hidden_grad[...] + part
    gain_sums[0:1, :] += first_gain


def input_back(enc_in, gq, gk, gv, hidden_grad, whole, gains):
    total = enc_in.shape[0]
    tile = 256
    fixed = lambda p, *_: (0, 0)
    row = pl.BlockSpec((tile, D), lambda p, *_: (p, 0))
    return pl.pallas_call(
        input_back_kernel,
        grid_spec=pltpu.PrefetchScalarGridSpec(
            num_scalar_prefetch=0,
            grid=(total // tile,),
            in_specs=[row, row, row, row, row, pl.BlockSpec(memory_space=pl.ANY), pl.BlockSpec((8, D), fixed)],
            out_specs=[row, row, pl.BlockSpec((8, D), fixed)],
            scratch_shapes=[pltpu.VMEM((3, D, D), bf16), pltpu.SemaphoreType.DMA((3,))],
        ),
        out_shape=[
            jax.ShapeDtypeStruct((total, D), f32),
            jax.ShapeDtypeStruct((total, D), bf16),
            jax.ShapeDtypeStruct((8, D), f32),
        ],
        compiler_params=pltpu.CompilerParams(vmem_limit_bytes=VMEM_CAP),
        name="input_back",
    )(enc_in, gq, gk, gv, hidden_grad, whole, gains)


HROWS = H * AROWS
SIDE = D + 2 * BLK


HELD = 16
REST = ALEN - HELD


def pack_rows(sides):
    main = jnp.concatenate([side[:HELD] for side in sides], axis=1)
    width = max(side.shape[1] for side in sides)
    rest = jnp.zeros((HELD, width), f32)
    for k, side in enumerate(sides):
        rows = side[HELD:ALEN].astype(f32)
        if side.shape[1] < width:
            rows = jnp.concatenate([rows, jnp.zeros((REST, width - side.shape[1]), f32)], axis=1)
        above, below = REST * k, HELD - REST * (k + 1)
        rows = [jnp.zeros((above, width), f32)] * (above > 0) + [rows] + [jnp.zeros((below, width), f32)] * (below > 0)
        rest = rest + jnp.concatenate(rows, axis=0)
    return jnp.concatenate([main, to_low(rest)], axis=1)


def spread_heads(rows):
    lane = lax.broadcasted_iota(jnp.int32, rows.shape, 1)
    zero = jnp.zeros_like(rows)
    return jnp.concatenate(
        [jnp.where((lane >= h * HD) & (lane < (h + 1) * HD), rows, zero) for h in range(H)], axis=0
    )


def gather_heads(spread):
    lane = lax.broadcasted_iota(jnp.int32, (AROWS, D), 1)
    total = jnp.zeros((AROWS, D), f32)
    for h in range(H):
        total = jnp.where(
            (lane >= h * HD) & (lane < (h + 1) * HD), spread[h * AROWS : (h + 1) * AROWS], total
        )
    return total


def heads_to_lanes(column):
    lane = lax.broadcasted_iota(jnp.int32, (AROWS, BLK), 1)
    total = jnp.zeros((AROWS, BLK), f32)
    for h in range(H):
        total = jnp.where(lane == h, column[h * AROWS : (h + 1) * AROWS], total)
    return total


def lanes_to_heads(lanes):
    return jnp.concatenate([lanes[:, h : h + 1] for h in range(H)], axis=0)


def lanes_over_heads(lanes):
    lane = lax.broadcasted_iota(jnp.int32, (AROWS, D), 1)
    total = jnp.zeros((AROWS, D), f32)
    for h in range(H):
        total = jnp.where((lane >= h * HD) & (lane < (h + 1) * HD), lanes[:, h : h + 1], total)
    return total


def causal_scores(queries, keys, bias):
    scores = dot_nt(spread_heads(queries), keys) + bias
    row = lax.broadcasted_iota(jnp.int32, scores.shape, 0)
    key_at = lax.broadcasted_iota(jnp.int32, scores.shape, 1)
    return jnp.where(key_at <= row % AROWS, scores, neg_fill)


def self_kernel(rows_ref, dec_ref, near, far, gains, bias, qkv, first, cross, early, wqkv, wout, wcq, sems):
    for m in range(3):
        start_blocks(rows_ref, (near, far), DEC_QKV + 36 * m, D, D, wqkv.at[m], sems.at[m])
    start_blocks(rows_ref, (near, far), DEC_OUT, D, D, wout, sems.at[3])
    start_blocks(rows_ref, (near, far), CROSS_Q, D, D, wcq, sems.at[4])
    values = dec_ref[...].astype(f32)
    low = normed = to_low(rms_scale(values, gains[3:4, :]))
    for m in range(3):
        wait_whole(wqkv.at[m], sems.at[m])
        qkv[:, m * D : (m + 1) * D] = to_low(dot(low, wqkv[m]))
    scores = causal_scores(qkv[:, 0:D], qkv[:, D : 2 * D], bias[...])
    peak = jnp.max(scores, axis=1, keepdims=True)
    expos = jnp.exp(scores - peak)
    probs = to_low(expos / jnp.sum(expos, axis=1, keepdims=True))
    heads = to_low(gather_heads(dot(probs, qkv[:, 2 * D : 3 * D])))
    wait_whole(wout, sems.at[3])
    after = values + dot(heads, wout[...])
    first[...] = after
    low = to_low(rms_scale(after, gains[4:5, :]))
    wait_whole(wcq, sems.at[4])
    cross[...] = to_low(dot(low, wcq[...]))
    early[...] = pack_rows((normed, heads, low))


def whole_spec(shape):
    return pl.BlockSpec(shape, lambda *_: (0,) * len(shape))


def decoder_call(body, name, rows, ins, outs, scratch):
    specs = [pl.BlockSpec(memory_space=pl.ANY) if x.shape[0] > 8192 else whole_spec(x.shape) for x in ins]
    return pl.pallas_call(
        body,
        grid_spec=pltpu.PrefetchScalarGridSpec(
            num_scalar_prefetch=1,
            grid=(1,),
            in_specs=specs,
            out_specs=[whole_spec(shape) for shape, kind in outs],
            scratch_shapes=scratch,
        ),
        out_shape=[jax.ShapeDtypeStruct(shape, kind) for shape, kind in outs],
        compiler_params=pltpu.CompilerParams(vmem_limit_bytes=VMEM_CAP),
        name=name,
    )(rows, *ins)


def decoder_self(rows, dec_rows, gathered, gains, bias):
    low, full = ((AROWS, D), bf16), ((AROWS, D), f32)
    square = pltpu.VMEM((D, D), bf16)
    return decoder_call(
        self_kernel, "decoder_self", rows, (dec_rows, *gathered, gains, bias),
        [((AROWS, 3 * D), bf16), full, low, ((HELD, 4 * D), bf16)],
        [pltpu.VMEM((3, D, D), bf16), square, square, pltpu.SemaphoreType.DMA((5,))],
    )


def memory_kernel(rows_ref, encoded, near, far, memory, wkv, sems):
    step = pl.program_id(0)

    @pl.when(step == 0)
    def _():
        for m in range(2):
            start_blocks(rows_ref, (near, far), CROSS_KV + 36 * m, D, D, wkv.at[m], sems.at[m])

    for m in range(2):

        @pl.when(step == 0)
        def _(m=m):
            wait_whole(wkv.at[m], sems.at[m])

        memory[:, m * D : (m + 1) * D] = to_low(dot(encoded[...], wkv[m]))


def cross_memory(rows, encoded, gathered):
    total = encoded.shape[0]
    return pl.pallas_call(
        memory_kernel,
        grid_spec=pltpu.PrefetchScalarGridSpec(
            num_scalar_prefetch=1,
            grid=(total // PASS_SLOT,),
            in_specs=[pl.BlockSpec((PASS_SLOT, D), lambda p, *_: (p, 0)), *[pl.BlockSpec(memory_space=pl.ANY)] * 2],
            out_specs=pl.BlockSpec((PASS_SLOT, 2 * D), lambda p, *_: (p, 0)),
            scratch_shapes=[pltpu.VMEM((2, D, D), bf16), pltpu.SemaphoreType.DMA((2,))],
        ),
        out_shape=jax.ShapeDtypeStruct((total, 2 * D), bf16),
        compiler_params=pltpu.CompilerParams(vmem_limit_bytes=VMEM_CAP),
        name="cross_memory",
    )(rows, encoded, *gathered)


def cross_kernel(lengths, offsets, queries, memory, result):
    length = lengths[pl.program_id(0)]
    scores = dot_nt(spread_heads(queries[0]), memory[:, 0:D])
    key_at = lax.broadcasted_iota(jnp.int32, scores.shape, 1)
    scores = jnp.where(key_at < length, scores, neg_fill)
    peak = jnp.max(scores, axis=1, keepdims=True)
    expos = jnp.exp(scores - peak)
    result[0, :, 0:D] = gather_heads(dot(to_low(expos), memory[:, D : 2 * D]))
    result[0, :, D : D + BLK] = heads_to_lanes(peak)
    result[0, :, D + BLK :] = heads_to_lanes(jnp.sum(expos, axis=1, keepdims=True))


def cross_attend(lengths, offsets, queries, memory):
    count = lengths.shape[0]
    at_offset = lambda p, lens, offs: (offs[p], 0, 0)
    return pl.pallas_call(
        cross_kernel,
        grid_spec=pltpu.PrefetchScalarGridSpec(
            num_scalar_prefetch=2,
            grid=(count,),
            in_specs=[
                pl.BlockSpec((1, AROWS, D), at_offset),
                pl.BlockSpec((PASS_SLOT, 2 * D), lambda p, *_: (p, 0)),
            ],
            out_specs=pl.BlockSpec((1, AROWS, SIDE), at_offset),
        ),
        out_shape=jax.ShapeDtypeStruct((count, AROWS, SIDE), f32),
        compiler_params=pltpu.CompilerParams(vmem_limit_bytes=VMEM_CAP),
        name="cross_attend",
    )(lengths, offsets, queries, memory)


def feed_decoder_kernel(
    rows_ref, parts, first, dec_cot, valid, early, near, far, gains,
    result, middle, back, second_grad, gain_sums, wout, wup, wdown, sems,
):
    start_blocks(rows_ref, (near, far), CROSS_OUT, D, D, wout, sems.at[0])
    start_blocks(rows_ref, (near, far), DEC_UP, D, FF, wup, sems.at[1])
    start_blocks(rows_ref, (near, far), DEC_DOWN, FF, D, wdown, sems.at[2])
    peaks = [parts[k, :, D : D + BLK] for k in range(PASS_EX)]
    peak = functools.reduce(jnp.maximum, peaks)
    scales = [jnp.exp(one - peak) for one in peaks]
    total = sum(parts[k, :, D + BLK :] * scales[k] for k in range(PASS_EX))
    lane = lax.broadcasted_iota(jnp.int32, total.shape, 1)
    total = jnp.where(lane < H, total, 1.0)
    heads = sum(parts[k, :, 0:D] * lanes_over_heads(scales[k] / total) for k in range(PASS_EX))
    low = mixed = to_low(heads)
    wait_whole(wout, sems.at[0])
    second = first[...] + dot(low, wout[...])
    low = to_low(rms_scale(second, gains[5:6, :]))
    output_grad = dec_cot[...].astype(f32) * valid[:, 0:1]
    grad_low = to_low(output_grad)
    acts, inner_grads = [], []
    wait_whole(wup, sems.at[1])
    wait_whole(wdown, sems.at[2])
    after = second
    back_sum = jnp.zeros((AROWS, D), f32)
    for c in range(FF // D):
        cols = slice(c * D, (c + 1) * D)
        value, slope = gate_both(dot(low, wup[:, cols]))
        value = to_low(value)
        acts.append(value)
        after = after + dot(value, wdown[cols, :])
        grad = to_low(slope * dot_nt(grad_low, wdown[cols, :]))
        inner_grads.append(grad)
        back_sum = back_sum + dot_nt(grad, wup[:, cols])
    result[...] = to_low(after)
    part, gain_grad = norm_back(second, gains[5:6, :], back_sum)
    grad = output_grad + part
    second_grad[...] = grad
    gain_sums[...] = jnp.broadcast_to(gain_grad, gain_sums.shape)
    normed, low = low, to_low(grad)
    middle[:, : 17 * D] = pack_rows(
        (
            jnp.concatenate([normed] + inner_grads, axis=1),
            jnp.concatenate(acts + [grad_low], axis=1),
            jnp.concatenate([mixed, low], axis=1),
        )
    )
    middle[:, 17 * D :] = early[...]
    head_grad = to_low(dot_nt(low, wout[...])).astype(f32)
    back[:, 0:D] = head_grad
    back[:, D : D + BLK] = peak + jnp.log(total)
    product = head_grad * heads
    at = lax.broadcasted_iota(jnp.int32, (AROWS, D), 1)
    inner = jnp.zeros((AROWS, BLK), f32)
    for h in range(H):
        one = jnp.where((at >= h * HD) & (at < (h + 1) * HD), product, 0.0)
        inner = jnp.where(lane == h, jnp.sum(one, axis=1, keepdims=True), inner)
    back[:, D + BLK :] = inner


def decoder_feed(rows, parts, first, dec_cot, valid, early, gathered, gains):
    low, full = ((AROWS, D), bf16), ((AROWS, D), f32)
    return decoder_call(
        feed_decoder_kernel, "decoder_feed", rows, (parts, first, dec_cot, valid, early, *gathered, gains),
        [low, ((HELD, 21 * D), bf16), ((AROWS, SIDE), f32), full, ((8, D), f32)],
        [pltpu.VMEM((D, D), bf16), pltpu.VMEM((D, FF), bf16), pltpu.VMEM((FF, D), bf16), pltpu.SemaphoreType.DMA((3,))],
    )


def cross_back_kernel(
    rows_ref, lengths, offsets, queries, back, memory, enc_cot, near, far,
    memory_grad, query_grad, upstream, wkv, sems,
):
    step = pl.program_id(0)

    @pl.when(step == 0)
    def _():
        for m in range(2):
            start_blocks(rows_ref, (near, far), CROSS_KV + 36 * m, D, D, wkv.at[m], sems.at[m])

    length = lengths[step]
    spread = spread_heads(queries[0])
    grads = spread_heads(to_low(back[0, :, 0:D]))
    keys = memory[:, 0:D]
    scores = dot_nt(spread, keys)
    key_at = lax.broadcasted_iota(jnp.int32, scores.shape, 1)
    scores = jnp.where(key_at < length, scores, neg_fill)
    probs = jnp.exp(scores - lanes_to_heads(back[0, :, D : D + BLK]))
    prob_grad = dot_nt(grads, memory[:, D : 2 * D])
    score_grad = to_low(probs * (prob_grad - lanes_to_heads(back[0, :, D + BLK :])))
    query_grad[0] = gather_heads(dot(score_grad, keys))
    key_low = to_low(dot_tn(score_grad, spread))
    value_low = to_low(dot_tn(to_low(probs), grads))
    memory_grad[:, 0:D] = key_low
    memory_grad[:, D : 2 * D] = value_low

    @pl.when(step == 0)
    def _():
        for m in range(2):
            wait_whole(wkv.at[m], sems.at[m])

    total = to_low(dot_nt(key_low, wkv[0]) + dot_nt(value_low, wkv[1])).astype(f32)
    row = lax.broadcasted_iota(jnp.int32, total.shape, 0)
    upstream[...] = total + jnp.where(row < length, enc_cot[...].astype(f32), 0.0)


def cross_back(rows, lengths, offsets, queries, back, memory, enc_cot, gathered):
    count = lengths.shape[0]
    total = count * PASS_SLOT
    at_offset = lambda p, rows, lens, offs: (offs[p], 0, 0)
    by_row = lambda p, *_: (p, 0)
    return pl.pallas_call(
        cross_back_kernel,
        grid_spec=pltpu.PrefetchScalarGridSpec(
            num_scalar_prefetch=3,
            grid=(count,),
            in_specs=[
                pl.BlockSpec((1, AROWS, D), at_offset),
                pl.BlockSpec((1, AROWS, SIDE), at_offset),
                pl.BlockSpec((PASS_SLOT, 2 * D), by_row),
                pl.BlockSpec((PASS_SLOT, D), by_row),
                *[pl.BlockSpec(memory_space=pl.ANY)] * 2,
            ],
            out_specs=[
                pl.BlockSpec((PASS_SLOT, 2 * D), by_row),
                pl.BlockSpec((1, AROWS, D), at_offset),
                pl.BlockSpec((PASS_SLOT, D), by_row),
            ],
            scratch_shapes=[pltpu.VMEM((2, D, D), bf16), pltpu.SemaphoreType.DMA((2,))],
        ),
        out_shape=[
            jax.ShapeDtypeStruct((total, 2 * D), bf16),
            jax.ShapeDtypeStruct((count, AROWS, D), f32),
            jax.ShapeDtypeStruct((total, D), f32),
        ],
        compiler_params=pltpu.CompilerParams(vmem_limit_bytes=VMEM_CAP),
        name="cross_back",
    )(rows, lengths, offsets, queries, back, memory, enc_cot, *gathered)


def self_back_kernel(
    rows_ref, part_zero, part_one, part_two, second_grad, first, dec_ref, qkv, near, far, gains, bias,
    result, late, score_grads, gain_sums, wqkv, wout, wcq, sems,
):
    start_blocks(rows_ref, (near, far), CROSS_Q, D, D, wcq, sems.at[4])
    start_blocks(rows_ref, (near, far), DEC_OUT, D, D, wout, sems.at[3])
    for m in range(3):
        start_blocks(rows_ref, (near, far), DEC_QKV + 36 * m, D, D, wqkv.at[m], sems.at[m])
    low = cross_grad = to_low(part_zero[...] + part_one[...] + part_two[...])
    wait_whole(wcq, sems.at[4])
    part, second_gain = norm_back(first[...], gains[4:5, :], dot_nt(low, wcq[...]))
    first_grad = second_grad[...] + part
    low = out_grad = to_low(first_grad)
    wait_whole(wout, sems.at[3])
    heads_grad = spread_heads(to_low(dot_nt(low, wout[...])))
    queries = qkv[:, 0:D]
    keys = qkv[:, D : 2 * D]
    scores = causal_scores(queries, keys, bias[...])
    peak = jnp.max(scores, axis=1, keepdims=True)
    expos = jnp.exp(scores - peak)
    probs = expos / jnp.sum(expos, axis=1, keepdims=True)
    prob_grad = dot_nt(heads_grad, qkv[:, 2 * D : 3 * D])
    inner = jnp.sum(probs * prob_grad, axis=1, keepdims=True)
    score_grad = to_low(probs * (prob_grad - inner))
    score_grads[...] = score_grad.astype(f32)
    grads = (
        gather_heads(dot(score_grad, keys)),
        dot_tn(score_grad, spread_heads(queries)),
        dot_tn(to_low(probs), heads_grad),
    )
    total = jnp.zeros((AROWS, D), f32)
    lows = [to_low(grad) for grad in grads]
    packed = pack_rows((jnp.concatenate(lows, axis=1), out_grad, cross_grad))
    for j in range(LATE_COLS):
        late[j * HELD : (j + 1) * HELD, :] = packed[:, j * BLK : (j + 1) * BLK]
    for m in range(3):
        low = lows[m]
        wait_whole(wqkv.at[m], sems.at[m])
        total = total + dot_nt(low, wqkv[m])
    part, first_gain = norm_back(dec_ref[...].astype(f32), gains[3:4, :], total)
    result[...] = first_grad + part
    gain_sums[0:1, :] = first_gain
    gain_sums[1:2, :] = second_gain


LATE_COLS = 8 * D // BLK


def decoder_self_back(rows, parts, second_grad, first, dec_rows, qkv, gathered, gains, bias):
    full = ((AROWS, D), f32)
    square = pltpu.VMEM((D, D), bf16)
    return decoder_call(
        self_back_kernel, "decoder_self_back", rows,
        (*parts, second_grad, first, dec_rows, qkv, *gathered, gains, bias),
        [full, ((LATE_COLS * HELD, BLK), bf16), ((HROWS, AROWS), f32), ((8, D), f32)],
        [pltpu.VMEM((3, D, D), bf16), square, square, pltpu.SemaphoreType.DMA((5,))],
    )


def shift_kernel(way, apart, source, got, ssem, rsem, lsem):
    size = lax.axis_size("dp")
    me = lax.axis_index("dp")
    core = lax.axis_index("opt")
    bar = pltpu.get_barrier_semaphore()
    for k in (1, 2):
        pl.semaphore_signal(bar, inc=1, device_id=((me - way * k + size) % size, core), device_id_type=MESH)
    own = pltpu.make_async_copy(source.at[0] if apart else source, got.at[0], lsem.at[0])
    own.start()
    pl.semaphore_wait(bar, 2)
    copies = [
        pltpu.make_async_remote_copy(
            src_ref=source.at[k] if apart else source, dst_ref=got.at[k], send_sem=ssem.at[k - 1], recv_sem=rsem.at[k - 1],
            device_id=((me + way * k + size) % size, core), device_id_type=MESH,
        )
        for k in (1, 2)
    ]
    for copy in copies:
        copy.start()
    own.wait()
    for copy in copies:
        copy.wait()


def shifted(source, way, apart, cid):
    shape = source.shape if apart else (PASS_EX,) + source.shape
    vmem = pl.BlockSpec(memory_space=pltpu.VMEM)
    return pl.pallas_call(
        functools.partial(shift_kernel, way, apart),
        in_specs=[vmem],
        out_specs=vmem,
        out_shape=jax.ShapeDtypeStruct(shape, source.dtype),
        scratch_shapes=[
            pltpu.SemaphoreType.DMA((2,)),
            pltpu.SemaphoreType.DMA((2,)),
            pltpu.SemaphoreType.DMA((1,)),
        ],
        compiler_params=pltpu.CompilerParams(collective_id=cid, has_side_effects=True),
        name="shift_rows",
    )(source)


def passed_along(values, by):
    size = lax.axis_size("dp")
    return lax.ppermute(values, "dp", [(i, (i + by) % size) for i in range(size)])


SQUARE = D * D // BLK
GROUP_ONE = 2 * D * FF // BLK + 3 * SQUARE
SMALL_ROWS = 512
GROUP_TWO = 3 * SQUARE + SMALL_ROWS


def put_blocks(out_ref, values, at=0):
    down, across = values.shape[0] // BLK, values.shape[1] // BLK
    for i in range(down):
        for j in range(across):
            out_ref[pl.ds(at + (i * across + j) * BLK, BLK), :] = to_low(
                values[i * BLK : (i + 1) * BLK, j * BLK : (j + 1) * BLK]
            )


def square_weight_kernel(columns, products, *refs):
    count = len(columns)
    sources, (out_ref, held, sems) = refs[:count], refs[count:]
    step = pl.program_id(0)

    def fetch(k):
        return pltpu.make_async_copy(sources[k].at[:, pl.ds(columns[k], D)], held.at[k], sems.at[k])

    @pl.when(step == 0)
    def _():
        for k in range(count):
            fetch(k).start()

    seen = set()
    for m, (a, b) in enumerate(products):
        fresh = [k for k in (a, b) if k not in seen]
        seen.update(fresh)

        @pl.when(step == m)
        def _(a=a, b=b, fresh=fresh):
            for k in fresh:
                fetch(k).wait()
            put_blocks(out_ref, dot_tn(held[a], held[b]))


def square_weight(operands, products, total):
    any_space = pl.BlockSpec(memory_space=pl.ANY)
    arrays = [array for array, _ in operands]
    columns = [col for _, col in operands]
    count = arrays[0].shape[0]
    return pl.pallas_call(
        functools.partial(square_weight_kernel, columns, products),
        grid=(len(products),),
        in_specs=[any_space] * len(arrays),
        out_specs=pl.BlockSpec((SQUARE, BLK), lambda p: (p, 0)),
        scratch_shapes=[pltpu.VMEM((len(arrays), count, D), bf16), pltpu.SemaphoreType.DMA((len(arrays),))],
        out_shape=jax.ShapeDtypeStruct((total, BLK), bf16),
        compiler_params=pltpu.CompilerParams(vmem_limit_bytes=VMEM_CAP),
        name="square_weight",
    )(*arrays)


def block_table():
    table = np.zeros((1009, 8), np.int32)
    wide = D // BLK
    early, late = 20 * wide, 5 * wide
    rows = (
        (DEC_QKV, 108, 1, 17 * wide, 0, early, late, 0),
        (DEC_OUT, 36, 1, 18 * wide, 3 * wide, early, late, 1),
        (CROSS_Q, 36, 1, 19 * wide, 4 * wide, early, late, 2),
        (DEC_UP, 144, 4, 0, wide, 12 * wide, 13 * wide, 0),
        (DEC_DOWN, 144, 4, 5 * wide, 9 * wide, 12 * wide, 16 * wide, 1),
        (CROSS_OUT, 36, 4, 10 * wide, 11 * wide, 12 * wide, 13 * wide, 2),
    )
    for first, count, kind, left, right, rest_left, rest_right, group in rows:
        for b in range(count):
            if first == DEC_QKV:
                m, k = divmod(b, 36)
                i, j = divmod(k, wide)
                j = j + wide * m
            else:
                i, j = divmod(b, 4 * wide if first == DEC_UP else wide)
            table[first + b] = (kind, 0, left + i, right + j, rest_left + i, rest_right + j, group, 0)
    for first, count, at in ((ENC_DOWN, 144, 144), (CROSS_KV, 72, 288), (ENC_OUT, 36, 360)):
        for b in range(count):
            table[first + b, :2] = (2, at + b)
    for b in range(144):
        i, j = divmod(b, 4 * wide)
        table[ENC_UP + b, :2] = (2, j // wide * 36 + i * wide + j % wide)
    for b in range(108):
        table[b, :2] = (3, b)
    return table


def update_kernel(
    slots, info, middle, late, one, two, master, stats, roots,
    grads, new_stats, new_master, sides, held, summed, sems,
):
    step = pl.program_id(0)
    steps = pl.num_programs(0)

    def each(step, action):
        buffer = lax.rem(step, 2)
        for s in range(slots):
            at = (step * slots + s) * 8
            kind = info[at]

            def copy(source, dest, k, s=s):
                return pltpu.make_async_copy(source, dest, sems.at[buffer, s, k])

            def rows_of(left, right, s=s, at=at, copy=copy):
                for k, source in enumerate((left, right, left, right)):
                    col = info[at + 2 + k]
                    if source is late:
                        part = source.at[:, pl.ds(pl.multiple_of(col * HELD, HELD), HELD)]
                    else:
                        part = source.at[:, :, pl.ds(pl.multiple_of(col * BLK, BLK), BLK)]
                    action(copy(part, sides.at[buffer, s, k], k))

            def block_of(source, s=s, at=at, copy=copy):
                row = pl.multiple_of(info[at + 1] * BLK, BLK)
                action(copy(source.at[pl.ds(row, BLK)], held.at[buffer, s], 4))

            pl.when(kind == 1)(functools.partial(rows_of, middle, late))
            pl.when(kind == 4)(functools.partial(rows_of, middle, middle))
            pl.when(kind == 2)(functools.partial(block_of, one))
            pl.when(kind == 3)(functools.partial(block_of, two))

    @pl.when(step == 0)
    def _():
        each(step, lambda copy: copy.start())

    @pl.when(step + 1 < steps)
    def _():
        each(step + 1, lambda copy: copy.start())

    each(step, lambda copy: copy.wait())
    buffer = lax.rem(step, 2)
    for s in range(slots):
        at = (step * slots + s) * 8
        kind = info[at]
        group = info[at + 6]

        @pl.when((kind == 1) | (kind == 4))
        def _(s=s, group=group):
            left, right, rest, rest_right = [sides[buffer, s, k].reshape(-1, BLK) for k in range(4)]
            row = lax.broadcasted_iota(jnp.int32, rest.shape, 0)
            mine = jnp.where(row % HELD // REST == group, rest, jnp.zeros_like(rest))
            summed[s] = dot_tn(left, right) + dot_tn(mine, rest_right)

        @pl.when((kind == 2) | (kind == 3))
        def _(s=s):
            summed[s] = held[buffer, s].astype(f32)

        @pl.when(kind == 0)
        def _(s=s):
            summed[s] = jnp.zeros((BLK, BLK), f32)

    for s in range(slots):
        grad = summed[s]
        low = to_low(grad)
        grads[s] = grad
        new_stats[s, 0] = stat_decay * stats[s, 0] + (1.0 - stat_decay) * dot_nt(low, low)
        new_stats[s, 1] = stat_decay * stats[s, 1] + (1.0 - stat_decay) * dot_tn(low, low)
        shaped = dot(to_low(roots[s, 0]), low)
        shaped = dot(to_low(shaped), to_low(roots[s, 1]))
        old = master[s]
        shaped_rms = jnp.sqrt(jnp.mean(shaped * shaped) + 1e-06)
        weight_rms = jnp.sqrt(jnp.mean(old * old) + 1e-06)
        new_master[s] = old - (block_rate * weight_rms / shaped_rms) * shaped


def update_blocks(info, middle, late, one, two, master, kron_stats, inverse_roots):
    count = master.shape[0]
    slots = min(4, count)
    devices = late.shape[0]
    any_space = pl.BlockSpec(memory_space=pl.ANY)
    block = pl.BlockSpec((slots, BLK, BLK), lambda p, *_: (p, 0, 0))
    pair = pl.BlockSpec((slots, 2, BLK, BLK), lambda p, *_: (p, 0, 0, 0))
    return pl.pallas_call(
        functools.partial(update_kernel, slots),
        grid_spec=pltpu.PrefetchScalarGridSpec(
            num_scalar_prefetch=1,
            grid=(count // slots,),
            in_specs=[any_space] * 4 + [block, pair, pair],
            out_specs=[block, pair, block],
            scratch_shapes=[
                pltpu.VMEM((2, slots, 4, devices, HELD, BLK), bf16),
                pltpu.VMEM((2, slots, BLK, BLK), bf16),
                pltpu.VMEM((slots, BLK, BLK), f32),
                pltpu.SemaphoreType.DMA((2, slots, 5)),
            ],
        ),
        out_shape=[
            jax.ShapeDtypeStruct(master.shape, f32),
            jax.ShapeDtypeStruct(kron_stats.shape, f32),
            jax.ShapeDtypeStruct(master.shape, f32),
        ],
        compiler_params=pltpu.CompilerParams(vmem_limit_bytes=VMEM_CAP),
        name="update_blocks",
    )(info, middle, late, one, two, master, kron_stats, inverse_roots)


def order_kernel(order, master, small, near, far, held, sems):
    count = held.shape[0]
    for s in range(count):
        pltpu.make_async_copy(master.at[order[s]], held.at[s], sems.at[s]).start()
    near[0:EXTRA, :] = small[...]
    first = near.shape[0]
    for s in range(count):
        pltpu.make_async_copy(master.at[order[s]], held.at[s], sems.at[s]).wait()
        at = EXTRA + s * BLK
        if at < first:
            near[at : at + BLK, :] = to_low(held[s])
        else:
            far[at - first : at - first + BLK, :] = to_low(held[s])


def ordered_shards(order, master, small, near_rows):
    count = master.shape[0]
    shapes = [(near_rows, BLK), (max(EXTRA + count * BLK - near_rows, EXTRA), BLK)]
    return pl.pallas_call(
        order_kernel,
        grid_spec=pltpu.PrefetchScalarGridSpec(
            num_scalar_prefetch=1,
            grid=(1,),
            in_specs=[pl.BlockSpec(memory_space=pl.ANY), whole_spec(small.shape)],
            out_specs=[whole_spec(shape) for shape in shapes],
            scratch_shapes=[pltpu.VMEM((count, BLK, BLK), f32), pltpu.SemaphoreType.DMA((count,))],
        ),
        out_shape=[jax.ShapeDtypeStruct(shape, bf16) for shape in shapes],
        name="ordered_shards",
    )(order, master, small)


def total_all(terms, dp_count):
    if dp_count == 16:
        return total_rows_all(terms, dp_count, 1)
    return lax.psum(terms, ("dp", "opt"))


def gather_low(rows):
    return lax.all_gather(rows, ("dp", "opt"), axis=0, tiled=True)


def pad_rows(array, rows):
    return jnp.pad(array, ((0, rows - array.shape[0]),) + ((0, 0),) * (array.ndim - 1))


def per_device(
    enc_in,
    enc_cot,
    dec_in,
    dec_cot,
    passage_lengths,
    passage_example,
    answer_tokens,
    owner_slot,
    master,
    kron_stats,
    inverse_roots,
    small_params,
    small_moment,
):
    dp_count = lax.axis_size("dp")
    pair_count = lax.axis_size("opt")
    devices = dp_count * pair_count
    slot_dev = master.shape[0]
    small_dev = small_params.shape[0]
    dev_rows = slot_dev * BLK + EXTRA
    table_size = NB * H
    device = lax.axis_index("dp") * pair_count + lax.axis_index("opt")

    kinds = jnp.asarray((np.arange(owner_slot.shape[0]) >= DEC_QKV).astype(np.int32))
    owners, local = owner_slot // slot_dev, owner_slot % slot_dev
    keys = (owners * 4 + kinds) * slot_dev + local
    before = (keys[None, :] < keys[:, None]) & (owners[None, :] == owners[:, None])
    rank = jnp.sum(before.astype(jnp.int32), axis=1)
    split = dp_count == 16 and slot_dev > EARLY_SLOTS
    near_slots = EARLY_SLOTS if split else slot_dev
    near_rows, far_rows = EXTRA + near_slots * BLK, (slot_dev - near_slots) * BLK
    rows = jnp.where(
        rank < near_slots,
        owners * near_rows + EXTRA + rank * BLK,
        -1 - (owners * far_rows + (rank - near_slots) * BLK),
    ).astype(jnp.int32)
    mine = owner_slot[None, :] == (device * slot_dev + jnp.arange(slot_dev))[:, None]
    block_at = jnp.sum(jnp.where(mine, jnp.arange(owner_slot.shape[0])[None, :] + 1, 0), axis=1)
    own_kind = 2 - jnp.sum(jnp.where(mine, 2 - kinds[None, :], 0), axis=1)
    own_keys = own_kind * slot_dev + jnp.arange(slot_dev)
    own_rank = jnp.sum((own_keys[None, :] < own_keys[:, None]).astype(jnp.int32), axis=1)
    order = jnp.sum(
        jnp.where(own_rank[None, :] == jnp.arange(slot_dev)[:, None], jnp.arange(slot_dev)[None, :], 0), axis=1
    ).astype(jnp.int32)

    padded = jnp.pad(to_low(small_params), (0, EXTRA * BLK - small_dev)).reshape(EXTRA, BLK)
    near, later = ordered_shards(order, master, padded, near_rows)
    if split:
        near = gather_rows(near, near_rows, dp_count, 0)
        later, near = lax.optimization_barrier((later, near))
        far = gather_low(later)
    else:
        near = far = gather_low(near)
    small_all = near.reshape(devices, near_rows, BLK)[:, :EXTRA]
    small_all = small_all.reshape(devices, EXTRA * BLK)[:, :small_dev].reshape(-1).astype(f32)
    gains = pad_rows(small_all[: 6 * D].reshape(6, D), 8)
    strips = bias_strips(small_all[6 * D : 6 * D + table_size])

    def encoder(rows, gathered):
        qkv, log_total, mixed, hidden, whole = encoder_attend(rows, passage_lengths, enc_in, gathered, gains, strips)
        inner, output, encoded, up, down = encoder_feed(rows, hidden, gathered, gains)
        return qkv, log_total, mixed, hidden, whole, inner, output, encoded, up, down

    gathered = (near, far)
    if split:
        state = encoder(jnp.maximum(rows, 0), (near, near))
        far, state = lax.optimization_barrier((far, state))
        gathered = (near, far)
        late_blocks = jnp.any((kinds == 0) & (rank >= near_slots))

        def again(carry):
            count, fresh_rows = lax.optimization_barrier((carry[0], rows))
            return count + 1, encoder(fresh_rows, gathered)

        _, state = lax.while_loop(
            lambda carry: carry[0] < late_blocks.astype(jnp.int32), again, (jnp.int32(0), state)
        )
    else:
        state = encoder(rows, gathered)
    qkv, log_total, mixed, hidden, whole, inner, output, encoded, up, down = state
    answer_at = np.arange(AROWS)
    dec_buckets = bucket_of(np.minimum(answer_at, ALEN - 1)[None, :] - np.minimum(answer_at, ALEN - 1)[:, None], False)
    dec_onehot = jnp.asarray((dec_buckets[..., None] == np.arange(NB)).reshape(-1, NB).astype(np.float32))
    dec_bias = jnp.dot(
        small_all[6 * D + table_size :].reshape(NB, H).T, dec_onehot.T, precision=exact_prec, preferred_element_type=f32
    ).reshape(HROWS, AROWS)

    dec_rows, encoded = lax.optimization_barrier((pad_rows(dec_in, AROWS), encoded))
    dec_qkv, first, cross_queries, early = decoder_self(rows, dec_rows, gathered, gains, dec_bias)
    moved = [passed_along(cross_queries, k) for k in (1, 2)]
    memory = cross_memory(rows, encoded, gathered)
    moved, memory = lax.optimization_barrier((moved, memory))
    queries = jnp.stack([cross_queries] + moved)
    owner_dp = passage_example // EX_DEV // pair_count
    offsets = ((lax.axis_index("dp") - owner_dp) % dp_count).astype(jnp.int32)

    parts = cross_attend(passage_lengths, offsets, queries, memory)
    parts = shifted(parts, -1, True, 3)
    valid = (pad_rows(answer_tokens.reshape(ALEN, 1), AROWS) != 0).astype(f32)
    dec_out, middle, back, second_grad, gain_six = decoder_feed(
        rows, parts, first, pad_rows(dec_cot, AROWS), jnp.broadcast_to(valid, (AROWS, BLK)), early, gathered, gains
    )
    middle, back = lax.optimization_barrier((middle, back))
    middle = gather_low(middle)
    memory_grad, query_parts, upstream = cross_back(
        rows, passage_lengths, offsets, queries, shifted(back, 1, False, 4), memory, enc_cot, gathered
    )
    query_parts = [query_parts[0]] + [passed_along(query_parts[k], -k) for k in (1, 2)]

    act, inner_grad, branch, normed_two, hidden_grad, attn_grad, mixed_grad, gain_two = feed_back(
        output, hidden, inner, upstream, down, up, whole, gains
    )
    query_parts, inner_grad = lax.optimization_barrier((query_parts, inner_grad))
    dec_in_grad, late, dec_scores, gain_four = decoder_self_back(
        rows, query_parts, second_grad, first, dec_rows, dec_qkv, gathered, gains, dec_bias
    )
    one = square_weight(
        [(normed_two, 0)] + [(inner_grad, k * D) for k in range(4)]
        + [(branch, 0)] + [(act, k * D) for k in range(4)]
        + [(encoded, 0), (memory_grad, 0), (memory_grad, D), (mixed, 0), (attn_grad, 0)],
        [(0, 1 + k) for k in range(4)] + [(6 + k, 5) for k in range(4)] + [(10, 11), (10, 12), (13, 14)],
        GROUP_ONE,
    )
    grad_query, grad_key, grad_value, enc_table, one, late = attend_back(
        passage_lengths, qkv, mixed_grad, log_total, strips, one, late, dp_count, 6
    )
    one, middle = lax.optimization_barrier((one, middle))
    one = gather_low(one)
    enc_in_grad, normed, gain_one = input_back(
        enc_in, grad_query, grad_key, grad_value, hidden_grad, whole, gains
    )
    two = square_weight(
        [(normed, 0), (grad_query, 0), (grad_key, 0), (grad_value, 0)], [(0, 1), (0, 2), (0, 3)], GROUP_TWO
    )

    enc_table = enc_table[:, :2, :NB].reshape(H, NB).T
    dec_table = jnp.dot(
        dec_scores.reshape(H, AROWS * AROWS), dec_onehot, precision=exact_prec, preferred_element_type=f32
    ).T
    small_terms = jnp.concatenate(
        [gain_one[0], gain_two[0], gain_two[1], gain_four[0], gain_four[1], gain_six[0], enc_table.reshape(-1), dec_table.reshape(-1)]
    )
    small_rows = pad_rows(to_low(small_terms).reshape(-1, BLK), SMALL_ROWS)
    two = total_all(lax.dynamic_update_slice(two, small_rows, (3 * SQUARE, 0)), dp_count)

    small_grads = lax.dynamic_slice(two[3 * SQUARE :].reshape(-1), (device * small_dev,), (small_dev,)).astype(f32)
    info = jnp.asarray(np.roll(block_table(), 1, axis=0))[block_at].reshape(-1)
    middle, late = (part.reshape(devices, -1, part.shape[1]) for part in (middle, late))
    block_grads, new_stats, new_master = update_blocks(info, middle, late, one, two, master, kron_stats, inverse_roots)
    new_moment = moment_decay * small_moment + small_grads
    new_small = small_params - small_rate * new_moment
    return (
        dec_out[:ALEN],
        encoded,
        enc_in_grad,
        dec_in_grad[:ALEN],
        block_grads,
        new_stats,
        new_master,
        small_grads,
        new_moment,
        new_small,
    )


def solution(mesh):
    placed = (
        P(("dp", "opt"), None),
        P(("dp", "opt"), None),
        P(("dp", "opt"), None),
        P(("dp", "opt"), None),
        P(("dp", "opt")),
        P(("dp", "opt")),
        P(("dp", "opt"), None),
        P(),
        P(("dp", "opt"), None, None),
        P(("dp", "opt"), None, None, None),
        P(("dp", "opt"), None, None, None),
        P(("dp", "opt")),
        P(("dp", "opt")),
    )
    return jax.shard_map(
        per_device,
        mesh=mesh,
        in_specs=placed,
        out_specs=(
            P(("dp", "opt"), None),
            P(("dp", "opt"), None),
            P(("dp", "opt"), None),
            P(("dp", "opt"), None),
            P(("dp", "opt"), None, None),
            P(("dp", "opt"), None, None, None),
            P(("dp", "opt"), None, None),
            P(("dp", "opt")),
            P(("dp", "opt")),
            P(("dp", "opt")),
        ),
        check_vma=False,
    )
```
